256 devices in a mesh: frame: 32 (over x, z_lo, core), tok: 8 (over y, z_hi).
Axes of the slice: x: 4, y: 4, z: 8 (z_hi: 2, z_lo: 4; z = z_hi * 4 + z_lo), core: 2. Of those that a mesh axis runs over, the one named last changes fastest.
Arguments:
- patches: bfloat16 [32, 1024, 1408], P('frame', 'tok'), may hold values from -6 to 6
- shift_offset: int32 [1024], P('tok'), may hold values from -1 to 1
- shift_slice: int32 [1024], P('tok'), may hold values from 0 to 3
- w_query: bfloat16 [1408, 1408], P('frame', 'tok'), may hold values from -0.15625 to 0.15625
- w_key: bfloat16 [1408, 1408], P('frame', 'tok'), may hold values from -0.15625 to 0.15625
- w_value: bfloat16 [1408, 1408], P('frame', 'tok'), may hold values from -0.15625 to 0.15625
- w_out: bfloat16 [1408, 1408], P('tok', 'frame'), may hold values from -1.25 to 1.25
- w_up: bfloat16 [1408, 6144], P('frame', 'tok'), may hold values from -0.15625 to 0.15625
- w_down: bfloat16 [6144, 1408], P('tok', 'frame'), may hold values from -0.078125 to 0.078125
- t_query: bfloat16 [1408, 1408], P('tok'), may hold values from -0.15625 to 0.15625
- t_key: bfloat16 [1408, 1408], P('tok'), may hold values from -0.15625 to 0.15625
- t_value: bfloat16 [1408, 1408], P('tok'), may hold values from -0.15625 to 0.15625
- t_out: bfloat16 [1408, 1408], P('tok'), may hold values from -0.15625 to 0.15625
- cache_keys: bfloat16 [1984, 1408], P('frame', 'tok'), may hold values from -6 to 6
- cache_values: bfloat16 [1984, 1408], P('frame', 'tok'), may hold values from -6 to 6
- cache_pos: int32 [1984], P('frame'), may hold values from 0 to 4095
Outputs:
- patch_out: bfloat16 [32, 1024, 1408], P('frame', 'tok')
- frame_out: bfloat16 [32, 1408], P('frame', 'tok')
The draws below stay inside these ranges and needn't reach their ends.
Inputs may be any that keep to these rules, and one draw needn't show every extreme that they name: `shift_offset`: -1 takes channels from the frame before, 1 from the frame after, 0 none. `cache_pos`: all cached positions lie before the new frames.
All inputs are finite; a program needn't handle non-finite values.
Results may differ from the reference program's by a relative error of at most 0.018.
Values may be sent and summed in bfloat16 or wider, within the bound.
A program may use at most 64 MiB of HBM per device.

```python
import jax
import jax.numpy as jnp
from jax import lax

D = 1408
HEADS = 16
FF = 6144
HD = 88
P_SIZE = 1024
SPAN = 4096
FRAMES = 32
CACHED = 1984


def plant(values, own_key, least, top_value):
    longest = values.shape.index(max(values.shape))
    spots = []
    for shift in (0, 1):
        where = [jax.random.randint(jax.random.fold_in(own_key, axis), (), 0, length) for axis, length in enumerate(values.shape)]
        where[longest] = (where[longest] + shift) % values.shape[longest]
        spots.append(tuple(where))
    return values.at[spots[0]].set(least).at[spots[1]].set(top_value)


def raised(drawn, stream_key, source, target, shards_of, factor):
    owner, partner = [(jnp.arange(drawn.shape[axis_at]) // (drawn.shape[axis_at] // shards_of)).reshape([-1 if axis == axis_at else 1 for axis in range(drawn.ndim)]) for axis_at in (source, target)]
    chosen = jax.random.permutation(stream_key, shards_of)[partner]
    strong = (owner == chosen) | (owner == (partner + shards_of // 2) % shards_of)
    return jnp.where(strong, factor * drawn, drawn)


def shard_levels(stream_key, shape, shards, low, largest):
    loudness, own = 1.0, jax.random.fold_in(stream_key, 6)
    for axis_at, shards_of in shards:
        draws = jnp.exp(jax.random.uniform(jax.random.fold_in(own, axis_at), (shards_of,), jnp.float32, low / len(shards), largest / len(shards)))
        loudness = loudness * jnp.repeat(draws, shape[axis_at] // shards_of).reshape([-1 if axis == axis_at else 1 for axis in range(len(shape))])
    return loudness


def normal_values(stream_key, dims, scale, most, shards=(), held_as=jnp.bfloat16):
    drawn = scale * jax.random.normal(stream_key, dims, jnp.float32)
    if shards:
        drawn = drawn * shard_levels(stream_key, dims, shards, -0.22, 0.18)
    return jnp.clip(drawn, -most, most).astype(held_as)


def noise_with(key, extent, deviation, bound, shards, heavy, held_as=jnp.bfloat16):
    drawn = deviation * jax.random.normal(key, extent, jnp.float32)
    if shards:
        drawn = drawn * shard_levels(key, extent, shards, -0.22, 0.18)
    return jnp.clip(raised(drawn, jax.random.fold_in(key, 3), *heavy), -bound, bound).astype(held_as)


def setup_inputs(seed: int = 0) -> dict:
    splits = jax.random.split(jax.random.key(seed), 17)
    return {
        "patches": normal_values(splits[0], (FRAMES, P_SIZE, D), 1.0, 6.0, ((0, 32), (1, 8))),
        "shift_offset": plant(jax.random.randint(splits[1], (P_SIZE,), -1, 2), jax.random.fold_in(splits[1], 1), -1, 1).astype(jnp.int32),
        "shift_slice": plant(jax.random.randint(splits[2], (P_SIZE,), 0, 4), jax.random.fold_in(splits[2], 1), 0, 3).astype(jnp.int32),
        "w_query": normal_values(splits[3], (D, D), D ** -0.5, 0.15625, ((0, 32), (1, 8))),
        "w_key": normal_values(splits[4], (D, D), D ** -0.5, 0.15625, ((0, 32), (1, 8))),
        "w_value": normal_values(splits[5], (D, D), D ** -0.5, 0.15625, ((0, 32), (1, 8))),
        "w_out": noise_with(splits[6], (D, D), (D // 16) ** -0.5, 1.25, ((0, 8), (1, 32)), (0, 1, 32, 2.75)),
        "w_up": normal_values(splits[7], (D, FF), D ** -0.5, 0.15625, ((0, 32), (1, 8))),
        "w_down": normal_values(splits[8], (FF, D), FF ** -0.5, 0.078125, ((0, 8), (1, 32))),
        "t_query": normal_values(splits[9], (D, D), D ** -0.5, 0.15625, ((0, 8),)),
        "t_key": normal_values(splits[10], (D, D), D ** -0.5, 0.15625, ((0, 8),)),
        "t_value": normal_values(splits[11], (D, D), D ** -0.5, 0.15625, ((0, 8),)),
        "t_out": normal_values(splits[12], (D, D), D ** -0.5, 0.15625, ((0, 8),)),
        "cache_keys": normal_values(splits[13], (CACHED, D), 1.0, 6.0, ((0, 32), (1, 8))),
        "cache_values": normal_values(splits[14], (CACHED, D), 1.0, 6.0, ((0, 32), (1, 8))),
        "cache_pos": plant(jax.random.randint(splits[15], (CACHED,), 0, SPAN), jax.random.fold_in(splits[15], 1), 0, SPAN - 1).astype(jnp.int32),
    }


def layer_norm(values):
    center = values - lax.optimization_barrier(jnp.mean(values, axis=-1, keepdims=True))
    spread = lax.optimization_barrier(jnp.mean(center * center, axis=-1, keepdims=True))
    return center * lax.rsqrt(spread + 1e-06)

def rotate(values, positions):
    half = values.shape[-1] // 2
    freq = 10000.0 ** (-jnp.arange(half, dtype=jnp.float32) / half)
    angle = positions[:, None, None] * freq[None, None, :]
    first = values[..., :half]
    second = values[..., half:]
    cosine = jnp.cos(angle)
    sine = jnp.sin(angle)
    return jnp.concatenate([first * cosine - second * sine, first * sine + second * cosine], axis=-1)

def reference(patches, shift_offset, shift_slice, w_query, w_key, w_value, w_out, w_up, w_down, t_query, t_key, t_value, t_out, cache_keys, cache_values, cache_pos):
    residual = patches.astype(jnp.float32)
    normed = layer_norm(residual).astype(jnp.bfloat16)
    blank = jnp.zeros_like(normed[:1])
    earlier = jnp.concatenate([blank, normed[:-1]], axis=0)
    later = jnp.concatenate([normed[1:], blank], axis=0)
    offsets = shift_offset[None, :, None]
    source = jnp.where(offsets == -1, earlier, jnp.where(offsets == 1, later, normed))
    quarter = jnp.arange(D, dtype=jnp.int32) // (D // 4)
    chosen = (quarter[None, :] == shift_slice[:, None])[None]
    shifted = jnp.where(chosen, source, normed)
    scale = HD ** (-0.5)

    def one_frame(pair):
        rows, resid = pair
        query = jnp.dot(rows, w_query, preferred_element_type=jnp.float32).astype(jnp.bfloat16).reshape(P_SIZE, HEADS, HD)
        key = jnp.dot(rows, w_key, preferred_element_type=jnp.float32).astype(jnp.bfloat16).reshape(P_SIZE, HEADS, HD)
        value = jnp.dot(rows, w_value, preferred_element_type=jnp.float32).astype(jnp.bfloat16).reshape(P_SIZE, HEADS, HD)
        scores = jnp.einsum('qhd,khd->hqk', query.astype(jnp.float32), key.astype(jnp.float32)) * scale
        weights = jax.nn.softmax(scores, axis=-1).astype(jnp.bfloat16)
        attended = jnp.einsum('hqk,khd->qhd', weights.astype(jnp.float32), value.astype(jnp.float32))
        attended = attended.reshape(P_SIZE, D).astype(jnp.bfloat16)
        mixed = (resid + jnp.dot(attended, w_out, preferred_element_type=jnp.float32)).astype(jnp.bfloat16)
        second = layer_norm(mixed.astype(jnp.float32)).astype(jnp.bfloat16)
        hidden = jax.nn.gelu(jnp.dot(second, w_up, preferred_element_type=jnp.float32)).astype(jnp.bfloat16)
        return (mixed.astype(jnp.float32) + jnp.dot(hidden, w_down, preferred_element_type=jnp.float32)).astype(jnp.bfloat16)
    patch_out = lax.map(one_frame, (shifted, residual))
    pooled = lax.optimization_barrier(jnp.sum(patch_out.astype(jnp.float32), axis=1)) / P_SIZE
    pooled_normed = layer_norm(pooled).astype(jnp.bfloat16)
    new_pos = (SPAN + jnp.arange(FRAMES, dtype=jnp.int32)).astype(jnp.float32)
    tq = rotate(jnp.dot(pooled_normed, t_query, preferred_element_type=jnp.float32).reshape(FRAMES, HEADS, HD), new_pos).astype(jnp.bfloat16)
    tk = rotate(jnp.dot(pooled_normed, t_key, preferred_element_type=jnp.float32).reshape(FRAMES, HEADS, HD), new_pos).astype(jnp.bfloat16)
    tv = jnp.dot(pooled_normed, t_value, preferred_element_type=jnp.float32).astype(jnp.bfloat16).reshape(FRAMES, HEADS, HD)
    ck = rotate(cache_keys.astype(jnp.float32).reshape(CACHED, HEADS, HD), cache_pos.astype(jnp.float32)).astype(jnp.bfloat16)
    keys = jnp.concatenate([ck, tk], axis=0).astype(jnp.float32)
    values = jnp.concatenate([cache_values.reshape(CACHED, HEADS, HD), tv], axis=0).astype(jnp.float32)
    scores = jnp.einsum('fhd,khd->hfk', tq.astype(jnp.float32), keys) * scale
    frame_ids = jnp.arange(FRAMES, dtype=jnp.int32)
    valid = jnp.concatenate([jnp.ones((FRAMES, CACHED), dtype=bool), frame_ids[None, :] <= frame_ids[:, None]], axis=1)
    scores = jnp.where(valid[None], scores, -1e+30)
    top = lax.optimization_barrier(jnp.max(scores, axis=-1, keepdims=True))
    weight = jnp.where(valid[None], jnp.exp(scores - top), 0.0)
    total = lax.optimization_barrier(jnp.sum(weight, axis=-1))
    summed = jnp.einsum('hfk,khd->fhd', weight, values) / jnp.transpose(total)[:, :, None]
    temporal = summed.reshape(FRAMES, D).astype(jnp.bfloat16)
    frame_out = (pooled + jnp.dot(temporal, t_out, preferred_element_type=jnp.float32)).astype(jnp.bfloat16)
    return (patch_out, frame_out)
```

```python
import jax
import jax.numpy as jnp
import numpy as np
from jax import lax
from jax.experimental import pallas as pl
from jax.experimental.pallas import tpu as pltpu
from jax.sharding import PartitionSpec as P

HEADS = 16
HD = 88
P_SIZE = 1024
SPAN = 4096
FRAMES = 32
D = 1408
DP = 1536
QW = 384
TOK = 128
SCALE = HD ** (-0.5)
RATE = SCALE * 1.4426950408889634
MESH = pl.DeviceIdType.MESH
F32 = jnp.float32
BF = jnp.bfloat16
WC = 768
W_ROWS, CACHE_ROWS, CACHE_COLS = 48, 64, 512
WINDOWS = ((0, 384), (256, 512), (640, 512), (1024, 384))


def dot(a, b):
    return jnp.dot(a, b, preferred_element_type=F32)


def dot_nt(a, b):
    return lax.dot_general(a, b, (((1,), (1,)), ((), ())), preferred_element_type=F32)


def iota(shape, axis):
    return lax.broadcasted_iota(jnp.int32, shape, axis)


def mod(a, n):
    return lax.rem(a + n, n)


class Copies:
    def __init__(self, send, recv):
        self.send, self.recv, self.used, self.open = send, recv, 0, []

    def start(self, src, dst, device):
        n = self.used
        self.used += 1
        copy = pltpu.make_async_remote_copy(
            src_ref=src,
            dst_ref=dst,
            send_sem=self.send.at[n],
            recv_sem=self.recv.at[n],
            device_id=device,
            device_id_type=MESH,
        )
        copy.start()
        self.open.append(copy)
        return copy

    def retire(self, keep=0):
        while len(self.open) > keep:
            self.open.pop(0).wait_send()


def norm_padded(v, valid):
    mean = jnp.sum(v, axis=1, keepdims=True) * (1.0 / D)
    center = jnp.where(valid, v - mean, 0.0)
    spread = jnp.sum(center * center, axis=1, keepdims=True) * (1.0 / D)
    return center * lax.rsqrt(spread + 1e-06)


def as_column(row):
    spread = jnp.where(iota((TOK, TOK), 0) == iota((TOK, TOK), 1), row, 0.0)
    return jnp.sum(spread, axis=1, keepdims=True)


def kernel(
    patches_hbm, offset_hbm, piece_hbm, wq_hbm, wk_hbm, wv_hbm, wo_hbm, wu_hbm, wd_hbm,
    tq_hbm, tk_hbm, tv_hbm, to_hbm, ck_hbm, cv_hbm, pos_hbm, table_hbm, turn_hbm,
    out, frame_out,
    patches, offset_in, piece_in, wq, wk, wv, wo, wu, wd, tq_w, tk_w, tv_w, to_w, ck_in, cv_in, pos_in, table, turn,
    meta, xin, meta_in, src, src_in, pad, res, WA, WU, WU2, WD, WD2, C, comp, around, H1, KV, Q,
    SB, RB, RC, mixed, H2, HID, SB2, RB2, RC2,
    result, swapped, sums, pooled, qkv_send, qkv_recv, new_send, new_all, last_send, last_recv,
    local, big_send, big_recv, swap_send, swap_recv, s1, r1, s2, r2, s3, r3, s4, r4,
):
    f = lax.axis_index("frame")
    t = lax.axis_index("tok")
    x, zl, c = lax.div(f, 8), lax.div(lax.rem(f, 8), 2), lax.rem(f, 2)
    y, zh = lax.div(t, 2), lax.rem(t, 2)
    z = zh * 4 + zl

    def place(r):
        return (r + 2) % 8

    loads = [
        pltpu.make_async_copy(a, b, local.at[n])
        for n, (a, b) in enumerate(
            (
                (patches_hbm, patches), (offset_hbm, offset_in), (piece_hbm, piece_in),
                (wq_hbm, wq), (wk_hbm, wk), (wv_hbm, wv), (wo_hbm, wo), (wu_hbm, wu), (wd_hbm, wd),
                (ck_hbm, ck_in), (cv_hbm, cv_in), (pos_hbm, pos_in), (table_hbm, table),
                (turn_hbm.at[f], turn), (tq_hbm, tq_w), (tk_hbm, tk_w), (tv_hbm, tv_w), (to_hbm, to_w),
            )
        )
    ]
    for load in loads:
        load.start()
    new_all[...] = jnp.zeros_like(new_all)

    def dev(x_at, z_at, y_at, c_at):
        return (x_at * 8 + lax.rem(z_at, 4) * 2 + c_at, y_at * 2 + lax.div(z_at, 4))

    xp, xm = dev(mod(x + 1, 4), z, y, c), dev(mod(x - 1, 4), z, y, c)
    yp, ym = dev(x, z, mod(y + 1, 4), c), dev(x, z, mod(y - 1, 4), c)
    zp, zm = dev(x, mod(z + 1, 8), y, c), dev(x, mod(z - 1, 8), y, c)
    sibling = dev(x, z, y, 1 - c)
    partner = dev(x, mod(z + 4, 8), y, 1 - c)
    after, before = (mod(f + 1, 32), t), (mod(f - 1, 32), t)

    barrier = pltpu.get_barrier_semaphore()
    friends = (xp, xm, yp, ym, zp, zm, sibling, partner, after, before)
    for friend in friends:
        pl.semaphore_signal(barrier, inc=1, device_id=friend, device_id_type=MESH)
    pl.semaphore_wait(barrier, len(friends))

    copies = Copies(big_send, big_recv)
    moves = c != zh

    def remote(src, dst, send, recv, device):
        return pltpu.make_async_remote_copy(
            src_ref=src, dst_ref=dst, send_sem=send, recv_sem=recv,
            device_id=device, device_id_type=MESH,
        )

    def swap(src, dst, n):
        return remote(src, dst, swap_send.at[n], swap_recv.at[n], partner)

    for load in loads[0:3]:
        load.wait()
    meta[0:1, :] = offset_in[...].astype(F32)
    meta[1:2, :] = piece_in[...].astype(F32)

    @pl.when(moves)
    def _():
        swap(patches, xin, 0).start()
        swap(meta, meta_in, 1).start()

    @pl.when(jnp.logical_not(moves))
    def _():
        xin[...] = patches[...]
        meta_in[...] = meta[...]

    for load in loads[3:7]:
        load.wait()
    grow = jnp.where(iota((48, 44), 0) == iota((48, 44), 1), 1.0, 0.0).astype(BF)
    total = None
    for n, w in enumerate((wq, wk, wv, wo)):
        to = jnp.where(
            iota((176, WC), 0) + n * 176 == iota((176, WC), 1), 1.0, 0.0
        ).astype(BF)
        term = dot(dot(grow, w[...]).astype(BF), to)
        total = term if total is None else total + term
    WA[0, 0, place(0)] = total.astype(BF)

    def z_first(B):
        def at(r):
            return B.at[0, 0, place(r)]

        waits = [copies.start(at(0), at(-1), zp), copies.start(at(0), at(1), zm)]
        yield
        firsts = []

        def across(run):
            firsts.append(copies.start(B.at[0, 0, run], B.at[0, 3, run], xp))
            firsts.append(copies.start(B.at[0, 0, run], B.at[0, 1, run], xm))

        half = B.shape[4] // 2
        low, high = pl.ds(0, half), pl.ds(half, half)
        for step in range(1, 5):
            for copy in waits:
                copy.wait_recv()
            if step < 3:
                waits = [
                    copies.start(at(-step), at(-step - 1), zp),
                    copies.start(at(step), at(step + 1), zm),
                ]
            elif step == 3:
                waits = [
                    copies.start(B.at[0, 0, place(-3), :, low], B.at[0, 0, place(4), :, low], zp),
                    copies.start(B.at[0, 0, place(3), :, high], B.at[0, 0, place(4), :, high], zm),
                ]
            if step == 2:
                across(pl.ds(0, 5))
            if step == 4:
                across(pl.ds(5, 3))
            if step < 4:
                yield

        def aside(x_at):
            return copies.start(B.at[0, x_at], B.at[1, x_at], sibling)

        sides = [aside(0)]
        yield
        for copy in firsts:
            copy.wait_recv()
        one, two = pl.ds(0, 4), pl.ds(4, 4)
        waits = [
            copies.start(B.at[0, 3, one], B.at[0, 2, one], xp),
            copies.start(B.at[0, 1, two], B.at[0, 2, two], xm),
        ]
        sides += [aside(3), aside(1)]
        yield
        for copy in waits:
            copy.wait_recv()
        sides.append(aside(2))
        yield
        for copy in sides:
            copy.wait_recv()

    def x_first(B):
        here = place(0)
        waits = [
            copies.start(B.at[0, here, 0], B.at[0, here, 3], xp),
            copies.start(B.at[0, here, 0], B.at[0, here, 1], xm),
        ]
        yield
        half = B.shape[4] // 2
        low, high = pl.ds(0, half), pl.ds(half, half)
        for copy in waits:
            copy.wait_recv()
        waits = [
            copies.start(B.at[0, here, 3, :, low], B.at[0, here, 2, :, low], xp),
            copies.start(B.at[0, here, 1, :, high], B.at[0, here, 2, :, high], xm),
        ]
        yield

        def at(r):
            return B.at[0, place(r)]

        one, two = pl.ds(0, 2), pl.ds(2, 2)
        for step in range(5):
            for copy in waits:
                copy.wait_recv()
            if step < 3:
                waits = [
                    copies.start(at(-step), at(-step - 1), zp),
                    copies.start(at(step), at(step + 1), zm),
                ]
                yield
            elif step == 3:
                waits = [
                    copies.start(B.at[0, place(-3), one], B.at[0, place(4), one], zp),
                    copies.start(B.at[0, place(3), two], B.at[0, place(4), two], zm),
                ]
                yield
        side = copies.start(B.at[0], B.at[1], sibling)
        yield
        side.wait_recv()

    def drain(task):
        for _ in task:
            pass

    def ahead(task, count):
        for _ in range(count):
            if next(task, "end") == "end":
                return

    def both(*tasks):
        tasks = list(tasks)
        while tasks:
            for task in list(tasks):
                if next(task, "end") == "end":
                    tasks.remove(task)
            if tasks:
                yield

    load1, load4 = z_first(WA), x_first(C)
    load2 = both(z_first(WU), x_first(WU2))
    load3 = both(z_first(WD), x_first(WD2))
    ahead(load1, 1)

    for q, (start, size) in enumerate(WINDOWS):
        r, k = iota((size, QW), 0) + start, iota((size, QW), 1)
        at = lax.rem(k, 48)
        hit = (r == 352 * q + lax.div(k, 48) * 44 + at) & (at < 44)
        pad[q, 0:size, :] = jnp.where(hit, 1.0, 0.0).astype(BF)
    valid = lax.rem(iota((1, DP), 1), 48) < 44

    def padded(rows):
        for q, (start, size) in enumerate(WINDOWS):
            res[:, q * QW : (q + 1) * QW] = dot(
                rows[:, start : start + size], pad[q, 0:size, :]
            ).astype(BF)
        normed = norm_padded(res[...].astype(F32), valid)
        return [normed[:, q * QW : (q + 1) * QW] for q in range(4)]

    quarters = padded(patches)
    offset, piece = as_column(meta[0:1, :]), as_column(meta[1:2, :])
    mine = quarters[0]
    for q in range(1, 4):
        mine = jnp.where(piece == float(q), quarters[q], mine)
    comp[...] = mine.astype(BF)
    hops = [
        copies.start(comp, around.at[0], after),
        copies.start(comp, around.at[1], before),
    ]
    for load in loads[7:9]:
        load.wait()
    for w, one, two in ((wu, WU, WU2), (wd, WD, WD2)):
        rows = dot(grow, w[...]).astype(BF)
        one[0, 0, place(0)] = rows[:, 0:512]
        two[0, place(0), 0] = rows[:, 512:768]
    ahead(load1, 1)
    for copy in hops:
        copy.wait_recv()
    earlier = jnp.where(f > 0, around[0].astype(F32), 0.0)
    later = jnp.where(f < FRAMES - 1, around[1].astype(F32), 0.0)
    source = jnp.where(
        offset == -1.0, earlier, jnp.where(offset == 1.0, later, comp[...].astype(F32))
    )
    src[...] = source.astype(BF)

    @pl.when(moves)
    def _():
        swap(src, src_in, 2).start()

    @pl.when(jnp.logical_not(moves))
    def _():
        src_in[...] = src[...]

    ahead(load1, 1)

    def turned(v):
        return jnp.concatenate([v[:, 44:88], v[:, 0:44], v[:, 132:176], v[:, 88:132]], axis=1)

    for load in loads[9:13]:
        load.wait()
    spot = jnp.where(
        iota((CACHE_ROWS, 62), 0) == iota((CACHE_ROWS, 62), 1), pos_in[...].astype(F32), 0.0
    )
    spot = jnp.sum(spot, axis=1, keepdims=True)
    high = jnp.floor(spot * (1.0 / 64))
    lanes = iota((CACHE_ROWS, 64), 1).astype(F32)

    def chosen(at, n):
        hit = jnp.where(lanes == at, 1.0, 0.0)
        both = jnp.dot(hit, table[n], preferred_element_type=F32, precision=lax.Precision.HIGHEST)
        return both[0:62, 0:176], both[0:62, 176:352]

    (cos_a, sin_a), (cos_b, sin_b) = chosen(high, 0), chosen(spot - 64.0 * high, 1)
    cosine, sine = cos_a * cos_b - sin_a * sin_b, sin_a * cos_b + cos_a * sin_b
    sine = jnp.where(lax.rem(iota((62, 176), 1), HD) < HD // 2, -sine, sine)
    raw = ck_in[...].astype(F32)
    C[0, place(0), 0] = jnp.zeros((CACHE_ROWS, CACHE_COLS), BF)
    C[0, place(0), 0, 0:62, 0:176] = (raw * cosine + turned(raw) * sine).astype(BF)
    C[0, place(0), 0, 0:62, 256:432] = cv_in[...]
    ahead(load1, 2)

    @pl.when(moves)
    def _():
        swap(patches, xin, 0).wait()
        swap(meta, meta_in, 1).wait()
        swap(src, src_in, 2).wait()

    quarters = padded(xin)
    piece = as_column(meta_in[1:2, :])
    for q in range(4):
        H1[0, :, q * QW : (q + 1) * QW] = jnp.where(
            piece == float(q), src_in[...].astype(F32), quarters[q]
        ).astype(BF)

    def gather(H):
        a, b = pl.ds(0, 64), pl.ds(64, 64)
        one = copies.start(H.at[0, a], H.at[3, a], yp)
        two = copies.start(H.at[0, b], H.at[1, b], ym)
        rest = [
            copies.start(H.at[0, b], H.at[3, b], yp), copies.start(H.at[0, a], H.at[1, a], ym)
        ]
        yield
        one.wait_recv()
        far = [copies.start(H.at[3, a], H.at[2, a], yp)]
        two.wait_recv()
        far.append(copies.start(H.at[1, b], H.at[2, b], ym))
        yield
        for copy in rest:
            copy.wait_recv()
        yield
        for copy in far:
            copy.wait_recv()

    rows1 = gather(H1)
    ahead(rows1, 1)
    ahead(load2, 2)
    ahead(rows1, 1)
    ahead(load1, 1)
    ahead(load2, 1)
    ahead(rows1, 1)
    ahead(load2, 1)
    drain(rows1)
    ahead(load1, 1)
    drain(load1)
    ahead(load2, 1)

    plane_of = [c, 1 - c]
    x_of = [mod(k - x, 4) for k in range(4)]
    z_of = [lax.rem(k - z + 8 + 2, 8) for k in range(8)]

    def weight(B, at, start, size):
        pieces = []
        for k in range(32):
            p, x_at, z_at = plane_of[k % 2], x_of[k // 8], z_of[at * 4 + k // 2 % 4]
            spot = (p, x_at, z_at) if B.shape[1] == 4 else (p, z_at, x_at)
            pieces.append(B[(*spot, slice(None), slice(start, start + size))])
        return jnp.concatenate(pieces, axis=0)

    def wider(rows, first, columns, start):
        r, k = iota((rows, columns), 0) + first, iota((rows, columns), 1) + start
        at = lax.rem(k, 128)
        return jnp.where((r == lax.div(k, 128) * HD + at) & (at < HD), 1.0, 0.0).astype(BF)

    wide_q, wide_kv = wider(256, 0, 256, 0), wider(512, 128, 512, 256)
    r, k = iota((256, 256), 1) + 512, iota((256, 256), 0)
    at = lax.rem(k, 128)
    narrow = jnp.where(
        (r == 528 + lax.div(k, 128) * HD + at) & (at < HD), 1.0, 0.0
    ).astype(BF)

    rows = H1[...].reshape(4 * TOK, DP)
    sides = []
    for at in range(2):
        joined = dot(rows, weight(WA, at, 128, 512)).astype(BF)
        KV[0, at] = dot(joined, wide_kv).astype(BF)
        sides.append(copies.start(KV.at[0, at], KV.at[1, at], sibling))
    ahead(load3, 1)
    for at in range(2):
        joined = dot(rows, weight(WA, at, 0, 256)).astype(BF)
        Q[at] = dot(joined, wide_q).astype(BF).reshape(4, TOK, 256)
    ahead(load3, 1)
    for copy in sides:
        copy.wait_recv()

    def attend(block):
        total = None
        for at in range(2):
            heads = []
            for h in range(2):
                span = slice(h * 128, h * 128 + 128)
                vspan = slice(256 + h * 128, 256 + h * 128 + 128)
                q = Q[at, block, :, span]
                s = [dot_nt(q, KV[k, at, :, span]) for k in range(2)]
                top = jnp.maximum(
                    jnp.max(s[0], axis=1, keepdims=True), jnp.max(s[1], axis=1, keepdims=True)
                )
                p = [jnp.exp2(part * RATE - top * RATE) for part in s]
                mass = jnp.sum(p[0], axis=1, keepdims=True) + jnp.sum(p[1], axis=1, keepdims=True)
                o = dot(p[0].astype(BF), KV[0, at, :, vspan]) + dot(
                    p[1].astype(BF), KV[1, at, :, vspan]
                )
                heads.append((o / mass).astype(BF))
            both_heads = dot(jnp.concatenate(heads, axis=1), narrow).astype(BF)
            term = dot_nt(both_heads, weight(WA, at, 512, 256))
            total = term if total is None else total + term
        return total

    def scatter(partial, S, B, R, far_first, between):
        a, b = pl.ds(0, 64), pl.ds(64, 64)

        def send_far():
            S[0] = partial(2).astype(BF)
            return [
                copies.start(S.at[0, a], B.at[0], yp), copies.start(S.at[0, b], B.at[1], ym)
            ]

        def send_near():
            S[1] = partial(1).astype(BF)
            one = copies.start(S.at[1, b], R.at[0, b], yp)
            S[2] = partial(3).astype(BF)
            return [one, copies.start(S.at[2, a], R.at[1, a], ym)]

        if far_first:
            far = send_far()
            between(0)
            near = send_near()
            between(1)
        else:
            near = send_near()
            far = send_far()
            between(0)
        far[0].wait_recv()
        S[1, 0:64, :] = (S[1, 0:64, :].astype(F32) + B[0].astype(F32)).astype(BF)
        near.append(copies.start(S.at[1, a], R.at[0, a], yp))
        far[1].wait_recv()
        S[2, 64:128, :] = (S[2, 64:128, :].astype(F32) + B[1].astype(F32)).astype(BF)
        near.append(copies.start(S.at[2, b], R.at[1, b], ym))
        own = partial(0)
        between(2)
        for copy in near:
            copy.wait_recv()
        return own + R[0].astype(F32) + R[1].astype(F32)

    def beside_attention(n):
        if n == 0:
            ahead(load2, 1)
            ahead(load3, 1)
            ahead(load4, 1)
        elif n == 1:
            ahead(load3, 1)
            ahead(load2, 1)
            ahead(load4, 1)
        else:
            ahead(load3, 1)
            drain(load2)

    total = scatter(attend, SB, RB, RC, True, beside_attention)
    mixed[...] = (res[...].astype(F32) + total).astype(BF)
    H2[0] = norm_padded(mixed[...].astype(F32), valid).astype(BF)
    rows2 = gather(H2)
    ahead(rows2, 1)
    ahead(load3, 1)
    ahead(load4, 1)

    def up(block, at):
        rows = H2[block]
        return [
            jax.nn.gelu(dot(rows, weight(WU, at, 0, 512))).astype(BF),
            jax.nn.gelu(dot(rows, weight(WU2, at, 0, 256))).astype(BF),
        ]

    def down(hidden, at):
        return dot_nt(hidden[0], weight(WD, at, 0, 512)) + dot_nt(
            hidden[1], weight(WD2, at, 0, 256)
        )

    def up_down(block):
        return down(up(block, 0), 0) + down(up(block, 1), 1)

    for at in range(2):
        first, second = up(0, at)
        HID[at, :, 0:512] = first
        HID[at, :, 512:768] = second
    ahead(rows2, 1)
    copies.retire(24)
    ahead(load4, 1)
    ahead(rows2, 1)
    ahead(load3, 1)
    drain(load3)

    def near_rows(block):
        return up_down(block)

    def far_rows(block):
        ahead(load4, 1)
        drain(rows2)
        return up_down(block)

    def own_rows(block):
        own = [(HID[at, :, 0:512], HID[at, :, 512:768]) for at in range(2)]
        return down(own[0], 0) + down(own[1], 1)

    def beside_mlp(n):
        if n == 0:
            ahead(load4, 1)
        else:
            ahead(load4, 1)
            copies.retire(8)

    calls = [near_rows, near_rows, far_rows, own_rows]
    total = scatter(lambda block: calls.pop(0)(block), SB2, RB2, RC2, False, beside_mlp)
    last = (mixed[...].astype(F32) + total).astype(BF)
    columns = [
        dot_nt(last[:, q * QW : (q + 1) * QW], pad[q, 0:size, :])
        for q, (_, size) in enumerate(WINDOWS)
    ]
    parts = [
        columns[0][:, 0:256],
        columns[0][:, 256:384] + columns[1][:, 0:128],
        columns[1][:, 128:384],
        columns[1][:, 384:512] + columns[2][:, 0:128],
        columns[2][:, 128:384],
        columns[2][:, 384:512] + columns[3][:, 0:128],
        columns[3][:, 128:384],
    ]
    plain = jnp.concatenate(parts, axis=1)
    sums[...] = jnp.sum(plain, axis=0, keepdims=True)

    other = f + 1 - 2 * c
    home = f - c + zh
    slot = 2 * y + c

    def share(k):
        return remote(sums, pooled.at[slot], s1, r1, (home, lax.rem(t + k, 8)))

    def all_of(ref, send, recv):
        return remote(ref, ref, send, recv, sibling)

    @pl.when(moves)
    def _():
        share(0).start()

    @pl.when(jnp.logical_not(moves))
    def _():
        pooled[slot] = sums[...]

    for k in range(1, 8):
        share(k).start()

    result[...] = plain.astype(BF)

    @pl.when(moves)
    def _():
        swap(result, swapped, 3).start()

    drain(load4)
    for load in loads[13:]:
        load.wait()

    @pl.when(moves)
    def _():
        all_of(pooled, s1, r1).wait_recv()

    @pl.when(jnp.logical_not(moves))
    def _():
        all_of(pooled.at[pl.ds(0, 7)], s1, r1).wait_recv()

    mean_frame = pooled[0]
    for k in range(1, 8):
        mean_frame = mean_frame + pooled[k]
    mean_frame = mean_frame * (1.0 / P_SIZE)
    center = mean_frame - jnp.sum(mean_frame, axis=1, keepdims=True) * (1.0 / D)
    spread = jnp.sum(center * center, axis=1, keepdims=True) * (1.0 / D)
    normed = center * lax.rsqrt(spread + 1e-06)

    def pick(v):
        got = v[:, 0:176]
        for k in range(1, 8):
            got = jnp.where(t == k, v[:, k * 176 : k * 176 + 176], got)
        return got

    features = jnp.broadcast_to(pick(normed), (8, 176)).astype(BF)
    for n, w in enumerate((tq_w, tk_w, tv_w)):
        part = dot(features, w[...])
        for k in range(8):
            qkv_send[k, n, :, 0:176] = part[0:1, k * 176 : k * 176 + 176]

    def send_heads(k):
        to = lax.rem(t + k, 8)
        return remote(qkv_send.at[to], qkv_recv.at[t], s2, r2, (f, to))

    for k in range(1, 8):
        send_heads(k).start()
    qkv_recv[t] = qkv_send[t]
    all_of(qkv_recv.at[pl.ds(0, 7)], s2, r2).wait_recv()

    whole = []
    for n in range(3):
        v = qkv_recv[0, n, :, 0:176]
        for k in range(1, 8):
            v = v + qkv_recv[k, n, :, 0:176]
        whole.append(v)

    def rot(v):
        return (v * turn[0:1, :] + turned(v) * turn[1:2, :]).astype(BF).astype(F32)

    new_send[...] = jnp.zeros_like(new_send)
    new_send[:, 0:176] = rot(whole[1])
    new_send[:, 256:432] = whole[2].astype(BF).astype(F32)


    @pl.loop(1, 32)
    def _(k):
        remote(new_send, new_all.at[f], s3, r3, (lax.rem(f + k, 32), t)).start()

    new_all[f] = new_send[...]
    query = rot(whole[0])
    lane = iota((1, 176), 1)
    wide_query = jnp.concatenate(
        [jnp.where(lane < HD, query, 0.0), jnp.where(lane >= HD, query, 0.0), jnp.zeros((6, 176), F32)],
        axis=0,
    )
    queries = jnp.concatenate([wide_query, jnp.zeros((8, 80), F32)], axis=1).astype(BF)
    count = 32 * CACHE_ROWS
    cached = [C[:, lax.rem(k - zl + 8 + 2, 8)] for k in range(4)]
    old_keys = jnp.concatenate([part[..., 0:256].reshape(-1, 256) for part in cached], axis=0)
    s_old = dot_nt(queries, old_keys)
    s_old = jnp.where(lax.rem(iota((8, count), 1), CACHE_ROWS) < 62, s_old, -1e30)

    all_of(new_all.at[pl.ds(0, 31)], s3, r3).wait_recv()
    known = new_all[:, 0, :]
    s_new = dot_nt(queries, known[:, 0:256].astype(BF))
    s_new = jnp.where(iota((8, 32), 1) <= f, s_new, -1e30)
    top = jnp.maximum(
        jnp.max(s_old, axis=1, keepdims=True), jnp.max(s_new, axis=1, keepdims=True)
    )
    p_old = jnp.exp2(s_old * RATE - top * RATE)
    p_new = jnp.exp2(s_new * RATE - top * RATE)
    p_old = jnp.where(lax.rem(iota((8, count), 1), CACHE_ROWS) < 62, p_old, 0.0)
    p_new = jnp.where(iota((8, 32), 1) <= f, p_new, 0.0)
    mass = jnp.sum(p_old, axis=1, keepdims=True) + jnp.sum(p_new, axis=1, keepdims=True)
    old_values = jnp.concatenate([part[..., 256:512].reshape(-1, 256) for part in cached], axis=0)
    o = dot(p_old.astype(BF), old_values) + dot(p_new.astype(BF), known[:, 256:512].astype(BF))
    o = o / mass
    temporal = jnp.where(lane < HD, o[0:1, 0:176], o[1:2, 0:176])
    part = dot(jnp.broadcast_to(temporal, (8, 176)).astype(BF), to_w[...])
    for k in range(8):
        last_send[k, :, 0:176] = part[0:1, k * 176 : k * 176 + 176]

    def send_last(k):
        to = lax.rem(t + k, 8)
        return remote(last_send.at[to], last_recv.at[t], s4, r4, (f, to))

    for k in range(1, 8):
        send_last(k).start()
    last_recv[t] = last_send[t]

    stored, kept = (pltpu.make_async_copy(a, out, local.at[0]) for a in (swapped, result))

    @pl.when(moves)
    def _():
        swap(result, swapped, 3).wait()
        stored.start()

    @pl.when(jnp.logical_not(moves))
    def _():
        kept.start()

    copies.retire()

    @pl.when(moves)
    def _():
        all_of(pooled, s1, r1).wait_send()

    @pl.when(jnp.logical_not(moves))
    def _():
        all_of(pooled.at[pl.ds(0, 7)], s1, r1).wait_send()

    all_of(qkv_recv.at[pl.ds(0, 7)], s2, r2).wait_send()
    all_of(new_all.at[pl.ds(0, 31)], s3, r3).wait_send()
    all_of(last_recv.at[pl.ds(0, 7)], s4, r4).wait_recv()
    total = pick(mean_frame)
    for k in range(8):
        total = total + last_recv[k, :, 0:176]
    frame_out[...] = total.astype(BF)
    all_of(last_recv.at[pl.ds(0, 7)], s4, r4).wait_send()

    @pl.when(moves)
    def _():
        stored.wait()

    @pl.when(jnp.logical_not(moves))
    def _():
        kept.wait()


BIG = 160


def call(*operands):
    turn = operands[-1]
    vmem = pl.BlockSpec(memory_space=pltpu.VMEM)
    dma = pltpu.SemaphoreType.DMA
    held = [pltpu.VMEM(a.shape, a.dtype) for a in operands[:-1]] + [
        pltpu.VMEM(turn.shape[1:], F32)
    ]
    return pl.pallas_call(
        kernel,
        out_shape=(
            jax.ShapeDtypeStruct((TOK, D), BF),
            jax.ShapeDtypeStruct((1, 176), BF),
        ),
        in_specs=[pl.BlockSpec(memory_space=pl.ANY)] * len(operands),
        out_specs=(pl.BlockSpec(memory_space=pl.ANY), vmem),
        scratch_shapes=held
        + [
            pltpu.VMEM((2, TOK), F32),
            pltpu.VMEM((TOK, D), BF),
            pltpu.VMEM((2, TOK), F32),
            pltpu.VMEM((TOK, QW), BF),
            pltpu.VMEM((TOK, QW), BF),
            pltpu.VMEM((4, 512, QW), BF),
            pltpu.VMEM((TOK, DP), BF),
            pltpu.VMEM((2, 4, 8, W_ROWS, WC), BF),
            pltpu.VMEM((2, 4, 8, W_ROWS, 512), BF),
            pltpu.VMEM((2, 8, 4, W_ROWS, 256), BF),
            pltpu.VMEM((2, 4, 8, W_ROWS, 512), BF),
            pltpu.VMEM((2, 8, 4, W_ROWS, 256), BF),
            pltpu.VMEM((2, 8, 4, CACHE_ROWS, CACHE_COLS), BF),
            pltpu.VMEM((TOK, QW), BF),
            pltpu.VMEM((2, TOK, QW), BF),
            pltpu.VMEM((4, TOK, DP), BF),
            pltpu.VMEM((2, 2, 4 * TOK, 512), BF),
            pltpu.VMEM((2, 4, TOK, 256), BF),
            pltpu.VMEM((3, TOK, DP), BF),
            pltpu.VMEM((2, 64, DP), BF),
            pltpu.VMEM((2, TOK, DP), BF),
            pltpu.VMEM((TOK, DP), BF),
            pltpu.VMEM((4, TOK, DP), BF),
            pltpu.VMEM((2, TOK, 768), BF),
            pltpu.VMEM((3, TOK, DP), BF),
            pltpu.VMEM((2, 64, DP), BF),
            pltpu.VMEM((2, TOK, DP), BF),
            pltpu.VMEM((TOK, D), BF),
            pltpu.VMEM((TOK, D), BF),
            pltpu.VMEM((1, D), F32),
            pltpu.VMEM((8, 1, D), F32),
            pltpu.VMEM((8, 3, 1, 256), F32),
            pltpu.VMEM((8, 3, 1, 256), F32),
            pltpu.VMEM((1, CACHE_COLS), F32),
            pltpu.VMEM((32, 1, CACHE_COLS), F32),
            pltpu.VMEM((8, 1, 256), F32),
            pltpu.VMEM((8, 1, 256), F32),
            dma((len(operands),)),
            dma((BIG,)), dma((BIG,)),
            dma((4,)), dma((4,)),
            dma, dma, dma, dma, dma, dma, dma, dma,
        ],
        compiler_params=pltpu.CompilerParams(
            collective_id=0, has_side_effects=True, vmem_limit_bytes=56 * 1024 * 1024
        ),
        cost_estimate=pl.CostEstimate(
            flops=8_000_000_000, bytes_accessed=20_000_000, transcendentals=3_000_000
        ),
    )(*operands)


def body(
    patches, shift_offset, shift_slice, w_query, w_key, w_value, w_out, w_up, w_down,
    t_query, t_key, t_value, t_out, cache_keys, cache_values, cache_pos,
):
    half = HD // 2
    freq = np.float32(10000.0) ** (-np.arange(half, dtype=np.float32) / np.float32(half))
    angle = (SPAN + np.arange(FRAMES)).astype(np.float32)[:, None] * freq[None, :]
    cosine, sine = np.cos(angle), np.sin(angle)
    turn = np.stack(
        [
            np.concatenate([cosine] * 4, axis=1),
            np.concatenate([-sine, sine, -sine, sine], axis=1),
        ],
        axis=1,
    ).astype(np.float32)
    steps = np.arange(64)[:, None] * (10000.0 ** (-np.arange(half) / half))[None, :]
    table = np.stack(
        [
            np.concatenate([np.cos(64 * steps)] * 4 + [np.sin(64 * steps)] * 4, axis=1),
            np.concatenate([np.cos(steps)] * 4 + [np.sin(steps)] * 4, axis=1),
        ]
    ).astype(np.float32)
    patch_out, frame_out = call(
        patches[0], shift_offset[None], shift_slice[None], w_query, w_key, w_value,
        w_out.T, w_up, w_down.T, t_query, t_key, t_value, t_out, cache_keys, cache_values, cache_pos[None],
        jnp.asarray(table), jnp.asarray(turn),
    )
    return (patch_out[None], frame_out)


def solution(mesh):
    return jax.shard_map(
        body,
        mesh=mesh,
        in_specs=(
            P("frame", "tok", None),
            P("tok"),
            P("tok"),
            P("frame", "tok"),
            P("frame", "tok"),
            P("frame", "tok"),
            P("tok", "frame"),
            P("frame", "tok"),
            P("tok", "frame"),
            P("tok", None),
            P("tok", None),
            P("tok", None),
            P("tok", None),
            P("frame", "tok"),
            P("frame", "tok"),
            P("frame"),
        ),
        out_specs=(P("frame", "tok", None), P("frame", "tok")),
        check_vma=False,
    )
```

```python
import jax
import jax.numpy as jnp
import numpy as np
from jax import lax
from jax.experimental import pallas as pl
from jax.experimental.pallas import tpu as pltpu
from jax.sharding import PartitionSpec as P

HEADS = 16
HD = 88
P_SIZE = 1024
SPAN = 4096
FRAMES = 32
D = 1408
DP = 1536
QW = 384
TOK = 128
SCALE = HD ** (-0.5)
RATE = SCALE * 1.4426950408889634
MESH = pl.DeviceIdType.MESH
F32 = jnp.float32
BF = jnp.bfloat16
WC = 768
W_ROWS, CACHE_ROWS, CACHE_COLS = 48, 64, 512
WINDOWS = ((0, 384), (256, 512), (640, 512), (1024, 384))


def dot(a, b):
    return jnp.dot(a, b, preferred_element_type=F32)


def dot_nt(a, b):
    return lax.dot_general(a, b, (((1,), (1,)), ((), ())), preferred_element_type=F32)


def iota(shape, axis):
    return lax.broadcasted_iota(jnp.int32, shape, axis)


def mod(a, n):
    return lax.rem(a + n, n)


class Copies:
    def __init__(self, send, recv):
        self.send, self.recv, self.used, self.open = send, recv, 0, []

    def start(self, src, dst, device):
        n = self.used
        self.used += 1
        copy = pltpu.make_async_remote_copy(
            src_ref=src,
            dst_ref=dst,
            send_sem=self.send.at[n],
            recv_sem=self.recv.at[n],
            device_id=device,
            device_id_type=MESH,
        )
        copy.start()
        self.open.append(copy)
        return copy

    def retire(self, keep=0):
        while len(self.open) > keep:
            self.open.pop(0).wait_send()


def norm_padded(v, valid):
    mean = jnp.sum(v, axis=1, keepdims=True) * (1.0 / D)
    center = jnp.where(valid, v - mean, 0.0)
    spread = jnp.sum(center * center, axis=1, keepdims=True) * (1.0 / D)
    return center * lax.rsqrt(spread + 1e-06)


def as_column(row):
    spread = jnp.where(iota((TOK, TOK), 0) == iota((TOK, TOK), 1), row, 0.0)
    return jnp.sum(spread, axis=1, keepdims=True)


def kernel(
    patches_hbm, offset_hbm, piece_hbm, wq_hbm, wk_hbm, wv_hbm, wo_hbm, wu_hbm, wd_hbm,
    tq_hbm, tk_hbm, tv_hbm, to_hbm, ck_hbm, cv_hbm, pos_hbm, table_hbm, turn_hbm,
    out, frame_out,
    patches, offset_in, piece_in, wq, wk, wv, wo, wu, wd, tq_w, tk_w, tv_w, to_w, ck_in, cv_in, pos_in, table, turn,
    meta, xin, meta_in, src, src_in, pad, res, WA, WA2, WU, WU2, WD, WD2, C, comp, around, H1, KV, Q,
    SB, RB, RC, mixed, H2, HID, SB2, RB2, RC2,
    result, swapped, sums, pooled, qkv_send, qkv_recv, new_send, new_all, last_send, last_recv,
    local, big_send, big_recv, swap_send, swap_recv, s1, r1, s2, r2, s3, r3, s4, r4,
):
    f = lax.axis_index("frame")
    t = lax.axis_index("tok")
    x, zl, c = lax.div(f, 8), lax.div(lax.rem(f, 8), 2), lax.rem(f, 2)
    y, zh = lax.div(t, 2), lax.rem(t, 2)
    z = zh * 4 + zl

    def place(r):
        return (r + 2) % 8

    loads = [
        pltpu.make_async_copy(a, b, local.at[n])
        for n, (a, b) in enumerate(
            (
                (patches_hbm, patches), (offset_hbm, offset_in), (piece_hbm, piece_in),
                (wq_hbm, wq), (wk_hbm, wk), (wv_hbm, wv), (wo_hbm, wo), (wu_hbm, wu), (wd_hbm, wd),
                (ck_hbm, ck_in), (cv_hbm, cv_in), (pos_hbm, pos_in), (table_hbm, table),
                (turn_hbm.at[f], turn), (tq_hbm, tq_w), (tk_hbm, tk_w), (tv_hbm, tv_w), (to_hbm, to_w),
            )
        )
    ]
    for load in loads:
        load.start()
    new_all[...] = jnp.zeros_like(new_all)

    def dev(x_at, z_at, y_at, c_at):
        return (x_at * 8 + lax.rem(z_at, 4) * 2 + c_at, y_at * 2 + lax.div(z_at, 4))

    xp, xm = dev(mod(x + 1, 4), z, y, c), dev(mod(x - 1, 4), z, y, c)
    yp, ym = dev(x, z, mod(y + 1, 4), c), dev(x, z, mod(y - 1, 4), c)
    zp, zm = dev(x, mod(z + 1, 8), y, c), dev(x, mod(z - 1, 8), y, c)
    sibling = dev(x, z, y, 1 - c)
    partner = dev(x, mod(z + 4, 8), y, 1 - c)
    after, before = (mod(f + 1, 32), t), (mod(f - 1, 32), t)

    barrier = pltpu.get_barrier_semaphore()
    friends = (xp, xm, yp, ym, zp, zm, sibling, partner, after, before)
    for friend in friends:
        pl.semaphore_signal(barrier, inc=1, device_id=friend, device_id_type=MESH)
    pl.semaphore_wait(barrier, len(friends))

    copies = Copies(big_send, big_recv)
    moves = c != zh

    def remote(src, dst, send, recv, device):
        return pltpu.make_async_remote_copy(
            src_ref=src, dst_ref=dst, send_sem=send, recv_sem=recv,
            device_id=device, device_id_type=MESH,
        )

    def swap(src, dst, n):
        return remote(src, dst, swap_send.at[n], swap_recv.at[n], partner)

    for load in loads[0:3]:
        load.wait()
    meta[0:1, :] = offset_in[...].astype(F32)
    meta[1:2, :] = piece_in[...].astype(F32)

    @pl.when(moves)
    def _():
        swap(patches, xin, 0).start()
        swap(meta, meta_in, 1).start()

    @pl.when(jnp.logical_not(moves))
    def _():
        xin[...] = patches[...]
        meta_in[...] = meta[...]

    for load in loads[3:7]:
        load.wait()
    grow = jnp.where(iota((48, 44), 0) == iota((48, 44), 1), 1.0, 0.0).astype(BF)
    total = None
    for n, w in enumerate((wq, wk, wv, wo)):
        to = jnp.where(
            iota((176, WC), 0) + n * 176 == iota((176, WC), 1), 1.0, 0.0
        ).astype(BF)
        term = dot(dot(grow, w[...]).astype(BF), to)
        total = term if total is None else total + term
    total = total.astype(BF)
    WA[0, 0, place(0)] = total[:, 0:512]
    WA2[0, place(0), 0] = total[:, 512:768]

    def z_first(B):
        def at(r):
            return B.at[0, 0, place(r)]

        waits = [copies.start(at(0), at(-1), zp), copies.start(at(0), at(1), zm)]
        yield
        firsts = []

        def across(run):
            firsts.append(copies.start(B.at[0, 0, run], B.at[0, 3, run], xp))
            firsts.append(copies.start(B.at[0, 0, run], B.at[0, 1, run], xm))

        half = B.shape[4] // 2
        low, high = pl.ds(0, half), pl.ds(half, half)
        for step in range(1, 5):
            for copy in waits:
                copy.wait_recv()
            if step < 3:
                waits = [
                    copies.start(at(-step), at(-step - 1), zp),
                    copies.start(at(step), at(step + 1), zm),
                ]
            elif step == 3:
                waits = [
                    copies.start(B.at[0, 0, place(-3), :, low], B.at[0, 0, place(4), :, low], zp),
                    copies.start(B.at[0, 0, place(3), :, high], B.at[0, 0, place(4), :, high], zm),
                ]
            if step == 2:
                across(pl.ds(0, 5))
            if step == 4:
                across(pl.ds(5, 3))
            if step < 4:
                yield

        def aside(x_at):
            return copies.start(B.at[0, x_at], B.at[1, x_at], sibling)

        sides = [aside(0)]
        yield
        for copy in firsts:
            copy.wait_recv()
        one, two = pl.ds(0, 4), pl.ds(4, 4)
        waits = [
            copies.start(B.at[0, 3, one], B.at[0, 2, one], xp),
            copies.start(B.at[0, 1, two], B.at[0, 2, two], xm),
        ]
        sides += [aside(3), aside(1)]
        yield
        for copy in waits:
            copy.wait_recv()
        sides.append(aside(2))
        yield
        for copy in sides:
            copy.wait_recv()

    def x_first(B):
        here = place(0)
        waits = [
            copies.start(B.at[0, here, 0], B.at[0, here, 3], xp),
            copies.start(B.at[0, here, 0], B.at[0, here, 1], xm),
        ]
        yield
        half = B.shape[4] // 2
        low, high = pl.ds(0, half), pl.ds(half, half)
        for copy in waits:
            copy.wait_recv()
        waits = [
            copies.start(B.at[0, here, 3, :, low], B.at[0, here, 2, :, low], xp),
            copies.start(B.at[0, here, 1, :, high], B.at[0, here, 2, :, high], xm),
        ]
        yield

        def at(r):
            return B.at[0, place(r)]

        one, two = pl.ds(0, 2), pl.ds(2, 2)
        for step in range(5):
            for copy in waits:
                copy.wait_recv()
            if step < 3:
                waits = [
                    copies.start(at(-step), at(-step - 1), zp),
                    copies.start(at(step), at(step + 1), zm),
                ]
                yield
            elif step == 3:
                waits = [
                    copies.start(B.at[0, place(-3), one], B.at[0, place(4), one], zp),
                    copies.start(B.at[0, place(3), two], B.at[0, place(4), two], zm),
                ]
                yield
        side = copies.start(B.at[0], B.at[1], sibling)
        yield
        side.wait_recv()

    def drain(task):
        for _ in task:
            pass

    def ahead(task, count):
        for _ in range(count):
            if next(task, "end") == "end":
                return

    def both(*tasks):
        tasks = list(tasks)
        while tasks:
            for task in list(tasks):
                if next(task, "end") == "end":
                    tasks.remove(task)
            if tasks:
                yield

    load4 = x_first(C)
    load1 = both(z_first(WA), x_first(WA2))
    load2 = both(z_first(WU), x_first(WU2))
    load3 = both(z_first(WD), x_first(WD2))
    ahead(load1, 1)

    for q, (start, size) in enumerate(WINDOWS):
        r, k = iota((size, QW), 0) + start, iota((size, QW), 1)
        at = lax.rem(k, 48)
        hit = (r == 352 * q + lax.div(k, 48) * 44 + at) & (at < 44)
        pad[q, 0:size, :] = jnp.where(hit, 1.0, 0.0).astype(BF)
    valid = lax.rem(iota((1, DP), 1), 48) < 44

    def padded(rows):
        for q, (start, size) in enumerate(WINDOWS):
            res[:, q * QW : (q + 1) * QW] = dot(
                rows[:, start : start + size], pad[q, 0:size, :]
            ).astype(BF)
        normed = norm_padded(res[...].astype(F32), valid)
        return [normed[:, q * QW : (q + 1) * QW] for q in range(4)]

    quarters = padded(patches)
    offset, piece = as_column(meta[0:1, :]), as_column(meta[1:2, :])
    mine = quarters[0]
    for q in range(1, 4):
        mine = jnp.where(piece == float(q), quarters[q], mine)
    comp[...] = mine.astype(BF)
    hops = [
        copies.start(comp, around.at[0], after),
        copies.start(comp, around.at[1], before),
    ]
    for load in loads[7:9]:
        load.wait()
    for w, one, two in ((wu, WU, WU2), (wd, WD, WD2)):
        rows = dot(grow, w[...]).astype(BF)
        one[0, 0, place(0)] = rows[:, 0:512]
        two[0, place(0), 0] = rows[:, 512:768]
    ahead(load1, 1)
    for copy in hops:
        copy.wait_recv()
    earlier = jnp.where(f > 0, around[0].astype(F32), 0.0)
    later = jnp.where(f < FRAMES - 1, around[1].astype(F32), 0.0)
    source = jnp.where(
        offset == -1.0, earlier, jnp.where(offset == 1.0, later, comp[...].astype(F32))
    )
    src[...] = source.astype(BF)

    @pl.when(moves)
    def _():
        swap(src, src_in, 2).start()

    @pl.when(jnp.logical_not(moves))
    def _():
        src_in[...] = src[...]

    ahead(load1, 1)

    def turned(v):
        return jnp.concatenate([v[:, 44:88], v[:, 0:44], v[:, 132:176], v[:, 88:132]], axis=1)

    for load in loads[9:13]:
        load.wait()
    spot = jnp.where(
        iota((CACHE_ROWS, 62), 0) == iota((CACHE_ROWS, 62), 1), pos_in[...].astype(F32), 0.0
    )
    spot = jnp.sum(spot, axis=1, keepdims=True)
    high = jnp.floor(spot * (1.0 / 64))
    lanes = iota((CACHE_ROWS, 64), 1).astype(F32)

    def chosen(at, n):
        hit = jnp.where(lanes == at, 1.0, 0.0)
        both = jnp.dot(hit, table[n], preferred_element_type=F32, precision=lax.Precision.HIGHEST)
        return both[0:62, 0:176], both[0:62, 176:352]

    (cos_a, sin_a), (cos_b, sin_b) = chosen(high, 0), chosen(spot - 64.0 * high, 1)
    cosine, sine = cos_a * cos_b - sin_a * sin_b, sin_a * cos_b + cos_a * sin_b
    sine = jnp.where(lax.rem(iota((62, 176), 1), HD) < HD // 2, -sine, sine)
    raw = ck_in[...].astype(F32)
    C[0, place(0), 0] = jnp.zeros((CACHE_ROWS, CACHE_COLS), BF)
    C[0, place(0), 0, 0:62, 0:176] = (raw * cosine + turned(raw) * sine).astype(BF)
    C[0, place(0), 0, 0:62, 256:432] = cv_in[...]
    ahead(load1, 2)

    @pl.when(moves)
    def _():
        swap(patches, xin, 0).wait()
        swap(meta, meta_in, 1).wait()
        swap(src, src_in, 2).wait()

    quarters = padded(xin)
    piece = as_column(meta_in[1:2, :])
    for q in range(4):
        H1[0, :, q * QW : (q + 1) * QW] = jnp.where(
            piece == float(q), src_in[...].astype(F32), quarters[q]
        ).astype(BF)

    def gather(H):
        a, b = pl.ds(0, 64), pl.ds(64, 64)
        one = copies.start(H.at[0, a], H.at[2, a], yp)
        two = copies.start(H.at[0, b], H.at[1, b], ym)
        rest = [
            copies.start(H.at[0, b], H.at[2, b], yp), copies.start(H.at[0, a], H.at[1, a], ym)
        ]
        yield
        one.wait_recv()
        far = [copies.start(H.at[2, a], H.at[3, a], yp)]
        two.wait_recv()
        far.append(copies.start(H.at[1, b], H.at[3, b], ym))
        yield
        for copy in rest:
            copy.wait_recv()
        yield
        for copy in far:
            copy.wait_recv()

    rows1 = gather(H1)
    ahead(rows1, 1)
    ahead(load2, 2)
    ahead(rows1, 1)
    ahead(load1, 1)
    ahead(load2, 1)
    ahead(rows1, 1)
    ahead(load1, 1)
    drain(load1)

    plane_of = [c, 1 - c]
    x_of = [mod(k - x, 4) for k in range(4)]
    z_of = [lax.rem(k - z + 8 + 2, 8) for k in range(8)]

    def weight(B, at, start, size):
        pieces = []
        for k in range(32):
            p, x_at, z_at = plane_of[k % 2], x_of[k // 8], z_of[at * 4 + k // 2 % 4]
            spot = (p, x_at, z_at) if B.shape[1] == 4 else (p, z_at, x_at)
            pieces.append(B[(*spot, slice(None), slice(start, start + size))])
        return jnp.concatenate(pieces, axis=0)

    def wider(rows, first, columns, start):
        r, k = iota((rows, columns), 0) + first, iota((rows, columns), 1) + start
        at = lax.rem(k, 128)
        return jnp.where((r == lax.div(k, 128) * HD + at) & (at < HD), 1.0, 0.0).astype(BF)

    wide_q, wide_kv = wider(256, 0, 256, 0), wider(512, 128, 512, 256)
    r, k = iota((256, 256), 1) + 512, iota((256, 256), 0)
    at = lax.rem(k, 128)
    narrow = jnp.where(
        (r == 528 + lax.div(k, 128) * HD + at) & (at < HD), 1.0, 0.0
    ).astype(BF)

    sides = []

    def key_value(start, count):
        rows = H1[start : start + count].reshape(count * TOK, DP)
        spot = slice(start * TOK, (start + count) * TOK)
        for at in range(2):
            joined = jnp.concatenate(
                [dot(rows, weight(WA, at, 128, 384)), dot(rows, weight(WA2, at, 0, 128))], axis=1
            )
            KV[0, at, spot, :] = dot(joined.astype(BF), wide_kv).astype(BF)
            part = pl.ds(start * TOK, count * TOK)
            sides.append(copies.start(KV.at[0, at, part], KV.at[1, at, part], sibling))

    key_value(0, 3)
    ahead(load2, 1)
    drain(rows1)
    key_value(3, 1)
    ahead(load2, 1)
    ahead(load3, 1)
    rows = H1[...].reshape(4 * TOK, DP)
    for at in range(2):
        joined = dot(rows, weight(WA, at, 0, 256)).astype(BF)
        Q[at] = dot(joined, wide_q).astype(BF).reshape(4, TOK, 256)
    ahead(load3, 1)
    for copy in sides:
        copy.wait_recv()

    def attend(block, count=1):
        total = None
        for at in range(2):
            heads = []
            for h in range(2):
                span = slice(h * 128, h * 128 + 128)
                vspan = slice(256 + h * 128, 256 + h * 128 + 128)
                q = Q[at, block : block + count, :, span].reshape(count * TOK, 128)
                s = [dot_nt(q, KV[k, at, :, span]) for k in range(2)]
                top = jnp.maximum(
                    jnp.max(s[0], axis=1, keepdims=True), jnp.max(s[1], axis=1, keepdims=True)
                )
                p = [jnp.exp2(part * RATE - top * RATE) for part in s]
                mass = jnp.sum(p[0], axis=1, keepdims=True) + jnp.sum(p[1], axis=1, keepdims=True)
                o = dot(p[0].astype(BF), KV[0, at, :, vspan]) + dot(
                    p[1].astype(BF), KV[1, at, :, vspan]
                )
                heads.append((o / mass).astype(BF))
            both_heads = dot(jnp.concatenate(heads, axis=1), narrow).astype(BF)
            term = dot_nt(both_heads, weight(WA2, at, 0, 256))
            total = term if total is None else total + term
        return total

    def scatter(partial, S, B, R, far_first, between):
        a, b = pl.ds(0, 64), pl.ds(64, 64)

        def send_far():
            S[0] = partial(3, 1).astype(BF)
            return [
                copies.start(S.at[0, a], B.at[0], yp), copies.start(S.at[0, b], B.at[1], ym)
            ]

        def send_near():
            pair = partial(1, 2).astype(BF)
            S[1], S[2] = pair[0:TOK], pair[TOK:]
            return [
                copies.start(S.at[1, b], R.at[0, b], yp), copies.start(S.at[2, a], R.at[1, a], ym)
            ]

        if far_first:
            far = send_far()
            between(0)
            near = send_near()
            between(1)
        else:
            near = send_near()
            far = send_far()
            between(0)
        far[0].wait_recv()
        S[1, 0:64, :] = (S[1, 0:64, :].astype(F32) + B[0].astype(F32)).astype(BF)
        near.append(copies.start(S.at[1, a], R.at[0, a], yp))
        far[1].wait_recv()
        S[2, 64:128, :] = (S[2, 64:128, :].astype(F32) + B[1].astype(F32)).astype(BF)
        near.append(copies.start(S.at[2, b], R.at[1, b], ym))
        own = partial(0, 1)
        between(2)
        for copy in near:
            copy.wait_recv()
        return own + R[0].astype(F32) + R[1].astype(F32)

    def beside_attention(n):
        if n == 0:
            ahead(load2, 1)
            ahead(load3, 1)
            ahead(load4, 1)
        elif n == 1:
            ahead(load3, 1)
            ahead(load2, 1)
            ahead(load4, 1)
        else:
            ahead(load3, 1)
            drain(load2)

    total = scatter(attend, SB, RB, RC, True, beside_attention)
    mixed[...] = (res[...].astype(F32) + total).astype(BF)
    H2[0] = norm_padded(mixed[...].astype(F32), valid).astype(BF)
    rows2 = gather(H2)
    ahead(rows2, 1)
    ahead(load3, 1)
    ahead(load4, 1)

    def up(block, count, at):
        rows = H2[block : block + count].reshape(count * TOK, DP)
        return [
            jax.nn.gelu(dot(rows, weight(WU, at, 0, 512))).astype(BF),
            jax.nn.gelu(dot(rows, weight(WU2, at, 0, 256))).astype(BF),
        ]

    def down(hidden, at):
        return dot_nt(hidden[0], weight(WD, at, 0, 512)) + dot_nt(
            hidden[1], weight(WD2, at, 0, 256)
        )

    def up_down(block, count):
        return down(up(block, count, 0), 0) + down(up(block, count, 1), 1)

    for at in range(2):
        first, second = up(0, 1, at)
        HID[at, :, 0:512] = first
        HID[at, :, 512:768] = second
    ahead(rows2, 1)
    copies.retire(24)
    ahead(load4, 1)
    ahead(rows2, 1)
    ahead(load3, 1)
    drain(load3)

    def far_rows():
        ahead(load4, 1)
        drain(rows2)
        return up_down(3, 1)

    def own_rows():
        own = [(HID[at, :, 0:512], HID[at, :, 512:768]) for at in range(2)]
        return down(own[0], 0) + down(own[1], 1)

    def mlp(block, count):
        return own_rows() if block == 0 else up_down(1, 2) if block == 1 else far_rows()

    def beside_mlp(n):
        if n == 0:
            ahead(load4, 1)
        else:
            ahead(load4, 1)
            copies.retire(8)

    total = scatter(mlp, SB2, RB2, RC2, False, beside_mlp)
    last = (mixed[...].astype(F32) + total).astype(BF)
    columns = [
        dot_nt(last[:, q * QW : (q + 1) * QW], pad[q, 0:size, :])
        for q, (_, size) in enumerate(WINDOWS)
    ]
    parts = [
        columns[0][:, 0:256],
        columns[0][:, 256:384] + columns[1][:, 0:128],
        columns[1][:, 128:384],
        columns[1][:, 384:512] + columns[2][:, 0:128],
        columns[2][:, 128:384],
        columns[2][:, 384:512] + columns[3][:, 0:128],
        columns[3][:, 128:384],
    ]
    plain = jnp.concatenate(parts, axis=1)
    sums[...] = jnp.sum(plain, axis=0, keepdims=True)

    other = f + 1 - 2 * c
    home = f - c + zh
    slot = 2 * y + c

    def share(k):
        return remote(sums, pooled.at[slot], s1, r1, (home, lax.rem(t + k, 8)))

    def all_of(ref, send, recv):
        return remote(ref, ref, send, recv, sibling)

    @pl.when(moves)
    def _():
        share(0).start()

    @pl.when(jnp.logical_not(moves))
    def _():
        pooled[slot] = sums[...]

    for k in range(1, 8):
        share(k).start()

    result[...] = plain.astype(BF)

    @pl.when(moves)
    def _():
        swap(result, swapped, 3).start()

    drain(load4)
    for load in loads[13:]:
        load.wait()

    @pl.when(moves)
    def _():
        all_of(pooled, s1, r1).wait_recv()

    @pl.when(jnp.logical_not(moves))
    def _():
        all_of(pooled.at[pl.ds(0, 7)], s1, r1).wait_recv()

    mean_frame = pooled[0]
    for k in range(1, 8):
        mean_frame = mean_frame + pooled[k]
    mean_frame = mean_frame * (1.0 / P_SIZE)
    center = mean_frame - jnp.sum(mean_frame, axis=1, keepdims=True) * (1.0 / D)
    spread = jnp.sum(center * center, axis=1, keepdims=True) * (1.0 / D)
    normed = center * lax.rsqrt(spread + 1e-06)

    def pick(v):
        got = v[:, 0:176]
        for k in range(1, 8):
            got = jnp.where(t == k, v[:, k * 176 : k * 176 + 176], got)
        return got

    features = jnp.broadcast_to(pick(normed), (8, 176)).astype(BF)
    for n, w in enumerate((tq_w, tk_w, tv_w)):
        part = dot(features, w[...])
        for k in range(8):
            qkv_send[k, n, :, 0:176] = part[0:1, k * 176 : k * 176 + 176]

    def send_heads(k):
        to = lax.rem(t + k, 8)
        return remote(qkv_send.at[to], qkv_recv.at[t], s2, r2, (f, to))

    for k in range(1, 8):
        send_heads(k).start()
    qkv_recv[t] = qkv_send[t]
    all_of(qkv_recv.at[pl.ds(0, 7)], s2, r2).wait_recv()

    whole = []
    for n in range(3):
        v = qkv_recv[0, n, :, 0:176]
        for k in range(1, 8):
            v = v + qkv_recv[k, n, :, 0:176]
        whole.append(v)

    def rot(v):
        return (v * turn[0:1, :] + turned(v) * turn[1:2, :]).astype(BF).astype(F32)

    new_send[...] = jnp.zeros_like(new_send)
    new_send[:, 0:176] = rot(whole[1])
    new_send[:, 256:432] = whole[2].astype(BF).astype(F32)


    @pl.loop(1, 32)
    def _(k):
        remote(new_send, new_all.at[f], s3, r3, (lax.rem(f + k, 32), t)).start()

    new_all[f] = new_send[...]
    query = rot(whole[0])
    lane = iota((1, 176), 1)
    wide_query = jnp.concatenate(
        [jnp.where(lane < HD, query, 0.0), jnp.where(lane >= HD, query, 0.0), jnp.zeros((6, 176), F32)],
        axis=0,
    )
    queries = jnp.concatenate([wide_query, jnp.zeros((8, 80), F32)], axis=1).astype(BF)
    count = 32 * CACHE_ROWS
    cached = [C[:, lax.rem(k - zl + 8 + 2, 8)] for k in range(4)]
    old_keys = jnp.concatenate([part[..., 0:256].reshape(-1, 256) for part in cached], axis=0)
    s_old = dot_nt(queries, old_keys)
    s_old = jnp.where(lax.rem(iota((8, count), 1), CACHE_ROWS) < 62, s_old, -1e30)

    all_of(new_all.at[pl.ds(0, 31)], s3, r3).wait_recv()
    known = new_all[:, 0, :]
    s_new = dot_nt(queries, known[:, 0:256].astype(BF))
    s_new = jnp.where(iota((8, 32), 1) <= f, s_new, -1e30)
    top = jnp.maximum(
        jnp.max(s_old, axis=1, keepdims=True), jnp.max(s_new, axis=1, keepdims=True)
    )
    p_old = jnp.exp2(s_old * RATE - top * RATE)
    p_new = jnp.exp2(s_new * RATE - top * RATE)
    p_old = jnp.where(lax.rem(iota((8, count), 1), CACHE_ROWS) < 62, p_old, 0.0)
    p_new = jnp.where(iota((8, 32), 1) <= f, p_new, 0.0)
    mass = jnp.sum(p_old, axis=1, keepdims=True) + jnp.sum(p_new, axis=1, keepdims=True)
    old_values = jnp.concatenate([part[..., 256:512].reshape(-1, 256) for part in cached], axis=0)
    o = dot(p_old.astype(BF), old_values) + dot(p_new.astype(BF), known[:, 256:512].astype(BF))
    o = o / mass
    temporal = jnp.where(lane < HD, o[0:1, 0:176], o[1:2, 0:176])
    part = dot(jnp.broadcast_to(temporal, (8, 176)).astype(BF), to_w[...])
    for k in range(8):
        last_send[k, :, 0:176] = part[0:1, k * 176 : k * 176 + 176]

    def send_last(k):
        to = lax.rem(t + k, 8)
        return remote(last_send.at[to], last_recv.at[t], s4, r4, (f, to))

    for k in range(1, 8):
        send_last(k).start()
    last_recv[t] = last_send[t]

    stored, kept = (pltpu.make_async_copy(a, out, local.at[0]) for a in (swapped, result))

    @pl.when(moves)
    def _():
        swap(result, swapped, 3).wait()
        stored.start()

    @pl.when(jnp.logical_not(moves))
    def _():
        kept.start()

    copies.retire()

    @pl.when(moves)
    def _():
        all_of(pooled, s1, r1).wait_send()

    @pl.when(jnp.logical_not(moves))
    def _():
        all_of(pooled.at[pl.ds(0, 7)], s1, r1).wait_send()

    all_of(qkv_recv.at[pl.ds(0, 7)], s2, r2).wait_send()
    all_of(new_all.at[pl.ds(0, 31)], s3, r3).wait_send()
    all_of(last_recv.at[pl.ds(0, 7)], s4, r4).wait_recv()
    total = pick(mean_frame)
    for k in range(8):
        total = total + last_recv[k, :, 0:176]
    frame_out[...] = total.astype(BF)
    all_of(last_recv.at[pl.ds(0, 7)], s4, r4).wait_send()

    @pl.when(moves)
    def _():
        stored.wait()

    @pl.when(jnp.logical_not(moves))
    def _():
        kept.wait()


BIG = 176


def call(*operands):
    turn = operands[-1]
    vmem = pl.BlockSpec(memory_space=pltpu.VMEM)
    dma = pltpu.SemaphoreType.DMA
    held = [pltpu.VMEM(a.shape, a.dtype) for a in operands[:-1]] + [
        pltpu.VMEM(turn.shape[1:], F32)
    ]
    return pl.pallas_call(
        kernel,
        out_shape=(
            jax.ShapeDtypeStruct((TOK, D), BF),
            jax.ShapeDtypeStruct((1, 176), BF),
        ),
        in_specs=[pl.BlockSpec(memory_space=pl.ANY)] * len(operands),
        out_specs=(pl.BlockSpec(memory_space=pl.ANY), vmem),
        scratch_shapes=held
        + [
            pltpu.VMEM((2, TOK), F32),
            pltpu.VMEM((TOK, D), BF),
            pltpu.VMEM((2, TOK), F32),
            pltpu.VMEM((TOK, QW), BF),
            pltpu.VMEM((TOK, QW), BF),
            pltpu.VMEM((4, 512, QW), BF),
            pltpu.VMEM((TOK, DP), BF),
            pltpu.VMEM((2, 4, 8, W_ROWS, 512), BF),
            pltpu.VMEM((2, 8, 4, W_ROWS, 256), BF),
            pltpu.VMEM((2, 4, 8, W_ROWS, 512), BF),
            pltpu.VMEM((2, 8, 4, W_ROWS, 256), BF),
            pltpu.VMEM((2, 4, 8, W_ROWS, 512), BF),
            pltpu.VMEM((2, 8, 4, W_ROWS, 256), BF),
            pltpu.VMEM((2, 8, 4, CACHE_ROWS, CACHE_COLS), BF),
            pltpu.VMEM((TOK, QW), BF),
            pltpu.VMEM((2, TOK, QW), BF),
            pltpu.VMEM((4, TOK, DP), BF),
            pltpu.VMEM((2, 2, 4 * TOK, 512), BF),
            pltpu.VMEM((2, 4, TOK, 256), BF),
            pltpu.VMEM((3, TOK, DP), BF),
            pltpu.VMEM((2, 64, DP), BF),
            pltpu.VMEM((2, TOK, DP), BF),
            pltpu.VMEM((TOK, DP), BF),
            pltpu.VMEM((4, TOK, DP), BF),
            pltpu.VMEM((2, TOK, 768), BF),
            pltpu.VMEM((3, TOK, DP), BF),
            pltpu.VMEM((2, 64, DP), BF),
            pltpu.VMEM((2, TOK, DP), BF),
            pltpu.VMEM((TOK, D), BF),
            pltpu.VMEM((TOK, D), BF),
            pltpu.VMEM((1, D), F32),
            pltpu.VMEM((8, 1, D), F32),
            pltpu.VMEM((8, 3, 1, 256), F32),
            pltpu.VMEM((8, 3, 1, 256), F32),
            pltpu.VMEM((1, CACHE_COLS), F32),
            pltpu.VMEM((32, 1, CACHE_COLS), F32),
            pltpu.VMEM((8, 1, 256), F32),
            pltpu.VMEM((8, 1, 256), F32),
            dma((len(operands),)),
            dma((BIG,)), dma((BIG,)),
            dma((4,)), dma((4,)),
            dma, dma, dma, dma, dma, dma, dma, dma,
        ],
        compiler_params=pltpu.CompilerParams(
            collective_id=0, has_side_effects=True, vmem_limit_bytes=56 * 1024 * 1024
        ),
        cost_estimate=pl.CostEstimate(
            flops=8_000_000_000, bytes_accessed=20_000_000, transcendentals=3_000_000
        ),
    )(*operands)


def body(
    patches, shift_offset, shift_slice, w_query, w_key, w_value, w_out, w_up, w_down,
    t_query, t_key, t_value, t_out, cache_keys, cache_values, cache_pos,
):
    half = HD // 2
    freq = np.float32(10000.0) ** (-np.arange(half, dtype=np.float32) / np.float32(half))
    angle = (SPAN + np.arange(FRAMES)).astype(np.float32)[:, None] * freq[None, :]
    cosine, sine = np.cos(angle), np.sin(angle)
    turn = np.stack(
        [
            np.concatenate([cosine] * 4, axis=1),
            np.concatenate([-sine, sine, -sine, sine], axis=1),
        ],
        axis=1,
    ).astype(np.float32)
    steps = np.arange(64)[:, None] * (10000.0 ** (-np.arange(half) / half))[None, :]
    table = np.stack(
        [
            np.concatenate([np.cos(64 * steps)] * 4 + [np.sin(64 * steps)] * 4, axis=1),
            np.concatenate([np.cos(steps)] * 4 + [np.sin(steps)] * 4, axis=1),
        ]
    ).astype(np.float32)
    patch_out, frame_out = call(
        patches[0], shift_offset[None], shift_slice[None], w_query, w_key, w_value,
        w_out.T, w_up, w_down.T, t_query, t_key, t_value, t_out, cache_keys, cache_values, cache_pos[None],
        jnp.asarray(table), jnp.asarray(turn),
    )
    return (patch_out[None], frame_out)


def solution(mesh):
    return jax.shard_map(
        body,
        mesh=mesh,
        in_specs=(
            P("frame", "tok", None),
            P("tok"),
            P("tok"),
            P("frame", "tok"),
            P("frame", "tok"),
            P("frame", "tok"),
            P("tok", "frame"),
            P("frame", "tok"),
            P("tok", "frame"),
            P("tok", None),
            P("tok", None),
            P("tok", None),
            P("tok", None),
            P("frame", "tok"),
            P("frame", "tok"),
            P("frame"),
        ),
        out_specs=(P("frame", "tok", None), P("frame", "tok")),
        check_vma=False,
    )
```

```python
import jax
import jax.numpy as jnp
import numpy as np
from jax import lax
from jax.experimental import pallas as pl
from jax.experimental.pallas import tpu as pltpu
from jax.sharding import PartitionSpec as P

HEADS = 16
HD = 88
P_SIZE = 1024
SPAN = 4096
FRAMES = 32
D = 1408
DP = 1536
QW = 384
TOK = 128
SCALE = HD ** (-0.5)
RATE = SCALE * 1.4426950408889634
MESH = pl.DeviceIdType.MESH
F32 = jnp.float32
BF = jnp.bfloat16
WC = 768
W_ROWS, CACHE_ROWS, CACHE_COLS = 48, 64, 512
WINDOWS = ((0, 384), (256, 512), (640, 512), (1024, 384))


def dot(a, b):
    return jnp.dot(a, b, preferred_element_type=F32)


def dot_nt(a, b):
    return lax.dot_general(a, b, (((1,), (1,)), ((), ())), preferred_element_type=F32)


def iota(shape, axis):
    return lax.broadcasted_iota(jnp.int32, shape, axis)


def mod(a, n):
    return lax.rem(a + n, n)


def remote(src, dst, send, recv, device):
    return pltpu.make_async_remote_copy(
        src_ref=src, dst_ref=dst, send_sem=send, recv_sem=recv,
        device_id=device, device_id_type=MESH,
    )


class Leg:
    def __init__(self, src, dst, device, send, recv):
        self.ends = (src, dst, send, recv, device)

    def start(self):
        remote(*self.ends).start()

    def wait_recv(self):
        remote(*self.ends).wait_recv()

    def wait_send(self):
        remote(*self.ends).wait_send()


class Copies:
    def __init__(self, send, recv):
        self.send, self.recv, self.used, self.open = send, recv, 0, []

    def start(self, src, dst, device):
        n = self.used
        self.used += 1
        copy = pltpu.make_async_remote_copy(
            src_ref=src,
            dst_ref=dst,
            send_sem=self.send.at[n],
            recv_sem=self.recv.at[n],
            device_id=device,
            device_id_type=MESH,
        )
        copy.start()
        self.open.append(copy)
        return copy

    def retire(self, keep=0):
        while len(self.open) > keep:
            self.open.pop(0).wait_send()


def norm_padded(v, valid):
    mean = jnp.sum(v, axis=1, keepdims=True) * (1.0 / D)
    center = jnp.where(valid, v - mean, 0.0)
    spread = jnp.sum(center * center, axis=1, keepdims=True) * (1.0 / D)
    return center * lax.rsqrt(spread + 1e-06)


def as_column(row):
    spread = jnp.where(iota((TOK, TOK), 0) == iota((TOK, TOK), 1), row, 0.0)
    return jnp.sum(spread, axis=1, keepdims=True)


def kernel(
    patches_hbm, offset_hbm, piece_hbm, wq_hbm, wk_hbm, wv_hbm, wo_hbm, wu_hbm, wd_hbm,
    tq_hbm, tk_hbm, tv_hbm, to_hbm, ck_hbm, cv_hbm, pos_hbm, table_hbm, turn_hbm,
    out, frame_out,
    patches, offset_in, piece_in, wq, wk, wv, wo, wu, wd, tq_w, tk_w, tv_w, to_w, ck_in, cv_in, pos_in, table, turn,
    meta, xin, meta_in, src, src_in, via_patches, via_src, pad, res, WA, WU, WU2, WD, WD2, C, comp, around, H1, KV, Q,
    SB, RB, RC, mixed, H2, HID, SB2, RB2, RC2,
    result, swapped, sums, pooled, qkv_send, qkv_recv, new_send, new_all, last_send, last_recv,
    local, big_send, big_recv, swap_send, swap_recv, leg_send, leg_recv, s1, r1, s2, r2, s3, r3, s4, r4,
):
    f = lax.axis_index("frame")
    t = lax.axis_index("tok")
    x, zl, c = lax.div(f, 8), lax.div(lax.rem(f, 8), 2), lax.rem(f, 2)
    y, zh = lax.div(t, 2), lax.rem(t, 2)
    z = zh * 4 + zl

    def place(r):
        return (r + 2) % 8

    loads = [
        pltpu.make_async_copy(a, b, local.at[n])
        for n, (a, b) in enumerate(
            (
                (patches_hbm, patches), (offset_hbm, offset_in), (piece_hbm, piece_in),
                (wq_hbm, wq), (wk_hbm, wk), (wv_hbm, wv), (wo_hbm, wo), (wu_hbm, wu), (wd_hbm, wd),
                (ck_hbm, ck_in), (cv_hbm, cv_in), (pos_hbm, pos_in), (table_hbm, table),
                (turn_hbm.at[f], turn), (tq_hbm, tq_w), (tk_hbm, tk_w), (tv_hbm, tv_w), (to_hbm, to_w),
            )
        )
    ]
    for load in loads:
        load.start()
    new_all[...] = jnp.zeros_like(new_all)

    def dev(x_at, z_at, y_at, c_at):
        return (x_at * 8 + lax.rem(z_at, 4) * 2 + c_at, y_at * 2 + lax.div(z_at, 4))

    xp, xm = dev(mod(x + 1, 4), z, y, c), dev(mod(x - 1, 4), z, y, c)
    yp, ym = dev(x, z, mod(y + 1, 4), c), dev(x, z, mod(y - 1, 4), c)
    zp, zm = dev(x, mod(z + 1, 8), y, c), dev(x, mod(z - 1, 8), y, c)
    sibling = dev(x, z, y, 1 - c)
    partner = dev(x, mod(z + 4, 8), y, 1 - c)
    target_up, target_down = dev(x, mod(z + 3, 8), y, 1 - c), dev(x, mod(z - 3, 8), y, 1 - c)
    after, before = (mod(f + 1, 32), t), (mod(f - 1, 32), t)

    barrier = pltpu.get_barrier_semaphore()
    friends = (xp, xm, yp, ym, zp, zm, sibling, partner, target_up, target_down, after, before)
    for friend in friends:
        pl.semaphore_signal(barrier, inc=1, device_id=friend, device_id_type=MESH)
    pl.semaphore_wait(barrier, len(friends))

    copies = Copies(big_send, big_recv)
    moves = c != zh

    def swap(src, dst, n):
        return remote(src, dst, swap_send.at[n], swap_recv.at[n], partner)

    carries_up = c != lax.div(mod(z - 1, 8), 4)
    carries_down = c != lax.div(mod(z + 1, 8), 4)
    first_rows, last_rows = pl.ds(0, 64), pl.ds(64, 64)

    def legs(n, a, via, b):
        sends = (
            (a.at[first_rows], via.at[0], zp), (a.at[last_rows], via.at[1], zm),
            (via.at[0], b.at[first_rows], target_up), (via.at[1], b.at[last_rows], target_down),
        )
        return [Leg(*ends, leg_send.at[n + k], leg_recv.at[n + k]) for k, ends in enumerate(sends)]

    def hand_on(make):
        @pl.when(carries_up)
        def _():
            make()[0].wait_recv()
            make()[2].start()

        @pl.when(carries_down)
        def _():
            make()[1].wait_recv()
            make()[3].start()

    def patch_legs():
        return legs(0, patches, via_patches, xin)

    def src_legs():
        return legs(4, src, via_src, src_in)

    for load in loads[0:3]:
        load.wait()
    meta[0:1, :] = offset_in[...].astype(F32)
    meta[1:2, :] = piece_in[...].astype(F32)

    @pl.when(moves)
    def _():
        for leg in patch_legs()[0:2]:
            leg.start()
        swap(meta, meta_in, 1).start()

    @pl.when(jnp.logical_not(moves))
    def _():
        xin[...] = patches[...]
        meta_in[...] = meta[...]

    for load in loads[3:7]:
        load.wait()
    grow = jnp.where(iota((48, 44), 0) == iota((48, 44), 1), 1.0, 0.0).astype(BF)
    total = None
    for n, w in enumerate((wq, wk, wv, wo)):
        to = jnp.where(
            iota((176, WC), 0) + n * 176 == iota((176, WC), 1), 1.0, 0.0
        ).astype(BF)
        term = dot(dot(grow, w[...]).astype(BF), to)
        total = term if total is None else total + term
    WA[0, 0, place(0)] = total.astype(BF)

    def z_first(B):
        def at(r):
            return B.at[0, 0, place(r)]

        waits = [copies.start(at(0), at(-1), zp), copies.start(at(0), at(1), zm)]
        yield
        firsts = []

        def across(run):
            firsts.append(copies.start(B.at[0, 0, run], B.at[0, 3, run], xp))
            firsts.append(copies.start(B.at[0, 0, run], B.at[0, 1, run], xm))

        half = B.shape[4] // 2
        low, high = pl.ds(0, half), pl.ds(half, half)
        for step in range(1, 5):
            for copy in waits:
                copy.wait_recv()
            if step < 3:
                waits = [
                    copies.start(at(-step), at(-step - 1), zp),
                    copies.start(at(step), at(step + 1), zm),
                ]
            elif step == 3:
                waits = [
                    copies.start(B.at[0, 0, place(-3), :, low], B.at[0, 0, place(4), :, low], zp),
                    copies.start(B.at[0, 0, place(3), :, high], B.at[0, 0, place(4), :, high], zm),
                ]
            if step == 2:
                across(pl.ds(0, 5))
            if step == 4:
                across(pl.ds(5, 3))
            if step < 4:
                yield

        def aside(x_at):
            return copies.start(B.at[0, x_at], B.at[1, x_at], sibling)

        sides = [aside(0)]
        yield
        for copy in firsts:
            copy.wait_recv()
        one, two = pl.ds(0, 4), pl.ds(4, 4)
        waits = [
            copies.start(B.at[0, 3, one], B.at[0, 2, one], xp),
            copies.start(B.at[0, 1, two], B.at[0, 2, two], xm),
        ]
        sides += [aside(3), aside(1)]
        yield
        for copy in waits:
            copy.wait_recv()
        sides.append(aside(2))
        yield
        for copy in sides:
            copy.wait_recv()

    def x_first(B):
        here = place(0)
        waits = [
            copies.start(B.at[0, here, 0], B.at[0, here, 3], xp),
            copies.start(B.at[0, here, 0], B.at[0, here, 1], xm),
        ]
        yield
        half = B.shape[4] // 2
        low, high = pl.ds(0, half), pl.ds(half, half)
        for copy in waits:
            copy.wait_recv()
        waits = [
            copies.start(B.at[0, here, 3, :, low], B.at[0, here, 2, :, low], xp),
            copies.start(B.at[0, here, 1, :, high], B.at[0, here, 2, :, high], xm),
        ]
        yield

        def at(r):
            return B.at[0, place(r)]

        one, two = pl.ds(0, 2), pl.ds(2, 2)
        for step in range(5):
            for copy in waits:
                copy.wait_recv()
            if step < 3:
                waits = [
                    copies.start(at(-step), at(-step - 1), zp),
                    copies.start(at(step), at(step + 1), zm),
                ]
                yield
            elif step == 3:
                waits = [
                    copies.start(B.at[0, place(-3), one], B.at[0, place(4), one], zp),
                    copies.start(B.at[0, place(3), two], B.at[0, place(4), two], zm),
                ]
                yield
        side = copies.start(B.at[0], B.at[1], sibling)
        yield
        side.wait_recv()

    def drain(task):
        for _ in task:
            pass

    def ahead(task, count):
        for _ in range(count):
            if next(task, "end") == "end":
                return

    def both(*tasks):
        tasks = list(tasks)
        while tasks:
            for task in list(tasks):
                if next(task, "end") == "end":
                    tasks.remove(task)
            if tasks:
                yield

    load1, load4 = z_first(WA), x_first(C)
    load2 = both(z_first(WU), x_first(WU2))
    load3 = both(z_first(WD), x_first(WD2))
    ahead(load1, 1)
    hand_on(patch_legs)

    for q, (start, size) in enumerate(WINDOWS):
        r, k = iota((size, QW), 0) + start, iota((size, QW), 1)
        at = lax.rem(k, 48)
        hit = (r == 352 * q + lax.div(k, 48) * 44 + at) & (at < 44)
        pad[q, 0:size, :] = jnp.where(hit, 1.0, 0.0).astype(BF)
    valid = lax.rem(iota((1, DP), 1), 48) < 44

    def padded(rows):
        for q, (start, size) in enumerate(WINDOWS):
            res[:, q * QW : (q + 1) * QW] = dot(
                rows[:, start : start + size], pad[q, 0:size, :]
            ).astype(BF)
        normed = norm_padded(res[...].astype(F32), valid)
        return [normed[:, q * QW : (q + 1) * QW] for q in range(4)]

    quarters = padded(patches)
    offset, piece = as_column(meta[0:1, :]), as_column(meta[1:2, :])
    mine = quarters[0]
    for q in range(1, 4):
        mine = jnp.where(piece == float(q), quarters[q], mine)
    comp[...] = mine.astype(BF)
    hops = [
        copies.start(comp, around.at[0], after),
        copies.start(comp, around.at[1], before),
    ]
    for load in loads[7:9]:
        load.wait()
    for w, one, two in ((wu, WU, WU2), (wd, WD, WD2)):
        rows = dot(grow, w[...]).astype(BF)
        one[0, 0, place(0)] = rows[:, 0:512]
        two[0, place(0), 0] = rows[:, 512:768]
    ahead(load1, 1)
    for copy in hops:
        copy.wait_recv()
    earlier = jnp.where(f > 0, around[0].astype(F32), 0.0)
    later = jnp.where(f < FRAMES - 1, around[1].astype(F32), 0.0)
    source = jnp.where(
        offset == -1.0, earlier, jnp.where(offset == 1.0, later, comp[...].astype(F32))
    )
    src[...] = source.astype(BF)

    @pl.when(moves)
    def _():
        for leg in src_legs()[0:2]:
            leg.start()

    @pl.when(jnp.logical_not(moves))
    def _():
        src_in[...] = src[...]

    ahead(load1, 1)
    hand_on(src_legs)

    def turned(v):
        return jnp.concatenate([v[:, 44:88], v[:, 0:44], v[:, 132:176], v[:, 88:132]], axis=1)

    for load in loads[9:13]:
        load.wait()
    spot = jnp.where(
        iota((CACHE_ROWS, 62), 0) == iota((CACHE_ROWS, 62), 1), pos_in[...].astype(F32), 0.0
    )
    spot = jnp.sum(spot, axis=1, keepdims=True)
    high = jnp.floor(spot * (1.0 / 64))
    lanes = iota((CACHE_ROWS, 64), 1).astype(F32)

    def chosen(at, n):
        hit = jnp.where(lanes == at, 1.0, 0.0)
        both = jnp.dot(hit, table[n], preferred_element_type=F32, precision=lax.Precision.HIGHEST)
        return both[0:62, 0:176], both[0:62, 176:352]

    (cos_a, sin_a), (cos_b, sin_b) = chosen(high, 0), chosen(spot - 64.0 * high, 1)
    cosine, sine = cos_a * cos_b - sin_a * sin_b, sin_a * cos_b + cos_a * sin_b
    sine = jnp.where(lax.rem(iota((62, 176), 1), HD) < HD // 2, -sine, sine)
    raw = ck_in[...].astype(F32)
    C[0, place(0), 0] = jnp.zeros((CACHE_ROWS, CACHE_COLS), BF)
    C[0, place(0), 0, 0:62, 0:176] = (raw * cosine + turned(raw) * sine).astype(BF)
    C[0, place(0), 0, 0:62, 256:432] = cv_in[...]
    ahead(load1, 2)

    @pl.when(moves)
    def _():
        swap(meta, meta_in, 1).wait()
        for leg in patch_legs()[2:4] + src_legs()[2:4]:
            leg.wait_recv()

    quarters = padded(xin)
    piece = as_column(meta_in[1:2, :])
    for q in range(4):
        H1[0, :, q * QW : (q + 1) * QW] = jnp.where(
            piece == float(q), src_in[...].astype(F32), quarters[q]
        ).astype(BF)

    def gather(H):
        a, b = pl.ds(0, 64), pl.ds(64, 64)
        one = copies.start(H.at[0, a], H.at[2, a], yp)
        two = copies.start(H.at[0, b], H.at[1, b], ym)
        rest = [
            copies.start(H.at[0, b], H.at[2, b], yp), copies.start(H.at[0, a], H.at[1, a], ym)
        ]
        yield
        one.wait_recv()
        far = [copies.start(H.at[2, a], H.at[3, a], yp)]
        two.wait_recv()
        far.append(copies.start(H.at[1, b], H.at[3, b], ym))
        yield
        for copy in rest:
            copy.wait_recv()
        yield
        for copy in far:
            copy.wait_recv()

    rows1 = gather(H1)
    ahead(rows1, 1)
    ahead(load2, 2)
    ahead(rows1, 1)
    ahead(load1, 1)
    ahead(load2, 1)
    ahead(rows1, 1)
    ahead(load1, 1)
    drain(load1)

    plane_of = [c, 1 - c]
    x_of = [mod(k - x, 4) for k in range(4)]
    z_of = [lax.rem(k - z + 8 + 2, 8) for k in range(8)]

    def weight(B, at, start, size):
        pieces = []
        for k in range(32):
            p, x_at, z_at = plane_of[k % 2], x_of[k // 8], z_of[at * 4 + k // 2 % 4]
            spot = (p, x_at, z_at) if B.shape[1] == 4 else (p, z_at, x_at)
            pieces.append(B[(*spot, slice(None), slice(start, start + size))])
        return jnp.concatenate(pieces, axis=0)

    def wider(rows, first, columns, start):
        r, k = iota((rows, columns), 0) + first, iota((rows, columns), 1) + start
        at = lax.rem(k, 128)
        return jnp.where((r == lax.div(k, 128) * HD + at) & (at < HD), 1.0, 0.0).astype(BF)

    wide_q, wide_kv = wider(256, 0, 256, 0), wider(512, 128, 512, 256)
    r, k = iota((256, 256), 1) + 512, iota((256, 256), 0)
    at = lax.rem(k, 128)
    narrow = jnp.where(
        (r == 528 + lax.div(k, 128) * HD + at) & (at < HD), 1.0, 0.0
    ).astype(BF)

    sides = []

    def key_value(start, count):
        rows = H1[start : start + count].reshape(count * TOK, DP)
        spot = slice(start * TOK, (start + count) * TOK)
        for at in range(2):
            joined = dot(rows, weight(WA, at, 128, 512)).astype(BF)
            KV[0, at, spot, :] = dot(joined, wide_kv).astype(BF)
            part = pl.ds(start * TOK, count * TOK)
            sides.append(copies.start(KV.at[0, at, part], KV.at[1, at, part], sibling))

    key_value(0, 3)
    ahead(load2, 1)
    drain(rows1)
    key_value(3, 1)
    ahead(load2, 1)
    ahead(load3, 1)
    rows = H1[...].reshape(4 * TOK, DP)
    for at in range(2):
        joined = dot(rows, weight(WA, at, 0, 256)).astype(BF)
        Q[at] = dot(joined, wide_q).astype(BF).reshape(4, TOK, 256)
    ahead(load3, 1)
    for copy in sides:
        copy.wait_recv()

    def attend(block, count=1):
        total = None
        for at in range(2):
            heads = []
            for h in range(2):
                span = slice(h * 128, h * 128 + 128)
                vspan = slice(256 + h * 128, 256 + h * 128 + 128)
                q = Q[at, block : block + count, :, span].reshape(count * TOK, 128)
                s = [dot_nt(q, KV[k, at, :, span]) for k in range(2)]
                top = jnp.maximum(
                    jnp.max(s[0], axis=1, keepdims=True), jnp.max(s[1], axis=1, keepdims=True)
                )
                p = [jnp.exp2(part * RATE - top * RATE) for part in s]
                mass = jnp.sum(p[0], axis=1, keepdims=True) + jnp.sum(p[1], axis=1, keepdims=True)
                o = dot(p[0].astype(BF), KV[0, at, :, vspan]) + dot(
                    p[1].astype(BF), KV[1, at, :, vspan]
                )
                heads.append((o / mass).astype(BF))
            both_heads = dot(jnp.concatenate(heads, axis=1), narrow).astype(BF)
            term = dot_nt(both_heads, weight(WA, at, 512, 256))
            total = term if total is None else total + term
        return total

    def scatter(partial, S, B, R, far_first, between):
        a, b = pl.ds(0, 64), pl.ds(64, 64)

        def send_far():
            S[0] = partial(3, 1).astype(BF)
            return [
                copies.start(S.at[0, a], B.at[0], yp), copies.start(S.at[0, b], B.at[1], ym)
            ]

        def send_near():
            pair = partial(1, 2).astype(BF)
            S[1], S[2] = pair[0:TOK], pair[TOK:]
            return [
                copies.start(S.at[1, b], R.at[0, b], yp), copies.start(S.at[2, a], R.at[1, a], ym)
            ]

        if far_first:
            far = send_far()
            between(0)
            near = send_near()
            between(1)
        else:
            near = send_near()
            far = send_far()
            between(0)
        far[0].wait_recv()
        S[1, 0:64, :] = (S[1, 0:64, :].astype(F32) + B[0].astype(F32)).astype(BF)
        near.append(copies.start(S.at[1, a], R.at[0, a], yp))
        far[1].wait_recv()
        S[2, 64:128, :] = (S[2, 64:128, :].astype(F32) + B[1].astype(F32)).astype(BF)
        near.append(copies.start(S.at[2, b], R.at[1, b], ym))
        own = partial(0, 1)
        between(2)
        for copy in near:
            copy.wait_recv()
        return own + R[0].astype(F32) + R[1].astype(F32)

    def beside_attention(n):
        if n == 0:
            ahead(load2, 1)
            ahead(load3, 1)
            ahead(load4, 1)
        elif n == 1:
            ahead(load3, 1)
            ahead(load2, 1)
            ahead(load4, 1)
        else:
            ahead(load3, 1)
            drain(load2)

    total = scatter(attend, SB, RB, RC, True, beside_attention)
    mixed[...] = (res[...].astype(F32) + total).astype(BF)
    H2[0] = norm_padded(mixed[...].astype(F32), valid).astype(BF)
    rows2 = gather(H2)
    ahead(rows2, 1)
    ahead(load3, 1)
    ahead(load4, 1)

    def up(block, count, at):
        rows = H2[block : block + count].reshape(count * TOK, DP)
        return [
            jax.nn.gelu(dot(rows, weight(WU, at, 0, 512))).astype(BF),
            jax.nn.gelu(dot(rows, weight(WU2, at, 0, 256))).astype(BF),
        ]

    def down(hidden, at):
        return dot_nt(hidden[0], weight(WD, at, 0, 512)) + dot_nt(
            hidden[1], weight(WD2, at, 0, 256)
        )

    def up_down(block, count):
        return down(up(block, count, 0), 0) + down(up(block, count, 1), 1)

    for at in range(2):
        first, second = up(0, 1, at)
        HID[at, :, 0:512] = first
        HID[at, :, 512:768] = second
    ahead(rows2, 1)
    copies.retire(24)
    ahead(load4, 1)
    ahead(rows2, 1)
    ahead(load3, 1)
    drain(load3)

    def far_rows():
        ahead(load4, 1)
        drain(rows2)
        return up_down(3, 1)

    def own_rows():
        own = [(HID[at, :, 0:512], HID[at, :, 512:768]) for at in range(2)]
        return down(own[0], 0) + down(own[1], 1)

    def mlp(block, count):
        return own_rows() if block == 0 else up_down(1, 2) if block == 1 else far_rows()

    def beside_mlp(n):
        if n == 0:
            ahead(load4, 1)
        else:
            ahead(load4, 1)
            copies.retire(8)

    total = scatter(mlp, SB2, RB2, RC2, False, beside_mlp)
    last = (mixed[...].astype(F32) + total).astype(BF)
    columns = [
        dot_nt(last[:, q * QW : (q + 1) * QW], pad[q, 0:size, :])
        for q, (_, size) in enumerate(WINDOWS)
    ]
    parts = [
        columns[0][:, 0:256],
        columns[0][:, 256:384] + columns[1][:, 0:128],
        columns[1][:, 128:384],
        columns[1][:, 384:512] + columns[2][:, 0:128],
        columns[2][:, 128:384],
        columns[2][:, 384:512] + columns[3][:, 0:128],
        columns[3][:, 128:384],
    ]
    plain = jnp.concatenate(parts, axis=1)
    sums[...] = jnp.sum(plain, axis=0, keepdims=True)

    other = f + 1 - 2 * c
    home = f - c + zh
    slot = 2 * y + c

    def share(k):
        return remote(sums, pooled.at[slot], s1, r1, (home, lax.rem(t + k, 8)))

    def all_of(ref, send, recv):
        return remote(ref, ref, send, recv, sibling)

    @pl.when(moves)
    def _():
        share(0).start()

    @pl.when(jnp.logical_not(moves))
    def _():
        pooled[slot] = sums[...]

    for k in range(1, 8):
        share(k).start()

    result[...] = plain.astype(BF)

    @pl.when(moves)
    def _():
        swap(result, swapped, 3).start()

    drain(load4)
    for load in loads[13:]:
        load.wait()

    @pl.when(moves)
    def _():
        all_of(pooled, s1, r1).wait_recv()

    @pl.when(jnp.logical_not(moves))
    def _():
        all_of(pooled.at[pl.ds(0, 7)], s1, r1).wait_recv()

    mean_frame = pooled[0]
    for k in range(1, 8):
        mean_frame = mean_frame + pooled[k]
    mean_frame = mean_frame * (1.0 / P_SIZE)
    center = mean_frame - jnp.sum(mean_frame, axis=1, keepdims=True) * (1.0 / D)
    spread = jnp.sum(center * center, axis=1, keepdims=True) * (1.0 / D)
    normed = center * lax.rsqrt(spread + 1e-06)

    def pick(v):
        got = v[:, 0:176]
        for k in range(1, 8):
            got = jnp.where(t == k, v[:, k * 176 : k * 176 + 176], got)
        return got

    features = jnp.broadcast_to(pick(normed), (8, 176)).astype(BF)
    for n, w in enumerate((tq_w, tk_w, tv_w)):
        part = dot(features, w[...])
        for k in range(8):
            qkv_send[k, n, :, 0:176] = part[0:1, k * 176 : k * 176 + 176]

    def send_heads(k):
        to = lax.rem(t + k, 8)
        return remote(qkv_send.at[to], qkv_recv.at[t], s2, r2, (f, to))

    for k in range(1, 8):
        send_heads(k).start()
    qkv_recv[t] = qkv_send[t]
    all_of(qkv_recv.at[pl.ds(0, 7)], s2, r2).wait_recv()

    whole = []
    for n in range(3):
        v = qkv_recv[0, n, :, 0:176]
        for k in range(1, 8):
            v = v + qkv_recv[k, n, :, 0:176]
        whole.append(v)

    def rot(v):
        return (v * turn[0:1, :] + turned(v) * turn[1:2, :]).astype(BF).astype(F32)

    new_send[...] = jnp.zeros_like(new_send)
    new_send[:, 0:176] = rot(whole[1])
    new_send[:, 256:432] = whole[2].astype(BF).astype(F32)


    @pl.loop(1, 32)
    def _(k):
        remote(new_send, new_all.at[f], s3, r3, (lax.rem(f + k, 32), t)).start()

    new_all[f] = new_send[...]
    query = rot(whole[0])
    lane = iota((1, 176), 1)
    wide_query = jnp.concatenate(
        [jnp.where(lane < HD, query, 0.0), jnp.where(lane >= HD, query, 0.0), jnp.zeros((6, 176), F32)],
        axis=0,
    )
    queries = jnp.concatenate([wide_query, jnp.zeros((8, 80), F32)], axis=1).astype(BF)
    count = 32 * CACHE_ROWS
    cached = [C[:, lax.rem(k - zl + 8 + 2, 8)] for k in range(4)]
    old_keys = jnp.concatenate([part[..., 0:256].reshape(-1, 256) for part in cached], axis=0)
    s_old = dot_nt(queries, old_keys)
    s_old = jnp.where(lax.rem(iota((8, count), 1), CACHE_ROWS) < 62, s_old, -1e30)

    all_of(new_all.at[pl.ds(0, 31)], s3, r3).wait_recv()
    known = new_all[:, 0, :]
    s_new = dot_nt(queries, known[:, 0:256].astype(BF))
    s_new = jnp.where(iota((8, 32), 1) <= f, s_new, -1e30)
    top = jnp.maximum(
        jnp.max(s_old, axis=1, keepdims=True), jnp.max(s_new, axis=1, keepdims=True)
    )
    p_old = jnp.exp2(s_old * RATE - top * RATE)
    p_new = jnp.exp2(s_new * RATE - top * RATE)
    p_old = jnp.where(lax.rem(iota((8, count), 1), CACHE_ROWS) < 62, p_old, 0.0)
    p_new = jnp.where(iota((8, 32), 1) <= f, p_new, 0.0)
    mass = jnp.sum(p_old, axis=1, keepdims=True) + jnp.sum(p_new, axis=1, keepdims=True)
    old_values = jnp.concatenate([part[..., 256:512].reshape(-1, 256) for part in cached], axis=0)
    o = dot(p_old.astype(BF), old_values) + dot(p_new.astype(BF), known[:, 256:512].astype(BF))
    o = o / mass
    temporal = jnp.where(lane < HD, o[0:1, 0:176], o[1:2, 0:176])
    part = dot(jnp.broadcast_to(temporal, (8, 176)).astype(BF), to_w[...])
    for k in range(8):
        last_send[k, :, 0:176] = part[0:1, k * 176 : k * 176 + 176]

    def send_last(k):
        to = lax.rem(t + k, 8)
        return remote(last_send.at[to], last_recv.at[t], s4, r4, (f, to))

    for k in range(1, 8):
        send_last(k).start()
    last_recv[t] = last_send[t]

    stored, kept = (pltpu.make_async_copy(a, out, local.at[0]) for a in (swapped, result))

    @pl.when(moves)
    def _():
        swap(result, swapped, 3).wait()
        stored.start()

    @pl.when(jnp.logical_not(moves))
    def _():
        kept.start()

    copies.retire()

    @pl.when(moves)
    def _():
        for leg in patch_legs()[0:2] + src_legs()[0:2]:
            leg.wait_send()

    @pl.when(carries_up)
    def _():
        patch_legs()[2].wait_send()
        src_legs()[2].wait_send()

    @pl.when(carries_down)
    def _():
        patch_legs()[3].wait_send()
        src_legs()[3].wait_send()

    @pl.when(moves)
    def _():
        all_of(pooled, s1, r1).wait_send()

    @pl.when(jnp.logical_not(moves))
    def _():
        all_of(pooled.at[pl.ds(0, 7)], s1, r1).wait_send()

    all_of(qkv_recv.at[pl.ds(0, 7)], s2, r2).wait_send()
    all_of(new_all.at[pl.ds(0, 31)], s3, r3).wait_send()
    all_of(last_recv.at[pl.ds(0, 7)], s4, r4).wait_recv()
    total = pick(mean_frame)
    for k in range(8):
        total = total + last_recv[k, :, 0:176]
    frame_out[...] = total.astype(BF)
    all_of(last_recv.at[pl.ds(0, 7)], s4, r4).wait_send()

    @pl.when(moves)
    def _():
        stored.wait()

    @pl.when(jnp.logical_not(moves))
    def _():
        kept.wait()


BIG = 176


def call(*operands):
    turn = operands[-1]
    vmem = pl.BlockSpec(memory_space=pltpu.VMEM)
    dma = pltpu.SemaphoreType.DMA
    held = [pltpu.VMEM(a.shape, a.dtype) for a in operands[:-1]] + [
        pltpu.VMEM(turn.shape[1:], F32)
    ]
    return pl.pallas_call(
        kernel,
        out_shape=(
            jax.ShapeDtypeStruct((TOK, D), BF),
            jax.ShapeDtypeStruct((1, 176), BF),
        ),
        in_specs=[pl.BlockSpec(memory_space=pl.ANY)] * len(operands),
        out_specs=(pl.BlockSpec(memory_space=pl.ANY), vmem),
        scratch_shapes=held
        + [
            pltpu.VMEM((2, TOK), F32),
            pltpu.VMEM((TOK, D), BF),
            pltpu.VMEM((2, TOK), F32),
            pltpu.VMEM((TOK, QW), BF),
            pltpu.VMEM((TOK, QW), BF),
            pltpu.VMEM((2, 64, D), BF),
            pltpu.VMEM((2, 64, QW), BF),
            pltpu.VMEM((4, 512, QW), BF),
            pltpu.VMEM((TOK, DP), BF),
            pltpu.VMEM((2, 4, 8, W_ROWS, WC), BF),
            pltpu.VMEM((2, 4, 8, W_ROWS, 512), BF),
            pltpu.VMEM((2, 8, 4, W_ROWS, 256), BF),
            pltpu.VMEM((2, 4, 8, W_ROWS, 512), BF),
            pltpu.VMEM((2, 8, 4, W_ROWS, 256), BF),
            pltpu.VMEM((2, 8, 4, CACHE_ROWS, CACHE_COLS), BF),
            pltpu.VMEM((TOK, QW), BF),
            pltpu.VMEM((2, TOK, QW), BF),
            pltpu.VMEM((4, TOK, DP), BF),
            pltpu.VMEM((2, 2, 4 * TOK, 512), BF),
            pltpu.VMEM((2, 4, TOK, 256), BF),
            pltpu.VMEM((3, TOK, DP), BF),
            pltpu.VMEM((2, 64, DP), BF),
            pltpu.VMEM((2, TOK, DP), BF),
            pltpu.VMEM((TOK, DP), BF),
            pltpu.VMEM((4, TOK, DP), BF),
            pltpu.VMEM((2, TOK, 768), BF),
            pltpu.VMEM((3, TOK, DP), BF),
            pltpu.VMEM((2, 64, DP), BF),
            pltpu.VMEM((2, TOK, DP), BF),
            pltpu.VMEM((TOK, D), BF),
            pltpu.VMEM((TOK, D), BF),
            pltpu.VMEM((1, D), F32),
            pltpu.VMEM((8, 1, D), F32),
            pltpu.VMEM((8, 3, 1, 256), F32),
            pltpu.VMEM((8, 3, 1, 256), F32),
            pltpu.VMEM((1, CACHE_COLS), F32),
            pltpu.VMEM((32, 1, CACHE_COLS), F32),
            pltpu.VMEM((8, 1, 256), F32),
            pltpu.VMEM((8, 1, 256), F32),
            dma((len(operands),)),
            dma((BIG,)), dma((BIG,)),
            dma((4,)), dma((4,)),
            dma((8,)), dma((8,)),
            dma, dma, dma, dma, dma, dma, dma, dma,
        ],
        compiler_params=pltpu.CompilerParams(
            collective_id=0, has_side_effects=True, vmem_limit_bytes=56 * 1024 * 1024
        ),
        cost_estimate=pl.CostEstimate(
            flops=8_000_000_000, bytes_accessed=20_000_000, transcendentals=3_000_000
        ),
    )(*operands)


def body(
    patches, shift_offset, shift_slice, w_query, w_key, w_value, w_out, w_up, w_down,
    t_query, t_key, t_value, t_out, cache_keys, cache_values, cache_pos,
):
    half = HD // 2
    freq = np.float32(10000.0) ** (-np.arange(half, dtype=np.float32) / np.float32(half))
    angle = (SPAN + np.arange(FRAMES)).astype(np.float32)[:, None] * freq[None, :]
    cosine, sine = np.cos(angle), np.sin(angle)
    turn = np.stack(
        [
            np.concatenate([cosine] * 4, axis=1),
            np.concatenate([-sine, sine, -sine, sine], axis=1),
        ],
        axis=1,
    ).astype(np.float32)
    steps = np.arange(64)[:, None] * (10000.0 ** (-np.arange(half) / half))[None, :]
    table = np.stack(
        [
            np.concatenate([np.cos(64 * steps)] * 4 + [np.sin(64 * steps)] * 4, axis=1),
            np.concatenate([np.cos(steps)] * 4 + [np.sin(steps)] * 4, axis=1),
        ]
    ).astype(np.float32)
    patch_out, frame_out = call(
        patches[0], shift_offset[None], shift_slice[None], w_query, w_key, w_value,
        w_out.T, w_up, w_down.T, t_query, t_key, t_value, t_out, cache_keys, cache_values, cache_pos[None],
        jnp.asarray(table), jnp.asarray(turn),
    )
    return (patch_out[None], frame_out)


def solution(mesh):
    return jax.shard_map(
        body,
        mesh=mesh,
        in_specs=(
            P("frame", "tok", None),
            P("tok"),
            P("tok"),
            P("frame", "tok"),
            P("frame", "tok"),
            P("frame", "tok"),
            P("tok", "frame"),
            P("frame", "tok"),
            P("tok", "frame"),
            P("tok", None),
            P("tok", None),
            P("tok", None),
            P("tok", None),
            P("frame", "tok"),
            P("frame", "tok"),
            P("frame"),
        ),
        out_specs=(P("frame", "tok", None), P("frame", "tok")),
        check_vma=False,
    )
```

```python
import jax
import jax.numpy as jnp
import numpy as np
from jax import lax
from jax.experimental import pallas as pl
from jax.experimental.pallas import tpu as pltpu
from jax.sharding import PartitionSpec as P

HEADS = 16
HD = 88
P_SIZE = 1024
SPAN = 4096
FRAMES = 32
D = 1408
DP = 1536
QW = 384
TOK = 128
SCALE = HD ** (-0.5)
RATE = SCALE * 1.4426950408889634
MESH = pl.DeviceIdType.MESH
F32 = jnp.float32
BF = jnp.bfloat16
WC = 768
W_ROWS, CACHE_ROWS, CACHE_COLS = 48, 64, 512
WINDOWS = ((0, 384), (256, 512), (640, 512), (1024, 384))


def dot(a, b):
    return jnp.dot(a, b, preferred_element_type=F32)


def dot_nt(a, b):
    return lax.dot_general(a, b, (((1,), (1,)), ((), ())), preferred_element_type=F32)


def iota(shape, axis):
    return lax.broadcasted_iota(jnp.int32, shape, axis)


def mod(a, n):
    return lax.rem(a + n, n)


def remote(src, dst, send, recv, device):
    return pltpu.make_async_remote_copy(
        src_ref=src, dst_ref=dst, send_sem=send, recv_sem=recv,
        device_id=device, device_id_type=MESH,
    )


class Leg:
    def __init__(self, src, dst, device, send, recv):
        self.ends = (src, dst, send, recv, device)

    def start(self):
        remote(*self.ends).start()

    def wait_recv(self):
        remote(*self.ends).wait_recv()

    def wait_send(self):
        remote(*self.ends).wait_send()


class Copies:
    def __init__(self, send, recv):
        self.send, self.recv, self.used, self.open = send, recv, 0, []

    def make(self, src, dst, device):
        n = self.used
        self.used += 1
        copy = Leg(src, dst, device, self.send.at[n], self.recv.at[n])
        self.open.append(copy)
        return copy

    def start(self, src, dst, device):
        copy = self.make(src, dst, device)
        copy.start()
        return copy

    def retire(self, keep=0):
        while len(self.open) > keep:
            self.open.pop(0).wait_send()


def norm_padded(v, valid):
    mean = jnp.sum(v, axis=1, keepdims=True) * (1.0 / D)
    center = jnp.where(valid, v - mean, 0.0)
    spread = jnp.sum(center * center, axis=1, keepdims=True) * (1.0 / D)
    return center * lax.rsqrt(spread + 1e-06)


def as_column(row):
    spread = jnp.where(iota((TOK, TOK), 0) == iota((TOK, TOK), 1), row, 0.0)
    return jnp.sum(spread, axis=1, keepdims=True)


def kernel(
    patches_hbm, offset_hbm, piece_hbm, wq_hbm, wk_hbm, wv_hbm, wo_hbm, wu_hbm, wd_hbm,
    tq_hbm, tk_hbm, tv_hbm, to_hbm, ck_hbm, cv_hbm, pos_hbm, table_hbm, turn_hbm,
    out, frame_out,
    patches, offset_in, piece_in, wq, wk, wv, wo, wu, wd, tq_w, tk_w, tv_w, to_w, ck_in, cv_in, pos_in, table, turn,
    meta, xin, meta_in, src, src_in, via_patches, via_src, pad, res, WA, WA2, WU, WU2, WD, WD2, C, comp, around, H1, KV, Q,
    SB, RB, RC, mixed, H2, HID, PB, SB2, RB2, RC2,
    result, swapped, sums, pooled, qkv_send, qkv_recv, new_send, new_all, last_send, last_recv,
    local, big_send, big_recv, swap_send, swap_recv, leg_send, leg_recv, s1, r1, s2, r2, s3, r3, s4, r4,
):
    f = lax.axis_index("frame")
    t = lax.axis_index("tok")
    x, zl, c = lax.div(f, 8), lax.div(lax.rem(f, 8), 2), lax.rem(f, 2)
    y, zh = lax.div(t, 2), lax.rem(t, 2)
    z = zh * 4 + zl

    def place(r):
        return (r + 2) % 8

    loads = [
        pltpu.make_async_copy(a, b, local.at[n])
        for n, (a, b) in enumerate(
            (
                (patches_hbm, patches), (offset_hbm, offset_in), (piece_hbm, piece_in),
                (wq_hbm, wq), (wk_hbm, wk), (wv_hbm, wv), (wo_hbm, wo), (wu_hbm, wu), (wd_hbm, wd),
                (ck_hbm, ck_in), (cv_hbm, cv_in), (pos_hbm, pos_in), (table_hbm, table),
                (turn_hbm.at[f], turn), (tq_hbm, tq_w), (tk_hbm, tk_w), (tv_hbm, tv_w), (to_hbm, to_w),
            )
        )
    ]
    for load in loads:
        load.start()
    new_all[...] = jnp.zeros_like(new_all)

    def dev(x_at, z_at, y_at, c_at):
        return (x_at * 8 + lax.rem(z_at, 4) * 2 + c_at, y_at * 2 + lax.div(z_at, 4))

    xp, xm = dev(mod(x + 1, 4), z, y, c), dev(mod(x - 1, 4), z, y, c)
    yp, ym = dev(x, z, mod(y + 1, 4), c), dev(x, z, mod(y - 1, 4), c)
    zp, zm = dev(x, mod(z + 1, 8), y, c), dev(x, mod(z - 1, 8), y, c)
    sibling = dev(x, z, y, 1 - c)
    partner = dev(x, mod(z + 4, 8), y, 1 - c)
    target_up, target_down = dev(x, mod(z + 3, 8), y, 1 - c), dev(x, mod(z - 3, 8), y, 1 - c)
    after, before = (mod(f + 1, 32), t), (mod(f - 1, 32), t)

    barrier = pltpu.get_barrier_semaphore()
    friends = (xp, xm, yp, ym, zp, zm, sibling, partner, target_up, target_down, after, before)
    for friend in friends:
        pl.semaphore_signal(barrier, inc=1, device_id=friend, device_id_type=MESH)
    pl.semaphore_wait(barrier, len(friends))

    copies = Copies(big_send, big_recv)
    moves = c != zh

    def swap(src, dst, n):
        return remote(src, dst, swap_send.at[n], swap_recv.at[n], partner)

    carries_up = c != lax.div(mod(z - 1, 8), 4)
    carries_down = c != lax.div(mod(z + 1, 8), 4)
    first_rows, last_rows = pl.ds(0, 64), pl.ds(64, 64)

    def legs(n, a, via, b):
        sends = (
            (a.at[first_rows], via.at[0], zp), (a.at[last_rows], via.at[1], zm),
            (via.at[0], b.at[first_rows], target_up), (via.at[1], b.at[last_rows], target_down),
        )
        return [Leg(*ends, leg_send.at[n + k], leg_recv.at[n + k]) for k, ends in enumerate(sends)]

    def hand_on(make):
        @pl.when(carries_up)
        def _():
            make()[0].wait_recv()
            make()[2].start()

        @pl.when(carries_down)
        def _():
            make()[1].wait_recv()
            make()[3].start()

    def patch_legs():
        return legs(0, patches, via_patches, xin)

    def src_legs():
        return legs(4, src, via_src, src_in)

    for load in loads[0:3]:
        load.wait()
    meta[0:1, :] = offset_in[...].astype(F32)
    meta[1:2, :] = piece_in[...].astype(F32)

    @pl.when(moves)
    def _():
        for leg in patch_legs()[0:2]:
            leg.start()
        swap(meta, meta_in, 1).start()

    for load in loads[3:7]:
        load.wait()
    grow = jnp.where(iota((48, 44), 0) == iota((48, 44), 1), 1.0, 0.0).astype(BF)
    total = None
    for n, w in enumerate((wq, wk, wv, wo)):
        to = jnp.where(
            iota((176, WC), 0) + n * 176 == iota((176, WC), 1), 1.0, 0.0
        ).astype(BF)
        term = dot(dot(grow, w[...]).astype(BF), to)
        total = term if total is None else total + term
    total = total.astype(BF)
    WA[0, 0, place(0)] = total[:, 0:640]
    WA2[0, place(0), 0] = total[:, 640:768]

    def z_first(B):
        def at(r):
            return B.at[0, 0, place(r)]

        waits = [copies.start(at(0), at(-1), zp), copies.start(at(0), at(1), zm)]
        yield
        firsts = []

        def across(run):
            firsts.append(copies.start(B.at[0, 0, run], B.at[0, 3, run], xp))
            firsts.append(copies.start(B.at[0, 0, run], B.at[0, 1, run], xm))

        half = B.shape[4] // 256 * 128
        low, high = pl.ds(0, half), pl.ds(half, B.shape[4] - half)
        for step in range(1, 5):
            for copy in waits:
                copy.wait_recv()
            if step < 3:
                waits = [
                    copies.start(at(-step), at(-step - 1), zp),
                    copies.start(at(step), at(step + 1), zm),
                ]
            elif step == 3:
                waits = [
                    copies.start(B.at[0, 0, place(-3), :, low], B.at[0, 0, place(4), :, low], zp),
                    copies.start(B.at[0, 0, place(3), :, high], B.at[0, 0, place(4), :, high], zm),
                ]
            if step == 2:
                across(pl.ds(0, 5))
            if step == 4:
                across(pl.ds(5, 3))
            if step < 4:
                yield

        def aside(x_at):
            return copies.start(B.at[0, x_at], B.at[1, x_at], sibling)

        sides = [aside(0)]
        yield
        for copy in firsts:
            copy.wait_recv()
        one, two = pl.ds(0, 4), pl.ds(4, 4)
        waits = [
            copies.start(B.at[0, 3, one], B.at[0, 2, one], xp),
            copies.start(B.at[0, 1, two], B.at[0, 2, two], xm),
        ]
        sides += [aside(3), aside(1)]
        yield
        for copy in waits:
            copy.wait_recv()
        sides.append(aside(2))
        yield
        for copy in sides:
            copy.wait_recv()

    def x_first(B):
        here = place(0)
        waits = [
            copies.start(B.at[0, here, 0], B.at[0, here, 3], xp),
            copies.start(B.at[0, here, 0], B.at[0, here, 1], xm),
        ]
        yield
        low, high = pl.ds(0, 32), pl.ds(32, B.shape[3] - 32)
        for copy in waits:
            copy.wait_recv()
        waits = [
            copies.start(B.at[0, here, 3, low], B.at[0, here, 2, low], xp),
            copies.start(B.at[0, here, 1, high], B.at[0, here, 2, high], xm),
        ]
        yield

        def at(r):
            return B.at[0, place(r)]

        one, two = pl.ds(0, 2), pl.ds(2, 2)
        for step in range(5):
            for copy in waits:
                copy.wait_recv()
            if step < 3:
                waits = [
                    copies.start(at(-step), at(-step - 1), zp),
                    copies.start(at(step), at(step + 1), zm),
                ]
                yield
            elif step == 3:
                waits = [
                    copies.start(B.at[0, place(-3), one], B.at[0, place(4), one], zp),
                    copies.start(B.at[0, place(3), two], B.at[0, place(4), two], zm),
                ]
                yield
        side = copies.start(B.at[0], B.at[1], sibling)
        yield
        side.wait_recv()

    def drain(task):
        for _ in task:
            pass

    def ahead(task, count):
        for _ in range(count):
            if next(task, "end") == "end":
                return

    def both(*tasks):
        tasks = list(tasks)
        while tasks:
            for task in list(tasks):
                if next(task, "end") == "end":
                    tasks.remove(task)
            if tasks:
                yield

    load1, load_out, load4 = z_first(WA), x_first(WA2), x_first(C)
    load2 = both(z_first(WU), x_first(WU2))
    load3 = both(z_first(WD), x_first(WD2))
    ahead(load1, 1)
    ahead(load_out, 1)
    hand_on(patch_legs)

    for q, (start, size) in enumerate(WINDOWS):
        r, k = iota((size, QW), 0) + start, iota((size, QW), 1)
        at = lax.rem(k, 48)
        hit = (r == 352 * q + lax.div(k, 48) * 44 + at) & (at < 44)
        pad[q, 0:size, :] = jnp.where(hit, 1.0, 0.0).astype(BF)
    valid = lax.rem(iota((1, DP), 1), 48) < 44

    def padded(rows):
        for q, (start, size) in enumerate(WINDOWS):
            res[:, q * QW : (q + 1) * QW] = dot(
                rows[:, start : start + size], pad[q, 0:size, :]
            ).astype(BF)
        normed = norm_padded(res[...].astype(F32), valid)
        return [normed[:, q * QW : (q + 1) * QW] for q in range(4)]

    quarters = padded(patches)
    offset, piece = as_column(meta[0:1, :]), as_column(meta[1:2, :])
    mine = quarters[0]
    for q in range(1, 4):
        mine = jnp.where(piece == float(q), quarters[q], mine)
    comp[...] = mine.astype(BF)
    for q in range(4):
        H1[0, :, q * QW : (q + 1) * QW] = quarters[q].astype(BF)
    hops = [
        copies.start(comp, around.at[0], after),
        copies.start(comp, around.at[1], before),
    ]
    for load in loads[7:9]:
        load.wait()
    for w, one, two in ((wu, WU, WU2), (wd, WD, WD2)):
        rows = dot(grow, w[...]).astype(BF)
        one[0, 0, place(0)] = rows[:, 0:512]
        two[0, place(0), 0] = rows[:, 512:768]
    ahead(load1, 1)
    ahead(load_out, 1)
    for copy in hops:
        copy.wait_recv()
    earlier = jnp.where(f > 0, around[0].astype(F32), 0.0)
    later = jnp.where(f < FRAMES - 1, around[1].astype(F32), 0.0)
    source = jnp.where(
        offset == -1.0, earlier, jnp.where(offset == 1.0, later, comp[...].astype(F32))
    )
    src[...] = source.astype(BF)

    def gather(H):
        a, b = pl.ds(0, 64), pl.ds(64, 64)
        one = copies.make(H.at[0, a], H.at[2, a], yp)
        two = copies.make(H.at[0, b], H.at[1, b], ym)
        rest = [
            copies.make(H.at[0, b], H.at[2, b], yp), copies.make(H.at[0, a], H.at[1, a], ym)
        ]
        far = [
            copies.make(H.at[2, a], H.at[3, a], yp), copies.make(H.at[1, b], H.at[3, b], ym)
        ]

        def begin():
            for copy in (one, two, *rest):
                copy.start()

        def forward():
            one.wait_recv()
            far[0].start()
            two.wait_recv()
            far[1].start()

        def near():
            for copy in rest:
                copy.wait_recv()

        def last():
            for copy in far:
                copy.wait_recv()

        return begin, forward, near, last

    begin1, forward1, near1, last1 = gather(H1)
    stays = jnp.logical_not(moves)

    @pl.when(moves)
    def _():
        for leg in src_legs()[0:2]:
            leg.start()

    @pl.when(stays)
    def _():
        for q in range(4):
            columns = slice(q * QW, (q + 1) * QW)
            H1[0, :, columns] = jnp.where(
                piece == float(q), src[...].astype(F32), H1[0, :, columns].astype(F32)
            ).astype(BF)
        begin1()

    ahead(load1, 1)
    hand_on(src_legs)

    def turned(v):
        return jnp.concatenate([v[:, 44:88], v[:, 0:44], v[:, 132:176], v[:, 88:132]], axis=1)

    for load in loads[9:13]:
        load.wait()
    spot = jnp.where(
        iota((CACHE_ROWS, 62), 0) == iota((CACHE_ROWS, 62), 1), pos_in[...].astype(F32), 0.0
    )
    spot = jnp.sum(spot, axis=1, keepdims=True)
    high = jnp.floor(spot * (1.0 / 64))
    lanes = iota((CACHE_ROWS, 64), 1).astype(F32)

    def chosen(at, n):
        hit = jnp.where(lanes == at, 1.0, 0.0)
        both = jnp.dot(hit, table[n], preferred_element_type=F32, precision=lax.Precision.HIGHEST)
        return both[0:62, 0:176], both[0:62, 176:352]

    (cos_a, sin_a), (cos_b, sin_b) = chosen(high, 0), chosen(spot - 64.0 * high, 1)
    cosine, sine = cos_a * cos_b - sin_a * sin_b, sin_a * cos_b + cos_a * sin_b
    sine = jnp.where(lax.rem(iota((62, 176), 1), HD) < HD // 2, -sine, sine)
    raw = ck_in[...].astype(F32)
    C[0, place(0), 0] = jnp.zeros((CACHE_ROWS, CACHE_COLS), BF)
    C[0, place(0), 0, 0:62, 0:176] = (raw * cosine + turned(raw) * sine).astype(BF)
    C[0, place(0), 0, 0:62, 256:432] = cv_in[...]
    ahead(load1, 2)

    pl.when(stays)(forward1)

    @pl.when(moves)
    def _():
        swap(meta, meta_in, 1).wait()
        for leg in patch_legs()[2:4] + src_legs()[2:4]:
            leg.wait_recv()
        quarters = padded(xin)
        piece = as_column(meta_in[1:2, :])
        for q in range(4):
            H1[0, :, q * QW : (q + 1) * QW] = jnp.where(
                piece == float(q), src_in[...].astype(F32), quarters[q]
            ).astype(BF)
        begin1()

    ahead(load_out, 1)
    ahead(load2, 2)
    pl.when(moves)(forward1)
    ahead(load1, 1)
    ahead(load2, 1)
    ahead(load_out, 1)
    near1()
    ahead(load2, 1)
    ahead(load_out, 1)
    last1()
    ahead(load1, 1)
    drain(load1)
    ahead(load2, 1)

    plane_of = [c, 1 - c]
    x_of = [mod(k - x, 4) for k in range(4)]
    z_of = [lax.rem(k - z + 8 + 2, 8) for k in range(8)]

    def weight(B, at, start, size):
        pieces = []
        for k in range(32):
            p, x_at, z_at = plane_of[k % 2], x_of[k // 8], z_of[at * 4 + k // 2 % 4]
            spot = (p, x_at, z_at) if B.shape[1] == 4 else (p, z_at, x_at)
            pieces.append(B[(*spot, slice(None), slice(start, start + size))])
        return jnp.concatenate(pieces, axis=0)

    def wider(rows, first, columns, start):
        r, k = iota((rows, columns), 0) + first, iota((rows, columns), 1) + start
        at = lax.rem(k, 128)
        return jnp.where((r == lax.div(k, 128) * HD + at) & (at < HD), 1.0, 0.0).astype(BF)

    wide_q, wide_kv = wider(256, 0, 256, 0), wider(512, 128, 512, 256)
    r, k = iota((256, 256), 1) + 512, iota((256, 256), 0)
    at = lax.rem(k, 128)
    narrow = jnp.where(
        (r == 528 + lax.div(k, 128) * HD + at) & (at < HD), 1.0, 0.0
    ).astype(BF)

    sides = []

    def key_value(start, count):
        rows = H1[start : start + count].reshape(count * TOK, DP)
        spot = slice(start * TOK, (start + count) * TOK)
        for at in range(2):
            joined = dot(rows, weight(WA, at, 128, 512)).astype(BF)
            KV[0, at, spot, :] = dot(joined, wide_kv).astype(BF)
            part = pl.ds(start * TOK, count * TOK)
            sides.append(copies.start(KV.at[0, at, part], KV.at[1, at, part], sibling))

    key_value(0, 4)
    ahead(load_out, 1)
    ahead(load3, 1)
    rows = H1[...].reshape(4 * TOK, DP)
    for at in range(2):
        joined = dot(rows, weight(WA, at, 0, 256)).astype(BF)
        Q[at] = dot(joined, wide_q).astype(BF).reshape(4, TOK, 256)
    ahead(load_out, 1)
    ahead(load3, 1)
    for copy in sides:
        copy.wait_recv()
    drain(load_out)
    ahead(load2, 1)
    ahead(load3, 1)

    def attend(block, count=1):
        total = None
        for at in range(2):
            heads = []
            for h in range(2):
                span = slice(h * 128, h * 128 + 128)
                vspan = slice(256 + h * 128, 256 + h * 128 + 128)
                q = Q[at, block : block + count, :, span].reshape(count * TOK, 128)
                s = [dot_nt(q, KV[k, at, :, span]) for k in range(2)]
                top = jnp.maximum(
                    jnp.max(s[0], axis=1, keepdims=True), jnp.max(s[1], axis=1, keepdims=True)
                )
                p = [jnp.exp2(part * RATE - top * RATE) for part in s]
                mass = jnp.sum(p[0], axis=1, keepdims=True) + jnp.sum(p[1], axis=1, keepdims=True)
                o = dot(p[0].astype(BF), KV[0, at, :, vspan]) + dot(
                    p[1].astype(BF), KV[1, at, :, vspan]
                )
                heads.append((o / mass).astype(BF))
            both_heads = dot(jnp.concatenate(heads, axis=1), narrow).astype(BF)
            term = dot_nt(both_heads[:, 0:128], weight(WA, at, 512, 128)) + dot_nt(
                both_heads[:, 128:256], weight(WA2, at, 0, 128)
            )
            total = term if total is None else total + term
        return total

    def scatter(partial, S, B, R, far_first, between):
        a, b = pl.ds(0, 64), pl.ds(64, 64)

        def send_far():
            S[0] = partial(3, 1).astype(BF)
            return [
                copies.start(S.at[0, a], B.at[0], yp), copies.start(S.at[0, b], B.at[1], ym)
            ]

        def send_near():
            if far_first:
                S[1] = partial(1, 1).astype(BF)
                one = copies.start(S.at[1, b], R.at[0, b], yp)
                between(1)
                S[2] = partial(2, 1).astype(BF)
            else:
                pair = partial(1, 2).astype(BF)
                S[1], S[2] = pair[0:TOK], pair[TOK:]
                one = copies.start(S.at[1, b], R.at[0, b], yp)
            return [one, copies.start(S.at[2, a], R.at[1, a], ym)]

        if far_first:
            far = send_far()
            between(0)
            near = send_near()
            between(2)
        else:
            near = send_near()
            far = send_far()
            between(0)
        far[0].wait_recv()
        S[1, 0:64, :] = (S[1, 0:64, :].astype(F32) + B[0].astype(F32)).astype(BF)
        near.append(copies.start(S.at[1, a], R.at[0, a], yp))
        far[1].wait_recv()
        S[2, 64:128, :] = (S[2, 64:128, :].astype(F32) + B[1].astype(F32)).astype(BF)
        near.append(copies.start(S.at[2, b], R.at[1, b], ym))
        own = partial(0, 1)
        between(3)
        for copy in near:
            copy.wait_recv()
        return own + R[0].astype(F32) + R[1].astype(F32)

    def beside_attention(n):
        if n == 0:
            ahead(load3, 1)
        elif n == 1:
            ahead(load2, 1)
            ahead(load3, 1)
        elif n == 2:
            drain(load2)
            ahead(load4, 1)
        else:
            ahead(load3, 1)
            ahead(load4, 1)

    total = scatter(attend, SB, RB, RC, True, beside_attention)
    mixed[...] = (res[...].astype(F32) + total).astype(BF)
    H2[0] = norm_padded(mixed[...].astype(F32), valid).astype(BF)
    begin2, forward2, near2, last2 = gather(H2)
    begin2()
    ahead(load3, 1)
    ahead(load4, 1)

    def up(block, count, at):
        rows = H2[block : block + count].reshape(count * TOK, DP)
        return [
            jax.nn.gelu(dot(rows, weight(WU, at, 0, 512))).astype(BF),
            jax.nn.gelu(dot(rows, weight(WU2, at, 0, 256))).astype(BF),
        ]

    def down(hidden, at):
        return dot_nt(hidden[0], weight(WD, at, 0, 512)) + dot_nt(
            hidden[1], weight(WD2, at, 0, 256)
        )

    def up_down(block, count):
        return down(up(block, count, 0), 0) + down(up(block, count, 1), 1)

    for at in range(2):
        first, second = up(0, 1, at)
        HID[at, :, 0:512] = first
        HID[at, :, 512:768] = second
    forward2()
    drain(load3)
    own = [(HID[at, :, 0:512], HID[at, :, 512:768]) for at in range(2)]
    PB[...] = down(own[0], 0) + down(own[1], 1)
    copies.retire(28)
    near2()

    def far_rows():
        ahead(load4, 1)
        last2()
        return up_down(3, 1)

    def mlp(block, count):
        return PB[...] if block == 0 else up_down(1, 2) if block == 1 else far_rows()

    def beside_mlp(n):
        ahead(load4, 1)
        if n == 3:
            copies.retire(12)
            ahead(load4, 1)

    total = scatter(mlp, SB2, RB2, RC2, False, beside_mlp)
    last = (mixed[...].astype(F32) + total).astype(BF)
    columns = [
        dot_nt(last[:, q * QW : (q + 1) * QW], pad[q, 0:size, :])
        for q, (_, size) in enumerate(WINDOWS)
    ]
    parts = [
        columns[0][:, 0:256],
        columns[0][:, 256:384] + columns[1][:, 0:128],
        columns[1][:, 128:384],
        columns[1][:, 384:512] + columns[2][:, 0:128],
        columns[2][:, 128:384],
        columns[2][:, 384:512] + columns[3][:, 0:128],
        columns[3][:, 128:384],
    ]
    plain = jnp.concatenate(parts, axis=1)
    sums[...] = jnp.sum(plain, axis=0, keepdims=True)

    other = f + 1 - 2 * c
    home = f - c + zh
    slot = 2 * y + c

    def share(k):
        return remote(sums, pooled.at[slot], s1, r1, (home, lax.rem(t + k, 8)))

    def all_of(ref, send, recv):
        return remote(ref, ref, send, recv, sibling)

    @pl.when(moves)
    def _():
        share(0).start()

    @pl.when(jnp.logical_not(moves))
    def _():
        pooled[slot] = sums[...]

    for k in range(1, 8):
        share(k).start()

    result[...] = plain.astype(BF)

    @pl.when(moves)
    def _():
        swap(result, swapped, 3).start()

    drain(load4)
    for load in loads[13:]:
        load.wait()

    @pl.when(moves)
    def _():
        all_of(pooled, s1, r1).wait_recv()

    @pl.when(jnp.logical_not(moves))
    def _():
        all_of(pooled.at[pl.ds(0, 7)], s1, r1).wait_recv()

    mean_frame = pooled[0]
    for k in range(1, 8):
        mean_frame = mean_frame + pooled[k]
    mean_frame = mean_frame * (1.0 / P_SIZE)
    center = mean_frame - jnp.sum(mean_frame, axis=1, keepdims=True) * (1.0 / D)
    spread = jnp.sum(center * center, axis=1, keepdims=True) * (1.0 / D)
    normed = center * lax.rsqrt(spread + 1e-06)

    def pick(v):
        got = v[:, 0:176]
        for k in range(1, 8):
            got = jnp.where(t == k, v[:, k * 176 : k * 176 + 176], got)
        return got

    features = jnp.broadcast_to(pick(normed), (8, 176)).astype(BF)
    for n, w in enumerate((tq_w, tk_w, tv_w)):
        part = dot(features, w[...])
        for k in range(8):
            qkv_send[k, n, :, 0:176] = part[0:1, k * 176 : k * 176 + 176]

    def send_heads(k):
        to = lax.rem(t + k, 8)
        return remote(qkv_send.at[to], qkv_recv.at[t], s2, r2, (f, to))

    for k in range(1, 8):
        send_heads(k).start()
    qkv_recv[t] = qkv_send[t]
    all_of(qkv_recv.at[pl.ds(0, 7)], s2, r2).wait_recv()

    whole = []
    for n in range(3):
        v = qkv_recv[0, n, :, 0:176]
        for k in range(1, 8):
            v = v + qkv_recv[k, n, :, 0:176]
        whole.append(v)

    def rot(v):
        return (v * turn[0:1, :] + turned(v) * turn[1:2, :]).astype(BF).astype(F32)

    new_send[...] = jnp.zeros_like(new_send)
    new_send[:, 0:176] = rot(whole[1])
    new_send[:, 256:432] = whole[2].astype(BF).astype(F32)


    @pl.loop(1, 32)
    def _(k):
        remote(new_send, new_all.at[f], s3, r3, (lax.rem(f + k, 32), t)).start()

    new_all[f] = new_send[...]
    query = rot(whole[0])
    lane = iota((1, 176), 1)
    wide_query = jnp.concatenate(
        [jnp.where(lane < HD, query, 0.0), jnp.where(lane >= HD, query, 0.0), jnp.zeros((6, 176), F32)],
        axis=0,
    )
    queries = jnp.concatenate([wide_query, jnp.zeros((8, 80), F32)], axis=1).astype(BF)
    count = 32 * CACHE_ROWS
    cached = [C[:, lax.rem(k - zl + 8 + 2, 8)] for k in range(4)]
    old_keys = jnp.concatenate([part[..., 0:256].reshape(-1, 256) for part in cached], axis=0)
    s_old = dot_nt(queries, old_keys)
    s_old = jnp.where(lax.rem(iota((8, count), 1), CACHE_ROWS) < 62, s_old, -1e30)

    all_of(new_all.at[pl.ds(0, 31)], s3, r3).wait_recv()
    known = new_all[:, 0, :]
    s_new = dot_nt(queries, known[:, 0:256].astype(BF))
    s_new = jnp.where(iota((8, 32), 1) <= f, s_new, -1e30)
    top = jnp.maximum(
        jnp.max(s_old, axis=1, keepdims=True), jnp.max(s_new, axis=1, keepdims=True)
    )
    p_old = jnp.exp2(s_old * RATE - top * RATE)
    p_new = jnp.exp2(s_new * RATE - top * RATE)
    p_old = jnp.where(lax.rem(iota((8, count), 1), CACHE_ROWS) < 62, p_old, 0.0)
    p_new = jnp.where(iota((8, 32), 1) <= f, p_new, 0.0)
    mass = jnp.sum(p_old, axis=1, keepdims=True) + jnp.sum(p_new, axis=1, keepdims=True)
    old_values = jnp.concatenate([part[..., 256:512].reshape(-1, 256) for part in cached], axis=0)
    o = dot(p_old.astype(BF), old_values) + dot(p_new.astype(BF), known[:, 256:512].astype(BF))
    o = o / mass
    temporal = jnp.where(lane < HD, o[0:1, 0:176], o[1:2, 0:176])
    part = dot(jnp.broadcast_to(temporal, (8, 176)).astype(BF), to_w[...])
    for k in range(8):
        last_send[k, :, 0:176] = part[0:1, k * 176 : k * 176 + 176]

    def send_last(k):
        to = lax.rem(t + k, 8)
        return remote(last_send.at[to], last_recv.at[t], s4, r4, (f, to))

    for k in range(1, 8):
        send_last(k).start()
    last_recv[t] = last_send[t]

    stored, kept = (pltpu.make_async_copy(a, out, local.at[0]) for a in (swapped, result))

    @pl.when(moves)
    def _():
        swap(result, swapped, 3).wait()
        stored.start()

    @pl.when(jnp.logical_not(moves))
    def _():
        kept.start()

    copies.retire()

    @pl.when(moves)
    def _():
        for leg in patch_legs()[0:2] + src_legs()[0:2]:
            leg.wait_send()

    @pl.when(carries_up)
    def _():
        patch_legs()[2].wait_send()
        src_legs()[2].wait_send()

    @pl.when(carries_down)
    def _():
        patch_legs()[3].wait_send()
        src_legs()[3].wait_send()

    @pl.when(moves)
    def _():
        all_of(pooled, s1, r1).wait_send()

    @pl.when(jnp.logical_not(moves))
    def _():
        all_of(pooled.at[pl.ds(0, 7)], s1, r1).wait_send()

    all_of(qkv_recv.at[pl.ds(0, 7)], s2, r2).wait_send()
    all_of(new_all.at[pl.ds(0, 31)], s3, r3).wait_send()
    all_of(last_recv.at[pl.ds(0, 7)], s4, r4).wait_recv()
    total = pick(mean_frame)
    for k in range(8):
        total = total + last_recv[k, :, 0:176]
    frame_out[...] = total.astype(BF)
    all_of(last_recv.at[pl.ds(0, 7)], s4, r4).wait_send()

    @pl.when(moves)
    def _():
        stored.wait()

    @pl.when(jnp.logical_not(moves))
    def _():
        kept.wait()


BIG = 176


def call(*operands):
    turn = operands[-1]
    vmem = pl.BlockSpec(memory_space=pltpu.VMEM)
    dma = pltpu.SemaphoreType.DMA
    held = [pltpu.VMEM(a.shape, a.dtype) for a in operands[:-1]] + [
        pltpu.VMEM(turn.shape[1:], F32)
    ]
    return pl.pallas_call(
        kernel,
        out_shape=(
            jax.ShapeDtypeStruct((TOK, D), BF),
            jax.ShapeDtypeStruct((1, 176), BF),
        ),
        in_specs=[pl.BlockSpec(memory_space=pl.ANY)] * len(operands),
        out_specs=(pl.BlockSpec(memory_space=pl.ANY), vmem),
        scratch_shapes=held
        + [
            pltpu.VMEM((2, TOK), F32),
            pltpu.VMEM((TOK, D), BF),
            pltpu.VMEM((2, TOK), F32),
            pltpu.VMEM((TOK, QW), BF),
            pltpu.VMEM((TOK, QW), BF),
            pltpu.VMEM((2, 64, D), BF),
            pltpu.VMEM((2, 64, QW), BF),
            pltpu.VMEM((4, 512, QW), BF),
            pltpu.VMEM((TOK, DP), BF),
            pltpu.VMEM((2, 4, 8, W_ROWS, 640), BF),
            pltpu.VMEM((2, 8, 4, W_ROWS, 128), BF),
            pltpu.VMEM((2, 4, 8, W_ROWS, 512), BF),
            pltpu.VMEM((2, 8, 4, W_ROWS, 256), BF),
            pltpu.VMEM((2, 4, 8, W_ROWS, 512), BF),
            pltpu.VMEM((2, 8, 4, W_ROWS, 256), BF),
            pltpu.VMEM((2, 8, 4, CACHE_ROWS, CACHE_COLS), BF),
            pltpu.VMEM((TOK, QW), BF),
            pltpu.VMEM((2, TOK, QW), BF),
            pltpu.VMEM((4, TOK, DP), BF),
            pltpu.VMEM((2, 2, 4 * TOK, 512), BF),
            pltpu.VMEM((2, 4, TOK, 256), BF),
            pltpu.VMEM((3, TOK, DP), BF),
            pltpu.VMEM((2, 64, DP), BF),
            pltpu.VMEM((2, TOK, DP), BF),
            pltpu.VMEM((TOK, DP), BF),
            pltpu.VMEM((4, TOK, DP), BF),
            pltpu.VMEM((2, TOK, 768), BF),
            pltpu.VMEM((TOK, DP), F32),
            pltpu.VMEM((3, TOK, DP), BF),
            pltpu.VMEM((2, 64, DP), BF),
            pltpu.VMEM((2, TOK, DP), BF),
            pltpu.VMEM((TOK, D), BF),
            pltpu.VMEM((TOK, D), BF),
            pltpu.VMEM((1, D), F32),
            pltpu.VMEM((8, 1, D), F32),
            pltpu.VMEM((8, 3, 1, 256), F32),
            pltpu.VMEM((8, 3, 1, 256), F32),
            pltpu.VMEM((1, CACHE_COLS), F32),
            pltpu.VMEM((32, 1, CACHE_COLS), F32),
            pltpu.VMEM((8, 1, 256), F32),
            pltpu.VMEM((8, 1, 256), F32),
            dma((len(operands),)),
            dma((BIG,)), dma((BIG,)),
            dma((4,)), dma((4,)),
            dma((8,)), dma((8,)),
            dma, dma, dma, dma, dma, dma, dma, dma,
        ],
        compiler_params=pltpu.CompilerParams(
            collective_id=0, has_side_effects=True, vmem_limit_bytes=56 * 1024 * 1024
        ),
        cost_estimate=pl.CostEstimate(
            flops=8_000_000_000, bytes_accessed=20_000_000, transcendentals=3_000_000
        ),
    )(*operands)


def body(
    patches, shift_offset, shift_slice, w_query, w_key, w_value, w_out, w_up, w_down,
    t_query, t_key, t_value, t_out, cache_keys, cache_values, cache_pos,
):
    half = HD // 2
    freq = np.float32(10000.0) ** (-np.arange(half, dtype=np.float32) / np.float32(half))
    angle = (SPAN + np.arange(FRAMES)).astype(np.float32)[:, None] * freq[None, :]
    cosine, sine = np.cos(angle), np.sin(angle)
    turn = np.stack(
        [
            np.concatenate([cosine] * 4, axis=1),
            np.concatenate([-sine, sine, -sine, sine], axis=1),
        ],
        axis=1,
    ).astype(np.float32)
    steps = np.arange(64)[:, None] * (10000.0 ** (-np.arange(half) / half))[None, :]
    table = np.stack(
        [
            np.concatenate([np.cos(64 * steps)] * 4 + [np.sin(64 * steps)] * 4, axis=1),
            np.concatenate([np.cos(steps)] * 4 + [np.sin(steps)] * 4, axis=1),
        ]
    ).astype(np.float32)
    patch_out, frame_out = call(
        patches[0], shift_offset[None], shift_slice[None], w_query, w_key, w_value,
        w_out.T, w_up, w_down.T, t_query, t_key, t_value, t_out, cache_keys, cache_values, cache_pos[None],
        jnp.asarray(table), jnp.asarray(turn),
    )
    return (patch_out[None], frame_out)


def solution(mesh):
    return jax.shard_map(
        body,
        mesh=mesh,
        in_specs=(
            P("frame", "tok", None),
            P("tok"),
            P("tok"),
            P("frame", "tok"),
            P("frame", "tok"),
            P("frame", "tok"),
            P("tok", "frame"),
            P("frame", "tok"),
            P("tok", "frame"),
            P("tok", None),
            P("tok", None),
            P("tok", None),
            P("tok", None),
            P("frame", "tok"),
            P("frame", "tok"),
            P("frame"),
        ),
        out_specs=(P("frame", "tok", None), P("frame", "tok")),
        check_vma=False,
    )
```

```python
import jax
import jax.numpy as jnp
import numpy as np
from jax import lax
from jax.experimental import pallas as pl
from jax.experimental.pallas import tpu as pltpu
from jax.sharding import PartitionSpec as P

HEADS = 16
HD = 88
P_SIZE = 1024
SPAN = 4096
FRAMES = 32
D = 1408
DP = 1536
QW = 384
TOK = 128
SCALE = HD ** (-0.5)
RATE = SCALE * 1.4426950408889634
MESH = pl.DeviceIdType.MESH
F32 = jnp.float32
BF = jnp.bfloat16
WC = 768
W_ROWS, CACHE_ROWS, CACHE_COLS = 48, 64, 384
WINDOWS = ((0, 384), (256, 512), (640, 512), (1024, 384))


def dot(a, b):
    return jnp.dot(a, b, preferred_element_type=F32)


def dot_nt(a, b):
    return lax.dot_general(a, b, (((1,), (1,)), ((), ())), preferred_element_type=F32)


def iota(shape, axis):
    return lax.broadcasted_iota(jnp.int32, shape, axis)


def mod(a, n):
    return lax.rem(a + n, n)


def remote(src, dst, send, recv, device):
    return pltpu.make_async_remote_copy(
        src_ref=src, dst_ref=dst, send_sem=send, recv_sem=recv,
        device_id=device, device_id_type=MESH,
    )


class Leg:
    def __init__(self, src, dst, device, send, recv):
        self.ends = (src, dst, send, recv, device)

    def start(self):
        remote(*self.ends).start()

    def wait_recv(self):
        remote(*self.ends).wait_recv()

    def wait_send(self):
        remote(*self.ends).wait_send()


class Copies:
    def __init__(self, send, recv):
        self.send, self.recv, self.used, self.open = send, recv, 0, []

    def make(self, src, dst, device):
        n = self.used
        self.used += 1
        copy = Leg(src, dst, device, self.send.at[n], self.recv.at[n])
        self.open.append(copy)
        return copy

    def start(self, src, dst, device):
        copy = self.make(src, dst, device)
        copy.start()
        return copy

    def retire(self, keep=0):
        while len(self.open) > keep:
            self.open.pop(0).wait_send()


def norm_padded(v, valid):
    mean = jnp.sum(v, axis=1, keepdims=True) * (1.0 / D)
    center = jnp.where(valid, v - mean, 0.0)
    spread = jnp.sum(center * center, axis=1, keepdims=True) * (1.0 / D)
    return center * lax.rsqrt(spread + 1e-06)


def as_column(row):
    spread = jnp.where(iota((TOK, TOK), 0) == iota((TOK, TOK), 1), row, 0.0)
    return jnp.sum(spread, axis=1, keepdims=True)


def kernel(
    patches_hbm, offset_hbm, piece_hbm, wq_hbm, wk_hbm, wv_hbm, wo_hbm, wu_hbm, wd_hbm,
    tq_hbm, tk_hbm, tv_hbm, to_hbm, ck_hbm, cv_hbm, pos_hbm, table_hbm, turn_hbm,
    out, frame_out,
    patches, offset_in, piece_in, wq, wk, wv, wo, wu, wd, tq_w, tk_w, tv_w, to_w, ck_in, cv_in, pos_in, table, turn,
    meta, xin, meta_in, src, src_in, pad, res, WA, WU, WU2, WD, WD2, C, comp, around, H1, KV, Q,
    SB, RB, RC, mixed, H2, HID, SB2, RB2, RC2,
    result, swapped, sums, pooled, qkv_send, qkv_recv, new_send, new_all, last_send, last_recv,
    local, big_send, big_recv, swap_send, swap_recv, c_send, c_recv, side_send, side_recv, s1, r1, s2, r2, s3, r3, s4, r4,
):
    f = lax.axis_index("frame")
    t = lax.axis_index("tok")
    x, zl, c = lax.div(f, 8), lax.div(lax.rem(f, 8), 2), lax.rem(f, 2)
    y, zh = lax.div(t, 2), lax.rem(t, 2)
    z = zh * 4 + zl

    def place(r):
        return (r + 2) % 8

    loads = [
        pltpu.make_async_copy(a, b, local.at[n])
        for n, (a, b) in enumerate(
            (
                (patches_hbm, patches), (offset_hbm, offset_in), (piece_hbm, piece_in),
                (wq_hbm, wq), (wk_hbm, wk), (wv_hbm, wv), (wo_hbm, wo), (wu_hbm, wu), (wd_hbm, wd),
                (ck_hbm, ck_in), (cv_hbm, cv_in), (pos_hbm, pos_in), (table_hbm, table),
                (turn_hbm.at[f], turn), (tq_hbm, tq_w), (tk_hbm, tk_w), (tv_hbm, tv_w), (to_hbm, to_w),
            )
        )
    ]
    for load in loads:
        load.start()
    new_all[...] = jnp.zeros_like(new_all)

    def dev(x_at, z_at, y_at, c_at):
        return (x_at * 8 + lax.rem(z_at, 4) * 2 + c_at, y_at * 2 + lax.div(z_at, 4))

    xp, xm = dev(mod(x + 1, 4), z, y, c), dev(mod(x - 1, 4), z, y, c)
    yp, ym = dev(x, z, mod(y + 1, 4), c), dev(x, z, mod(y - 1, 4), c)
    zp, zm = dev(x, mod(z + 1, 8), y, c), dev(x, mod(z - 1, 8), y, c)
    sibling = dev(x, z, y, 1 - c)
    partner = dev(x, mod(z + 4, 8), y, 1 - c)
    after, before = (mod(f + 1, 32), t), (mod(f - 1, 32), t)

    own_cache = x * 4 + zl

    def all_of(ref, send, recv):
        return remote(ref, ref, send, recv, sibling)

    barrier = pltpu.get_barrier_semaphore()
    friends = (xp, xm, yp, ym, zp, zm, sibling, partner, after, before)
    for friend in friends:
        pl.semaphore_signal(barrier, inc=1, device_id=friend, device_id_type=MESH)
    pl.semaphore_wait(barrier, len(friends))

    copies = Copies(big_send, big_recv)
    moves = c != zh

    def swap(src, dst, n):
        return remote(src, dst, swap_send.at[n], swap_recv.at[n], partner)

    for load in loads[0:3]:
        load.wait()
    meta[0:1, :] = offset_in[...].astype(F32)
    meta[1:2, :] = piece_in[...].astype(F32)

    @pl.when(moves)
    def _():
        swap(patches, xin, 0).start()
        swap(meta, meta_in, 1).start()

    for load in loads[3:7]:
        load.wait()
    grow = jnp.where(iota((48, 44), 0) == iota((48, 44), 1), 1.0, 0.0).astype(BF)
    total = None
    for n, w in enumerate((wq, wk, wv, wo)):
        to = jnp.where(
            iota((176, WC), 0) + n * 176 == iota((176, WC), 1), 1.0, 0.0
        ).astype(BF)
        term = dot(dot(grow, w[...]).astype(BF), to)
        total = term if total is None else total + term
    WA[0, 0, place(0)] = total.astype(BF)

    def z_first(B):
        def at(r):
            return B.at[0, 0, place(r)]

        waits = [copies.start(at(0), at(-1), zp), copies.start(at(0), at(1), zm)]
        yield
        firsts = []

        def across(run):
            firsts.append(copies.start(B.at[0, 0, run], B.at[0, 3, run], xp))
            firsts.append(copies.start(B.at[0, 0, run], B.at[0, 1, run], xm))

        half = B.shape[4] // 2
        low, high = pl.ds(0, half), pl.ds(half, half)
        for step in range(1, 5):
            for copy in waits:
                copy.wait_recv()
            if step < 3:
                waits = [
                    copies.start(at(-step), at(-step - 1), zp),
                    copies.start(at(step), at(step + 1), zm),
                ]
            elif step == 3:
                waits = [
                    copies.start(B.at[0, 0, place(-3), :, low], B.at[0, 0, place(4), :, low], zp),
                    copies.start(B.at[0, 0, place(3), :, high], B.at[0, 0, place(4), :, high], zm),
                ]
            if step == 2:
                across(pl.ds(0, 5))
            if step == 4:
                across(pl.ds(5, 3))
            if step < 4:
                yield

        def aside(x_at):
            return copies.start(B.at[0, x_at], B.at[1, x_at], sibling)

        sides = [aside(0)]
        yield
        for copy in firsts:
            copy.wait_recv()
        one, two = pl.ds(0, 4), pl.ds(4, 4)
        waits = [
            copies.start(B.at[0, 3, one], B.at[0, 2, one], xp),
            copies.start(B.at[0, 1, two], B.at[0, 2, two], xm),
        ]
        sides += [aside(3), aside(1)]
        yield
        for copy in waits:
            copy.wait_recv()
        sides.append(aside(2))
        yield
        for copy in sides:
            copy.wait_recv()

    def x_first(B):
        here = place(0)
        waits = [
            copies.start(B.at[0, here, 0], B.at[0, here, 3], xp),
            copies.start(B.at[0, here, 0], B.at[0, here, 1], xm),
        ]
        yield
        half = B.shape[4] // 2
        low, high = pl.ds(0, half), pl.ds(half, half)
        for copy in waits:
            copy.wait_recv()
        waits = [
            copies.start(B.at[0, here, 3, :, low], B.at[0, here, 2, :, low], xp),
            copies.start(B.at[0, here, 1, :, high], B.at[0, here, 2, :, high], xm),
        ]
        yield

        def at(r):
            return B.at[0, place(r)]

        one, two = pl.ds(0, 2), pl.ds(2, 2)
        for step in range(5):
            for copy in waits:
                copy.wait_recv()
            if step < 3:
                waits = [
                    copies.start(at(-step), at(-step - 1), zp),
                    copies.start(at(step), at(step + 1), zm),
                ]
                yield
            elif step == 3:
                waits = [
                    copies.start(B.at[0, place(-3), one], B.at[0, place(4), one], zp),
                    copies.start(B.at[0, place(3), two], B.at[0, place(4), two], zm),
                ]
                yield
        side = copies.start(B.at[0], B.at[1], sibling)
        yield
        side.wait_recv()

    def drain(task):
        for _ in task:
            pass

    def ahead(task, count):
        for _ in range(count):
            if next(task, "end") == "end":
                return

    def both(*tasks):
        tasks = list(tasks)
        while tasks:
            for task in list(tasks):
                if next(task, "end") == "end":
                    tasks.remove(task)
            if tasks:
                yield

    load1 = z_first(WA)
    load2 = both(z_first(WU), x_first(WU2))
    load3 = both(z_first(WD), x_first(WD2))
    ahead(load1, 1)

    for q, (start, size) in enumerate(WINDOWS):
        r, k = iota((size, QW), 0) + start, iota((size, QW), 1)
        at = lax.rem(k, 48)
        hit = (r == 352 * q + lax.div(k, 48) * 44 + at) & (at < 44)
        pad[q, 0:size, :] = jnp.where(hit, 1.0, 0.0).astype(BF)
    valid = lax.rem(iota((1, DP), 1), 48) < 44

    def padded(rows):
        for q, (start, size) in enumerate(WINDOWS):
            res[:, q * QW : (q + 1) * QW] = dot(
                rows[:, start : start + size], pad[q, 0:size, :]
            ).astype(BF)
        normed = norm_padded(res[...].astype(F32), valid)
        return [normed[:, q * QW : (q + 1) * QW] for q in range(4)]

    quarters = padded(patches)
    offset, piece = as_column(meta[0:1, :]), as_column(meta[1:2, :])
    mine = quarters[0]
    for q in range(1, 4):
        mine = jnp.where(piece == float(q), quarters[q], mine)
    comp[...] = mine.astype(BF)
    for q in range(4):
        H1[0, :, q * QW : (q + 1) * QW] = quarters[q].astype(BF)
    hops = [
        copies.start(comp, around.at[0], after),
        copies.start(comp, around.at[1], before),
    ]
    for load in loads[7:9]:
        load.wait()
    for w, one, two in ((wu, WU, WU2), (wd, WD, WD2)):
        rows = dot(grow, w[...]).astype(BF)
        one[0, 0, place(0)] = rows[:, 0:512]
        two[0, place(0), 0] = rows[:, 512:768]
    ahead(load1, 1)
    for copy in hops:
        copy.wait_recv()
    earlier = jnp.where(f > 0, around[0].astype(F32), 0.0)
    later = jnp.where(f < FRAMES - 1, around[1].astype(F32), 0.0)
    source = jnp.where(
        offset == -1.0, earlier, jnp.where(offset == 1.0, later, comp[...].astype(F32))
    )
    src[...] = source.astype(BF)

    def gather(H):
        a, b = pl.ds(0, 64), pl.ds(64, 64)
        one = copies.make(H.at[0, a], H.at[3, a], yp)
        two = copies.make(H.at[0, b], H.at[1, b], ym)
        rest = [
            copies.make(H.at[0, b], H.at[3, b], yp), copies.make(H.at[0, a], H.at[1, a], ym)
        ]
        far = [
            copies.make(H.at[3, a], H.at[2, a], yp), copies.make(H.at[1, b], H.at[2, b], ym)
        ]

        def begin():
            for copy in (one, two, *rest):
                copy.start()

        def forward():
            one.wait_recv()
            far[0].start()
            two.wait_recv()
            far[1].start()

        def near():
            for copy in rest:
                copy.wait_recv()

        def last():
            for copy in far:
                copy.wait_recv()

        return begin, forward, near, last

    begin1, forward1, near1, last1 = gather(H1)
    stays = jnp.logical_not(moves)

    @pl.when(moves)
    def _():
        swap(src, src_in, 2).start()

    @pl.when(stays)
    def _():
        for q in range(4):
            columns = slice(q * QW, (q + 1) * QW)
            H1[0, :, columns] = jnp.where(
                piece == float(q), src[...].astype(F32), H1[0, :, columns].astype(F32)
            ).astype(BF)
        begin1()

    ahead(load1, 1)

    def turned(v):
        return jnp.concatenate([v[:, 44:88], v[:, 0:44], v[:, 132:176], v[:, 88:132]], axis=1)

    for load in loads[9:13]:
        load.wait()
    spot = jnp.where(
        iota((CACHE_ROWS, 62), 0) == iota((CACHE_ROWS, 62), 1), pos_in[...].astype(F32), 0.0
    )
    spot = jnp.sum(spot, axis=1, keepdims=True)
    high = jnp.floor(spot * (1.0 / 64))
    lanes = iota((CACHE_ROWS, 64), 1).astype(F32)

    def chosen(at, n):
        hit = jnp.where(lanes == at, 1.0, 0.0)
        both = jnp.dot(hit, table[n], preferred_element_type=F32, precision=lax.Precision.HIGHEST)
        return both[0:62, 0:176], both[0:62, 176:352]

    (cos_a, sin_a), (cos_b, sin_b) = chosen(high, 0), chosen(spot - 64.0 * high, 1)
    cosine, sine = cos_a * cos_b - sin_a * sin_b, sin_a * cos_b + cos_a * sin_b
    sine = jnp.where(lax.rem(iota((62, 176), 1), HD) < HD // 2, -sine, sine)
    raw = ck_in[...].astype(F32)
    cache_row = jnp.concatenate(
        [raw * cosine + turned(raw) * sine, cv_in[...].astype(F32), jnp.zeros((62, 32), F32)], axis=1
    )
    C[0, own_cache] = jnp.zeros((CACHE_ROWS, CACHE_COLS), BF)
    C[0, own_cache, 0:62, :] = cache_row.astype(BF)
    ahead(load1, 2)

    pl.when(stays)(forward1)

    @pl.when(moves)
    def _():
        swap(patches, xin, 0).wait()
        swap(meta, meta_in, 1).wait()
        swap(src, src_in, 2).wait()
        quarters = padded(xin)
        piece = as_column(meta_in[1:2, :])
        for q in range(4):
            H1[0, :, q * QW : (q + 1) * QW] = jnp.where(
                piece == float(q), src_in[...].astype(F32), quarters[q]
            ).astype(BF)
        begin1()

    ahead(load2, 2)
    pl.when(moves)(forward1)
    ahead(load1, 1)
    ahead(load2, 1)
    near1()
    ahead(load2, 1)
    last1()
    ahead(load1, 1)
    drain(load1)
    ahead(load2, 1)

    plane_of = [c, 1 - c]
    x_of = [mod(k - x, 4) for k in range(4)]
    z_of = [lax.rem(k - z + 8 + 2, 8) for k in range(8)]

    def weight(B, at, start, size):
        pieces = []
        for k in range(32):
            p, x_at, z_at = plane_of[k % 2], x_of[k // 8], z_of[at * 4 + k // 2 % 4]
            spot = (p, x_at, z_at) if B.shape[1] == 4 else (p, z_at, x_at)
            pieces.append(B[(*spot, slice(None), slice(start, start + size))])
        return jnp.concatenate(pieces, axis=0)

    def wider(rows, first, columns, start):
        r, k = iota((rows, columns), 0) + first, iota((rows, columns), 1) + start
        at = lax.rem(k, 128)
        return jnp.where((r == lax.div(k, 128) * HD + at) & (at < HD), 1.0, 0.0).astype(BF)

    wide_q, wide_kv = wider(256, 0, 256, 0), wider(512, 128, 512, 256)
    r, k = iota((256, 256), 1) + 512, iota((256, 256), 0)
    at = lax.rem(k, 128)
    narrow = jnp.where(
        (r == 528 + lax.div(k, 128) * HD + at) & (at < HD), 1.0, 0.0
    ).astype(BF)

    rows = H1[...].reshape(4 * TOK, DP)
    sides = []
    for at in range(2):
        joined = dot(rows, weight(WA, at, 128, 512)).astype(BF)
        KV[0, at] = dot(joined, wide_kv).astype(BF)
        sides.append(copies.start(KV.at[0, at], KV.at[1, at], sibling))
    ahead(load3, 1)
    for at in range(2):
        joined = dot(rows, weight(WA, at, 0, 256)).astype(BF)
        Q[at] = dot(joined, wide_q).astype(BF).reshape(4, TOK, 256)
    ahead(load3, 1)
    for copy in sides:
        copy.wait_recv()

    def attend(block):
        total = None
        for at in range(2):
            heads = []
            for h in range(2):
                span = slice(h * 128, h * 128 + 128)
                vspan = slice(256 + h * 128, 256 + h * 128 + 128)
                q = Q[at, block, :, span]
                s = [dot_nt(q, KV[k, at, :, span]) for k in range(2)]
                top = jnp.maximum(
                    jnp.max(s[0], axis=1, keepdims=True), jnp.max(s[1], axis=1, keepdims=True)
                )
                p = [jnp.exp2(part * RATE - top * RATE) for part in s]
                mass = jnp.sum(p[0], axis=1, keepdims=True) + jnp.sum(p[1], axis=1, keepdims=True)
                o = dot(p[0].astype(BF), KV[0, at, :, vspan]) + dot(
                    p[1].astype(BF), KV[1, at, :, vspan]
                )
                heads.append((o / mass).astype(BF))
            both_heads = dot(jnp.concatenate(heads, axis=1), narrow).astype(BF)
            term = dot_nt(both_heads, weight(WA, at, 512, 256))
            total = term if total is None else total + term
        return total

    def scatter(partial, S, B, R, far_first, between):
        a, b = pl.ds(0, 64), pl.ds(64, 64)

        def send_far():
            S[0] = partial(2).astype(BF)
            return [
                copies.start(S.at[0, a], B.at[0], yp), copies.start(S.at[0, b], B.at[1], ym)
            ]

        def send_near():
            S[1] = partial(1).astype(BF)
            one = copies.start(S.at[1, b], R.at[0, b], yp)
            S[2] = partial(3).astype(BF)
            return [one, copies.start(S.at[2, a], R.at[1, a], ym)]

        if far_first:
            far = send_far()
            between(0)
            near = send_near()
            between(1)
        else:
            near = send_near()
            far = send_far()
            between(0)
        far[0].wait_recv()
        S[1, 0:64, :] = (S[1, 0:64, :].astype(F32) + B[0].astype(F32)).astype(BF)
        near.append(copies.start(S.at[1, a], R.at[0, a], yp))
        far[1].wait_recv()
        S[2, 64:128, :] = (S[2, 64:128, :].astype(F32) + B[1].astype(F32)).astype(BF)
        near.append(copies.start(S.at[2, b], R.at[1, b], ym))
        own = partial(0)
        between(2)
        for copy in near:
            copy.wait_recv()
        return own + R[0].astype(F32) + R[1].astype(F32)

    def beside_attention(n):
        if n == 0:
            ahead(load2, 1)
            ahead(load3, 1)
        elif n == 1:
            ahead(load3, 1)
            ahead(load2, 1)
        else:
            ahead(load3, 1)
            drain(load2)

    total = scatter(attend, SB, RB, RC, True, beside_attention)
    mixed[...] = (res[...].astype(F32) + total).astype(BF)
    H2[0] = norm_padded(mixed[...].astype(F32), valid).astype(BF)
    begin2, forward2, near2, last2 = gather(H2)
    begin2()

    @pl.loop(1, 16)
    def _(k):
        to = lax.rem(own_cache + k, 16)
        spot = C.at[0, own_cache]
        device = dev(lax.div(to, 4), zh * 4 + lax.rem(to, 4), y, c)
        remote(spot, spot, c_send, c_recv, device).start()

    ahead(load3, 1)

    def up(block, at):
        rows = H2[block]
        return [
            jax.nn.gelu(dot(rows, weight(WU, at, 0, 512))).astype(BF),
            jax.nn.gelu(dot(rows, weight(WU2, at, 0, 256))).astype(BF),
        ]

    def down(hidden, at):
        return dot_nt(hidden[0], weight(WD, at, 0, 512)) + dot_nt(
            hidden[1], weight(WD2, at, 0, 256)
        )

    def up_down(block):
        return down(up(block, 0), 0) + down(up(block, 1), 1)

    for at in range(2):
        first, second = up(0, at)
        HID[at, :, 0:512] = first
        HID[at, :, 512:768] = second
    forward2()
    copies.retire(24)
    near2()
    ahead(load3, 1)
    drain(load3)

    def near_rows(block):
        return up_down(block)

    def far_rows(block):
        last2()
        return up_down(block)

    def own_rows(block):
        own = [(HID[at, :, 0:512], HID[at, :, 512:768]) for at in range(2)]
        return down(own[0], 0) + down(own[1], 1)

    def beside_mlp(n):
        if n == 2:
            copies.retire(8)
            all_of(C.at[0, pl.ds(0, 15)], c_send, c_recv).wait_recv()
            remote(C.at[0], C.at[1], side_send, side_recv, sibling).start()

    calls = [near_rows, near_rows, far_rows, own_rows]
    total = scatter(lambda block: calls.pop(0)(block), SB2, RB2, RC2, False, beside_mlp)
    last = (mixed[...].astype(F32) + total).astype(BF)
    columns = [
        dot_nt(last[:, q * QW : (q + 1) * QW], pad[q, 0:size, :])
        for q, (_, size) in enumerate(WINDOWS)
    ]
    parts = [
        columns[0][:, 0:256],
        columns[0][:, 256:384] + columns[1][:, 0:128],
        columns[1][:, 128:384],
        columns[1][:, 384:512] + columns[2][:, 0:128],
        columns[2][:, 128:384],
        columns[2][:, 384:512] + columns[3][:, 0:128],
        columns[3][:, 128:384],
    ]
    plain = jnp.concatenate(parts, axis=1)
    sums[...] = jnp.sum(plain, axis=0, keepdims=True)

    other = f + 1 - 2 * c
    home = f - c + zh
    slot = 2 * y + c

    def share(k):
        return remote(sums, pooled.at[slot], s1, r1, (home, lax.rem(t + k, 8)))

    @pl.when(moves)
    def _():
        share(0).start()

    @pl.when(jnp.logical_not(moves))
    def _():
        pooled[slot] = sums[...]

    for k in range(1, 8):
        share(k).start()

    result[...] = plain.astype(BF)

    @pl.when(moves)
    def _():
        swap(result, swapped, 3).start()

    remote(C.at[0], C.at[1], side_send, side_recv, sibling).wait_recv()
    for load in loads[13:]:
        load.wait()

    @pl.when(moves)
    def _():
        all_of(pooled, s1, r1).wait_recv()

    @pl.when(jnp.logical_not(moves))
    def _():
        all_of(pooled.at[pl.ds(0, 7)], s1, r1).wait_recv()

    mean_frame = pooled[0]
    for k in range(1, 8):
        mean_frame = mean_frame + pooled[k]
    mean_frame = mean_frame * (1.0 / P_SIZE)
    center = mean_frame - jnp.sum(mean_frame, axis=1, keepdims=True) * (1.0 / D)
    spread = jnp.sum(center * center, axis=1, keepdims=True) * (1.0 / D)
    normed = center * lax.rsqrt(spread + 1e-06)

    def pick(v):
        got = v[:, 0:176]
        for k in range(1, 8):
            got = jnp.where(t == k, v[:, k * 176 : k * 176 + 176], got)
        return got

    features = jnp.broadcast_to(pick(normed), (8, 176)).astype(BF)
    for n, w in enumerate((tq_w, tk_w, tv_w)):
        part = dot(features, w[...])
        for k in range(8):
            qkv_send[k, n, :, 0:176] = part[0:1, k * 176 : k * 176 + 176]

    def send_heads(k):
        to = lax.rem(t + k, 8)
        return remote(qkv_send.at[to], qkv_recv.at[t], s2, r2, (f, to))

    for k in range(1, 8):
        send_heads(k).start()
    qkv_recv[t] = qkv_send[t]
    all_of(qkv_recv.at[pl.ds(0, 7)], s2, r2).wait_recv()

    whole = []
    for n in range(3):
        v = qkv_recv[0, n, :, 0:176]
        for k in range(1, 8):
            v = v + qkv_recv[k, n, :, 0:176]
        whole.append(v)

    def rot(v):
        return (v * turn[0:1, :] + turned(v) * turn[1:2, :]).astype(BF).astype(F32)

    new_send[...] = jnp.zeros_like(new_send)
    new_send[:, 0:176] = rot(whole[1])
    new_send[:, 176:352] = whole[2].astype(BF).astype(F32)


    @pl.loop(1, 32)
    def _(k):
        remote(new_send, new_all.at[f], s3, r3, (lax.rem(f + k, 32), t)).start()

    new_all[f] = new_send[...]
    query = rot(whole[0])
    lane = iota((1, 176), 1)
    wide_query = jnp.concatenate(
        [jnp.where(lane < HD, query, 0.0), jnp.where(lane >= HD, query, 0.0), jnp.zeros((6, 176), F32)],
        axis=0,
    )
    queries = jnp.concatenate([wide_query, jnp.zeros((8, 80), F32)], axis=1).astype(BF)
    count = 32 * CACHE_ROWS
    old_keys = C[:, :, :, 0:256].reshape(count, 256)
    s_old = dot_nt(queries, old_keys)
    s_old = jnp.where(lax.rem(iota((8, count), 1), CACHE_ROWS) < 62, s_old, -1e30)

    all_of(new_all.at[pl.ds(0, 31)], s3, r3).wait_recv()
    known = new_all[:, 0, :]
    s_new = dot_nt(queries, known[:, 0:256].astype(BF))
    s_new = jnp.where(iota((8, 32), 1) <= f, s_new, -1e30)
    top = jnp.maximum(
        jnp.max(s_old, axis=1, keepdims=True), jnp.max(s_new, axis=1, keepdims=True)
    )
    p_old = jnp.exp2(s_old * RATE - top * RATE)
    p_new = jnp.exp2(s_new * RATE - top * RATE)
    p_old = jnp.where(lax.rem(iota((8, count), 1), CACHE_ROWS) < 62, p_old, 0.0)
    p_new = jnp.where(iota((8, 32), 1) <= f, p_new, 0.0)
    mass = jnp.sum(p_old, axis=1, keepdims=True) + jnp.sum(p_new, axis=1, keepdims=True)
    old_values = C[:, :, :, 128:384].reshape(count, 256)
    o = dot(p_old.astype(BF), old_values) + dot(p_new.astype(BF), known[:, 128:384].astype(BF))
    o = o / mass
    temporal = jnp.where(lane < HD, o[0:1, 48:224], o[1:2, 48:224])
    part = dot(jnp.broadcast_to(temporal, (8, 176)).astype(BF), to_w[...])
    for k in range(8):
        last_send[k, :, 0:176] = part[0:1, k * 176 : k * 176 + 176]

    def send_last(k):
        to = lax.rem(t + k, 8)
        return remote(last_send.at[to], last_recv.at[t], s4, r4, (f, to))

    for k in range(1, 8):
        send_last(k).start()
    last_recv[t] = last_send[t]

    stored, kept = (pltpu.make_async_copy(a, out, local.at[0]) for a in (swapped, result))

    @pl.when(moves)
    def _():
        swap(result, swapped, 3).wait()
        stored.start()

    @pl.when(jnp.logical_not(moves))
    def _():
        kept.start()

    copies.retire()
    all_of(C.at[0, pl.ds(0, 15)], c_send, c_recv).wait_send()
    remote(C.at[0], C.at[1], side_send, side_recv, sibling).wait_send()

    @pl.when(moves)
    def _():
        all_of(pooled, s1, r1).wait_send()

    @pl.when(jnp.logical_not(moves))
    def _():
        all_of(pooled.at[pl.ds(0, 7)], s1, r1).wait_send()

    all_of(qkv_recv.at[pl.ds(0, 7)], s2, r2).wait_send()
    all_of(new_all.at[pl.ds(0, 31)], s3, r3).wait_send()
    all_of(last_recv.at[pl.ds(0, 7)], s4, r4).wait_recv()
    total = pick(mean_frame)
    for k in range(8):
        total = total + last_recv[k, :, 0:176]
    frame_out[...] = total.astype(BF)
    all_of(last_recv.at[pl.ds(0, 7)], s4, r4).wait_send()

    @pl.when(moves)
    def _():
        stored.wait()

    @pl.when(jnp.logical_not(moves))
    def _():
        kept.wait()


BIG = 160


def call(*operands):
    turn = operands[-1]
    vmem = pl.BlockSpec(memory_space=pltpu.VMEM)
    dma = pltpu.SemaphoreType.DMA
    held = [pltpu.VMEM(a.shape, a.dtype) for a in operands[:-1]] + [
        pltpu.VMEM(turn.shape[1:], F32)
    ]
    return pl.pallas_call(
        kernel,
        out_shape=(
            jax.ShapeDtypeStruct((TOK, D), BF),
            jax.ShapeDtypeStruct((1, 176), BF),
        ),
        in_specs=[pl.BlockSpec(memory_space=pl.ANY)] * len(operands),
        out_specs=(pl.BlockSpec(memory_space=pl.ANY), vmem),
        scratch_shapes=held
        + [
            pltpu.VMEM((2, TOK), F32),
            pltpu.VMEM((TOK, D), BF),
            pltpu.VMEM((2, TOK), F32),
            pltpu.VMEM((TOK, QW), BF),
            pltpu.VMEM((TOK, QW), BF),
            pltpu.VMEM((4, 512, QW), BF),
            pltpu.VMEM((TOK, DP), BF),
            pltpu.VMEM((2, 4, 8, W_ROWS, WC), BF),
            pltpu.VMEM((2, 4, 8, W_ROWS, 512), BF),
            pltpu.VMEM((2, 8, 4, W_ROWS, 256), BF),
            pltpu.VMEM((2, 4, 8, W_ROWS, 512), BF),
            pltpu.VMEM((2, 8, 4, W_ROWS, 256), BF),
            pltpu.VMEM((2, 16, CACHE_ROWS, CACHE_COLS), BF),
            pltpu.VMEM((TOK, QW), BF),
            pltpu.VMEM((2, TOK, QW), BF),
            pltpu.VMEM((4, TOK, DP), BF),
            pltpu.VMEM((2, 2, 4 * TOK, 512), BF),
            pltpu.VMEM((2, 4, TOK, 256), BF),
            pltpu.VMEM((3, TOK, DP), BF),
            pltpu.VMEM((2, 64, DP), BF),
            pltpu.VMEM((2, TOK, DP), BF),
            pltpu.VMEM((TOK, DP), BF),
            pltpu.VMEM((4, TOK, DP), BF),
            pltpu.VMEM((2, TOK, 768), BF),
            pltpu.VMEM((3, TOK, DP), BF),
            pltpu.VMEM((2, 64, DP), BF),
            pltpu.VMEM((2, TOK, DP), BF),
            pltpu.VMEM((TOK, D), BF),
            pltpu.VMEM((TOK, D), BF),
            pltpu.VMEM((1, D), F32),
            pltpu.VMEM((8, 1, D), F32),
            pltpu.VMEM((8, 3, 1, 256), F32),
            pltpu.VMEM((8, 3, 1, 256), F32),
            pltpu.VMEM((1, CACHE_COLS), F32),
            pltpu.VMEM((32, 1, CACHE_COLS), F32),
            pltpu.VMEM((8, 1, 256), F32),
            pltpu.VMEM((8, 1, 256), F32),
            dma((len(operands),)),
            dma((BIG,)), dma((BIG,)),
            dma((4,)), dma((4,)),
            dma, dma, dma, dma,
            dma, dma, dma, dma, dma, dma, dma, dma,
        ],
        compiler_params=pltpu.CompilerParams(
            collective_id=0, has_side_effects=True, vmem_limit_bytes=56 * 1024 * 1024
        ),
        cost_estimate=pl.CostEstimate(
            flops=8_000_000_000, bytes_accessed=20_000_000, transcendentals=3_000_000
        ),
    )(*operands)


def body(
    patches, shift_offset, shift_slice, w_query, w_key, w_value, w_out, w_up, w_down,
    t_query, t_key, t_value, t_out, cache_keys, cache_values, cache_pos,
):
    half = HD // 2
    freq = np.float32(10000.0) ** (-np.arange(half, dtype=np.float32) / np.float32(half))
    angle = (SPAN + np.arange(FRAMES)).astype(np.float32)[:, None] * freq[None, :]
    cosine, sine = np.cos(angle), np.sin(angle)
    turn = np.stack(
        [
            np.concatenate([cosine] * 4, axis=1),
            np.concatenate([-sine, sine, -sine, sine], axis=1),
        ],
        axis=1,
    ).astype(np.float32)
    steps = np.arange(64)[:, None] * (10000.0 ** (-np.arange(half) / half))[None, :]
    table = np.stack(
        [
            np.concatenate([np.cos(64 * steps)] * 4 + [np.sin(64 * steps)] * 4, axis=1),
            np.concatenate([np.cos(steps)] * 4 + [np.sin(steps)] * 4, axis=1),
        ]
    ).astype(np.float32)
    patch_out, frame_out = call(
        patches[0], shift_offset[None], shift_slice[None], w_query, w_key, w_value,
        w_out.T, w_up, w_down.T, t_query, t_key, t_value, t_out, cache_keys, cache_values, cache_pos[None],
        jnp.asarray(table), jnp.asarray(turn),
    )
    return (patch_out[None], frame_out)


def solution(mesh):
    return jax.shard_map(
        body,
        mesh=mesh,
        in_specs=(
            P("frame", "tok", None),
            P("tok"),
            P("tok"),
            P("frame", "tok"),
            P("frame", "tok"),
            P("frame", "tok"),
            P("tok", "frame"),
            P("frame", "tok"),
            P("tok", "frame"),
            P("tok", None),
            P("tok", None),
            P("tok", None),
            P("tok", None),
            P("frame", "tok"),
            P("frame", "tok"),
            P("frame"),
        ),
        out_specs=(P("frame", "tok", None), P("frame", "tok")),
        check_vma=False,
    )
```

```python
import jax
import jax.numpy as jnp
import numpy as np
from jax import lax
from jax.experimental import pallas as pl
from jax.experimental.pallas import tpu as pltpu
from jax.sharding import PartitionSpec as P

HEADS = 16
HD = 88
P_SIZE = 1024
SPAN = 4096
FRAMES = 32
D = 1408
DP = 1536
QW = 384
TOK = 128
SCALE = HD ** (-0.5)
RATE = SCALE * 1.4426950408889634
MESH = pl.DeviceIdType.MESH
F32 = jnp.float32
BF = jnp.bfloat16
WC = 768
W_ROWS, CACHE_ROWS, CACHE_COLS = 48, 64, 384
WINDOWS = ((0, 384), (256, 512), (640, 512), (1024, 384))


def dot(a, b):
    return jnp.dot(a, b, preferred_element_type=F32)


def dot_nt(a, b):
    return lax.dot_general(a, b, (((1,), (1,)), ((), ())), preferred_element_type=F32)


def iota(shape, axis):
    return lax.broadcasted_iota(jnp.int32, shape, axis)


def mod(a, n):
    return lax.rem(a + n, n)


def remote(src, dst, send, recv, device):
    return pltpu.make_async_remote_copy(
        src_ref=src, dst_ref=dst, send_sem=send, recv_sem=recv,
        device_id=device, device_id_type=MESH,
    )


class Leg:
    def __init__(self, src, dst, device, send, recv):
        self.ends = (src, dst, send, recv, device)

    def start(self):
        remote(*self.ends).start()

    def wait_recv(self):
        remote(*self.ends).wait_recv()

    def wait_send(self):
        remote(*self.ends).wait_send()


class Copies:
    def __init__(self, send, recv):
        self.send, self.recv, self.used, self.open = send, recv, 0, []

    def make(self, src, dst, device):
        n = self.used
        self.used += 1
        copy = Leg(src, dst, device, self.send.at[n], self.recv.at[n])
        self.open.append(copy)
        return copy

    def start(self, src, dst, device):
        copy = self.make(src, dst, device)
        copy.start()
        return copy

    def retire(self, keep=0):
        while len(self.open) > keep:
            self.open.pop(0).wait_send()


def norm_padded(v, valid):
    mean = jnp.sum(v, axis=1, keepdims=True) * (1.0 / D)
    center = jnp.where(valid, v - mean, 0.0)
    spread = jnp.sum(center * center, axis=1, keepdims=True) * (1.0 / D)
    return center * lax.rsqrt(spread + 1e-06)


def as_column(row):
    spread = jnp.where(iota((TOK, TOK), 0) == iota((TOK, TOK), 1), row, 0.0)
    return jnp.sum(spread, axis=1, keepdims=True)


def kernel(
    patches_hbm, offset_hbm, piece_hbm, wq_hbm, wk_hbm, wv_hbm, wo_hbm, wu_hbm, wd_hbm,
    tq_hbm, tk_hbm, tv_hbm, to_hbm, ck_hbm, cv_hbm, pos_hbm, table_hbm,
    pad_hbm, grow_hbm, spread_hbm, wide_kv_hbm, wide_q_hbm, narrow_hbm, valid_hbm, turn_hbm,
    out, frame_out,
    patches, offset_in, piece_in, wq, wk, wv, wo, wu, wd, tq_w, tk_w, tv_w, to_w, ck_in, cv_in, pos_in, table,
    pad, grow_in, spread, wide_kv_in, wide_q_in, narrow_in, valid_in, turn,
    meta, xin, meta_in, src, src_in, res, WA, WU, WU2, WD, WD2, C, comp, around, H1, KV, Q,
    SB, RB, RC, mixed, H2, HID, SB2, RB2, RC2,
    result, swapped, sums, pooled, qkv_send, qkv_recv, new_send, new_all, last_send, last_recv,
    local, big_send, big_recv, swap_send, swap_recv, c_send, c_recv, side_send, side_recv, s1, r1, s2, r2, s3, r3, s4, r4,
):
    f = lax.axis_index("frame")
    t = lax.axis_index("tok")
    x, zl, c = lax.div(f, 8), lax.div(lax.rem(f, 8), 2), lax.rem(f, 2)
    y, zh = lax.div(t, 2), lax.rem(t, 2)
    z = zh * 4 + zl

    def place(r):
        return (r + 2) % 8

    loads = [
        pltpu.make_async_copy(a, b, local.at[n])
        for n, (a, b) in enumerate(
            (
                (patches_hbm, patches), (offset_hbm, offset_in), (piece_hbm, piece_in),
                (wq_hbm, wq), (wk_hbm, wk), (wv_hbm, wv), (wo_hbm, wo), (wu_hbm, wu), (wd_hbm, wd),
                (ck_hbm, ck_in), (cv_hbm, cv_in), (pos_hbm, pos_in), (table_hbm, table),
                (grow_hbm, grow_in), (spread_hbm, spread), (pad_hbm, pad), (valid_hbm, valid_in),
                (wide_kv_hbm, wide_kv_in), (wide_q_hbm, wide_q_in), (narrow_hbm, narrow_in),
                (turn_hbm.at[f], turn), (tq_hbm, tq_w), (tk_hbm, tk_w), (tv_hbm, tv_w), (to_hbm, to_w),
            )
        )
    ]
    for load in loads:
        load.start()
    new_all[...] = jnp.zeros_like(new_all)

    def dev(x_at, z_at, y_at, c_at):
        return (x_at * 8 + lax.rem(z_at, 4) * 2 + c_at, y_at * 2 + lax.div(z_at, 4))

    xp, xm = dev(mod(x + 1, 4), z, y, c), dev(mod(x - 1, 4), z, y, c)
    yp, ym = dev(x, z, mod(y + 1, 4), c), dev(x, z, mod(y - 1, 4), c)
    zp, zm = dev(x, mod(z + 1, 8), y, c), dev(x, mod(z - 1, 8), y, c)
    sibling = dev(x, z, y, 1 - c)
    partner = dev(x, mod(z + 4, 8), y, 1 - c)
    after, before = (mod(f + 1, 32), t), (mod(f - 1, 32), t)

    own_cache = x * 4 + zl

    def all_of(ref, send, recv):
        return remote(ref, ref, send, recv, sibling)

    barrier = pltpu.get_barrier_semaphore()
    friends = (xp, xm, yp, ym, zp, zm, sibling, partner, after, before)
    for friend in friends:
        pl.semaphore_signal(barrier, inc=1, device_id=friend, device_id_type=MESH)
    pl.semaphore_wait(barrier, len(friends))

    copies = Copies(big_send, big_recv)
    moves = c != zh

    def swap(src, dst, n):
        return remote(src, dst, swap_send.at[n], swap_recv.at[n], partner)

    for load in loads[0:3]:
        load.wait()
    meta[0:1, :] = offset_in[...].astype(F32)
    meta[1:2, :] = piece_in[...].astype(F32)

    @pl.when(moves)
    def _():
        swap(patches, xin, 0).start()
        swap(meta, meta_in, 1).start()

    for load in loads[3:7] + loads[13:15]:
        load.wait()
    grow = grow_in[...]
    total = None
    for n, w in enumerate((wq, wk, wv, wo)):
        term = dot(dot(grow, w[...]).astype(BF), spread[n])
        total = term if total is None else total + term
    WA[0, 0, place(0)] = total.astype(BF)

    def z_first(B):
        def at(r):
            return B.at[0, 0, place(r)]

        waits = [copies.start(at(0), at(-1), zp), copies.start(at(0), at(1), zm)]
        yield
        firsts = []

        def across(run):
            firsts.append(copies.start(B.at[0, 0, run], B.at[0, 3, run], xp))
            firsts.append(copies.start(B.at[0, 0, run], B.at[0, 1, run], xm))

        half = B.shape[4] // 2
        low, high = pl.ds(0, half), pl.ds(half, half)
        for step in range(1, 5):
            for copy in waits:
                copy.wait_recv()
            if step < 3:
                waits = [
                    copies.start(at(-step), at(-step - 1), zp),
                    copies.start(at(step), at(step + 1), zm),
                ]
            elif step == 3:
                waits = [
                    copies.start(B.at[0, 0, place(-3), :, low], B.at[0, 0, place(4), :, low], zp),
                    copies.start(B.at[0, 0, place(3), :, high], B.at[0, 0, place(4), :, high], zm),
                ]
            if step == 2:
                across(pl.ds(0, 5))
            if step == 4:
                across(pl.ds(5, 3))
            if step < 4:
                yield

        def aside(x_at):
            return copies.start(B.at[0, x_at], B.at[1, x_at], sibling)

        sides = [aside(0)]
        yield
        for copy in firsts:
            copy.wait_recv()
        one, two = pl.ds(0, 4), pl.ds(4, 4)
        waits = [
            copies.start(B.at[0, 3, one], B.at[0, 2, one], xp),
            copies.start(B.at[0, 1, two], B.at[0, 2, two], xm),
        ]
        sides += [aside(3), aside(1)]
        yield
        for copy in waits:
            copy.wait_recv()
        sides.append(aside(2))
        yield
        for copy in sides:
            copy.wait_recv()

    def x_first(B):
        here = place(0)
        waits = [
            copies.start(B.at[0, here, 0], B.at[0, here, 3], xp),
            copies.start(B.at[0, here, 0], B.at[0, here, 1], xm),
        ]
        yield
        half = B.shape[4] // 2
        low, high = pl.ds(0, half), pl.ds(half, half)
        for copy in waits:
            copy.wait_recv()
        waits = [
            copies.start(B.at[0, here, 3, :, low], B.at[0, here, 2, :, low], xp),
            copies.start(B.at[0, here, 1, :, high], B.at[0, here, 2, :, high], xm),
        ]
        yield

        def at(r):
            return B.at[0, place(r)]

        one, two = pl.ds(0, 2), pl.ds(2, 2)
        for step in range(5):
            for copy in waits:
                copy.wait_recv()
            if step < 3:
                waits = [
                    copies.start(at(-step), at(-step - 1), zp),
                    copies.start(at(step), at(step + 1), zm),
                ]
                yield
            elif step == 3:
                waits = [
                    copies.start(B.at[0, place(-3), one], B.at[0, place(4), one], zp),
                    copies.start(B.at[0, place(3), two], B.at[0, place(4), two], zm),
                ]
                yield
        side = copies.start(B.at[0], B.at[1], sibling)
        yield
        side.wait_recv()

    def drain(task):
        for _ in task:
            pass

    def ahead(task, count):
        for _ in range(count):
            if next(task, "end") == "end":
                return

    def both(*tasks):
        tasks = list(tasks)
        while tasks:
            for task in list(tasks):
                if next(task, "end") == "end":
                    tasks.remove(task)
            if tasks:
                yield

    load1 = z_first(WA)
    load2 = both(z_first(WU), x_first(WU2))
    load3 = both(z_first(WD), x_first(WD2))
    ahead(load1, 1)

    for load in loads[15:17]:
        load.wait()
    valid = valid_in[...] > 0.5

    def padded(rows):
        for q, (start, size) in enumerate(WINDOWS):
            res[:, q * QW : (q + 1) * QW] = dot(
                rows[:, start : start + size], pad[q, 0:size, :]
            ).astype(BF)
        normed = norm_padded(res[...].astype(F32), valid)
        return [normed[:, q * QW : (q + 1) * QW] for q in range(4)]

    quarters = padded(patches)
    offset, piece = as_column(meta[0:1, :]), as_column(meta[1:2, :])
    mine = quarters[0]
    for q in range(1, 4):
        mine = jnp.where(piece == float(q), quarters[q], mine)
    comp[...] = mine.astype(BF)
    for q in range(4):
        H1[0, :, q * QW : (q + 1) * QW] = quarters[q].astype(BF)
    hops = [
        copies.start(comp, around.at[0], after),
        copies.start(comp, around.at[1], before),
    ]
    for load in loads[7:9]:
        load.wait()
    for w, one, two in ((wu, WU, WU2), (wd, WD, WD2)):
        rows = dot(grow, w[...]).astype(BF)
        one[0, 0, place(0)] = rows[:, 0:512]
        two[0, place(0), 0] = rows[:, 512:768]
    ahead(load1, 1)
    for copy in hops:
        copy.wait_recv()
    earlier = jnp.where(f > 0, around[0].astype(F32), 0.0)
    later = jnp.where(f < FRAMES - 1, around[1].astype(F32), 0.0)
    source = jnp.where(
        offset == -1.0, earlier, jnp.where(offset == 1.0, later, comp[...].astype(F32))
    )
    src[...] = source.astype(BF)

    def gather(H):
        a, b = pl.ds(0, 64), pl.ds(64, 64)
        one = copies.make(H.at[0, a], H.at[3, a], yp)
        two = copies.make(H.at[0, b], H.at[1, b], ym)
        rest = [
            copies.make(H.at[0, b], H.at[3, b], yp), copies.make(H.at[0, a], H.at[1, a], ym)
        ]
        far = [
            copies.make(H.at[3, a], H.at[2, a], yp), copies.make(H.at[1, b], H.at[2, b], ym)
        ]

        def begin():
            for copy in (one, two, *rest):
                copy.start()

        def forward():
            one.wait_recv()
            far[0].start()
            two.wait_recv()
            far[1].start()

        def near():
            for copy in rest:
                copy.wait_recv()

        def last():
            for copy in far:
                copy.wait_recv()

        return begin, forward, near, last

    begin1, forward1, near1, last1 = gather(H1)
    stays = jnp.logical_not(moves)

    @pl.when(moves)
    def _():
        swap(src, src_in, 2).start()

    @pl.when(stays)
    def _():
        for q in range(4):
            columns = slice(q * QW, (q + 1) * QW)
            H1[0, :, columns] = jnp.where(
                piece == float(q), src[...].astype(F32), H1[0, :, columns].astype(F32)
            ).astype(BF)
        begin1()

    ahead(load1, 1)

    def turned(v):
        return jnp.concatenate([v[:, 44:88], v[:, 0:44], v[:, 132:176], v[:, 88:132]], axis=1)

    for load in loads[9:13]:
        load.wait()
    spot = jnp.where(
        iota((CACHE_ROWS, 62), 0) == iota((CACHE_ROWS, 62), 1), pos_in[...].astype(F32), 0.0
    )
    spot = jnp.sum(spot, axis=1, keepdims=True)
    high = jnp.floor(spot * (1.0 / 64))
    lanes = iota((CACHE_ROWS, 64), 1).astype(F32)

    def chosen(at, n):
        hit = jnp.where(lanes == at, 1.0, 0.0)
        both = jnp.dot(hit, table[n], preferred_element_type=F32, precision=lax.Precision.HIGHEST)
        return both[0:62, 0:176], both[0:62, 176:352]

    (cos_a, sin_a), (cos_b, sin_b) = chosen(high, 0), chosen(spot - 64.0 * high, 1)
    cosine, sine = cos_a * cos_b - sin_a * sin_b, sin_a * cos_b + cos_a * sin_b
    raw = ck_in[...].astype(F32)
    cache_row = jnp.concatenate(
        [raw * cosine + turned(raw) * sine, cv_in[...].astype(F32), jnp.zeros((62, 32), F32)], axis=1
    )
    C[0, own_cache] = jnp.zeros((CACHE_ROWS, CACHE_COLS), BF)
    C[0, own_cache, 0:62, :] = cache_row.astype(BF)
    ahead(load1, 2)

    pl.when(stays)(forward1)

    @pl.when(moves)
    def _():
        swap(patches, xin, 0).wait()
        swap(meta, meta_in, 1).wait()
        swap(src, src_in, 2).wait()
        quarters = padded(xin)
        piece = as_column(meta_in[1:2, :])
        for q in range(4):
            H1[0, :, q * QW : (q + 1) * QW] = jnp.where(
                piece == float(q), src_in[...].astype(F32), quarters[q]
            ).astype(BF)
        begin1()

    ahead(load2, 2)
    pl.when(moves)(forward1)
    ahead(load1, 1)
    ahead(load2, 1)
    near1()
    ahead(load2, 1)
    last1()
    ahead(load1, 1)
    drain(load1)
    ahead(load2, 1)

    plane_of = [c, 1 - c]
    x_of = [mod(k - x, 4) for k in range(4)]
    z_of = [lax.rem(k - z + 8 + 2, 8) for k in range(8)]

    def weight(B, at, start, size):
        pieces = []
        for k in range(32):
            p, x_at, z_at = plane_of[k % 2], x_of[k // 8], z_of[at * 4 + k // 2 % 4]
            spot = (p, x_at, z_at) if B.shape[1] == 4 else (p, z_at, x_at)
            pieces.append(B[(*spot, slice(None), slice(start, start + size))])
        return jnp.concatenate(pieces, axis=0)

    for load in loads[17:20]:
        load.wait()
    wide_kv, wide_q, narrow = wide_kv_in[...], wide_q_in[...], narrow_in[...]

    rows = H1[...].reshape(4 * TOK, DP)
    sides = []
    for at in range(2):
        joined = dot(rows, weight(WA, at, 128, 512)).astype(BF)
        KV[0, at] = dot(joined, wide_kv).astype(BF)
        sides.append(copies.start(KV.at[0, at], KV.at[1, at], sibling))
    ahead(load3, 1)
    for at in range(2):
        joined = dot(rows, weight(WA, at, 0, 256)).astype(BF)
        Q[at] = dot(joined, wide_q).astype(BF).reshape(4, TOK, 256)
    ahead(load3, 1)
    for copy in sides:
        copy.wait_recv()

    def attend(block):
        total = None
        for at in range(2):
            heads = []
            for h in range(2):
                span = slice(h * 128, h * 128 + 128)
                vspan = slice(256 + h * 128, 256 + h * 128 + 128)
                q = Q[at, block, :, span]
                s = [dot_nt(q, KV[k, at, :, span]) for k in range(2)]
                top = jnp.maximum(
                    jnp.max(s[0], axis=1, keepdims=True), jnp.max(s[1], axis=1, keepdims=True)
                )
                p = [jnp.exp2(part * RATE - top * RATE) for part in s]
                mass = jnp.sum(p[0], axis=1, keepdims=True) + jnp.sum(p[1], axis=1, keepdims=True)
                o = dot(p[0].astype(BF), KV[0, at, :, vspan]) + dot(
                    p[1].astype(BF), KV[1, at, :, vspan]
                )
                heads.append((o / mass).astype(BF))
            both_heads = dot(jnp.concatenate(heads, axis=1), narrow).astype(BF)
            term = dot_nt(both_heads, weight(WA, at, 512, 256))
            total = term if total is None else total + term
        return total

    def scatter(partial, S, B, R, far_first, between):
        a, b = pl.ds(0, 64), pl.ds(64, 64)

        def send_far():
            S[0] = partial(2).astype(BF)
            return [
                copies.start(S.at[0, a], B.at[0], yp), copies.start(S.at[0, b], B.at[1], ym)
            ]

        def send_near():
            S[1] = partial(1).astype(BF)
            one = copies.start(S.at[1, b], R.at[0, b], yp)
            S[2] = partial(3).astype(BF)
            return [one, copies.start(S.at[2, a], R.at[1, a], ym)]

        if far_first:
            far = send_far()
            between(0)
            near = send_near()
            between(1)
        else:
            near = send_near()
            far = send_far()
            between(0)
        far[0].wait_recv()
        S[1, 0:64, :] = (S[1, 0:64, :].astype(F32) + B[0].astype(F32)).astype(BF)
        near.append(copies.start(S.at[1, a], R.at[0, a], yp))
        far[1].wait_recv()
        S[2, 64:128, :] = (S[2, 64:128, :].astype(F32) + B[1].astype(F32)).astype(BF)
        near.append(copies.start(S.at[2, b], R.at[1, b], ym))
        own = partial(0)
        between(2)
        for copy in near:
            copy.wait_recv()
        return own + R[0].astype(F32) + R[1].astype(F32)

    def beside_attention(n):
        if n == 0:
            ahead(load2, 1)
            ahead(load3, 1)
        elif n == 1:
            ahead(load3, 1)
            ahead(load2, 1)
        else:
            ahead(load3, 1)
            drain(load2)

    total = scatter(attend, SB, RB, RC, True, beside_attention)
    mixed[...] = (res[...].astype(F32) + total).astype(BF)
    H2[0] = norm_padded(mixed[...].astype(F32), valid).astype(BF)
    begin2, forward2, near2, last2 = gather(H2)
    begin2()

    @pl.loop(1, 16)
    def _(k):
        to = lax.rem(own_cache + k, 16)
        spot = C.at[0, own_cache]
        device = dev(lax.div(to, 4), zh * 4 + lax.rem(to, 4), y, c)
        remote(spot, spot, c_send, c_recv, device).start()

    ahead(load3, 1)

    def up(block, at):
        rows = H2[block]
        return [
            jax.nn.gelu(dot(rows, weight(WU, at, 0, 512))).astype(BF),
            jax.nn.gelu(dot(rows, weight(WU2, at, 0, 256))).astype(BF),
        ]

    def down(hidden, at):
        return dot_nt(hidden[0], weight(WD, at, 0, 512)) + dot_nt(
            hidden[1], weight(WD2, at, 0, 256)
        )

    def up_down(block):
        return down(up(block, 0), 0) + down(up(block, 1), 1)

    for at in range(2):
        first, second = up(0, at)
        HID[at, :, 0:512] = first
        HID[at, :, 512:768] = second
    forward2()
    copies.retire(24)
    near2()
    ahead(load3, 1)
    drain(load3)

    def near_rows(block):
        return up_down(block)

    def far_rows(block):
        last2()
        return up_down(block)

    def own_rows(block):
        own = [(HID[at, :, 0:512], HID[at, :, 512:768]) for at in range(2)]
        return down(own[0], 0) + down(own[1], 1)

    def beside_mlp(n):
        if n == 2:
            copies.retire(8)
            all_of(C.at[0, pl.ds(0, 15)], c_send, c_recv).wait_recv()
            remote(C.at[0], C.at[1], side_send, side_recv, sibling).start()

    calls = [near_rows, near_rows, far_rows, own_rows]
    total = scatter(lambda block: calls.pop(0)(block), SB2, RB2, RC2, False, beside_mlp)
    last = (mixed[...].astype(F32) + total).astype(BF)
    columns = [
        dot_nt(last[:, q * QW : (q + 1) * QW], pad[q, 0:size, :])
        for q, (_, size) in enumerate(WINDOWS)
    ]
    parts = [
        columns[0][:, 0:256],
        columns[0][:, 256:384] + columns[1][:, 0:128],
        columns[1][:, 128:384],
        columns[1][:, 384:512] + columns[2][:, 0:128],
        columns[2][:, 128:384],
        columns[2][:, 384:512] + columns[3][:, 0:128],
        columns[3][:, 128:384],
    ]
    plain = jnp.concatenate(parts, axis=1)
    sums[...] = jnp.sum(plain, axis=0, keepdims=True)

    other = f + 1 - 2 * c
    home = f - c + zh
    slot = 2 * y + c

    def share(k):
        return remote(sums, pooled.at[slot], s1, r1, (home, lax.rem(t + k, 8)))

    @pl.when(moves)
    def _():
        share(0).start()

    @pl.when(jnp.logical_not(moves))
    def _():
        pooled[slot] = sums[...]

    for k in range(1, 8):
        share(k).start()

    result[...] = plain.astype(BF)

    @pl.when(moves)
    def _():
        swap(result, swapped, 3).start()

    remote(C.at[0], C.at[1], side_send, side_recv, sibling).wait_recv()
    for load in loads[20:]:
        load.wait()

    @pl.when(moves)
    def _():
        all_of(pooled, s1, r1).wait_recv()

    @pl.when(jnp.logical_not(moves))
    def _():
        all_of(pooled.at[pl.ds(0, 7)], s1, r1).wait_recv()

    mean_frame = pooled[0]
    for k in range(1, 8):
        mean_frame = mean_frame + pooled[k]
    mean_frame = mean_frame * (1.0 / P_SIZE)
    center = mean_frame - jnp.sum(mean_frame, axis=1, keepdims=True) * (1.0 / D)
    spread = jnp.sum(center * center, axis=1, keepdims=True) * (1.0 / D)
    normed = center * lax.rsqrt(spread + 1e-06)

    def pick(v):
        got = v[:, 0:176]
        for k in range(1, 8):
            got = jnp.where(t == k, v[:, k * 176 : k * 176 + 176], got)
        return got

    features = jnp.broadcast_to(pick(normed), (8, 176)).astype(BF)
    for n, w in enumerate((tq_w, tk_w, tv_w)):
        part = dot(features, w[...])
        for k in range(8):
            qkv_send[k, n, :, 0:176] = part[0:1, k * 176 : k * 176 + 176]

    def send_heads(k):
        to = lax.rem(t + k, 8)
        return remote(qkv_send.at[to], qkv_recv.at[t], s2, r2, (f, to))

    for k in range(1, 8):
        send_heads(k).start()
    qkv_recv[t] = qkv_send[t]
    all_of(qkv_recv.at[pl.ds(0, 7)], s2, r2).wait_recv()

    whole = []
    for n in range(3):
        v = qkv_recv[0, n, :, 0:176]
        for k in range(1, 8):
            v = v + qkv_recv[k, n, :, 0:176]
        whole.append(v)

    def rot(v):
        return (v * turn[0:1, :] + turned(v) * turn[1:2, :]).astype(BF).astype(F32)

    new_send[...] = jnp.zeros_like(new_send)
    new_send[:, 0:176] = rot(whole[1])
    new_send[:, 176:352] = whole[2].astype(BF).astype(F32)


    @pl.loop(1, 32)
    def _(k):
        remote(new_send, new_all.at[f], s3, r3, (lax.rem(f + k, 32), t)).start()

    new_all[f] = new_send[...]
    query = rot(whole[0])
    lane = iota((1, 176), 1)
    wide_query = jnp.concatenate(
        [jnp.where(lane < HD, query, 0.0), jnp.where(lane >= HD, query, 0.0), jnp.zeros((6, 176), F32)],
        axis=0,
    )
    queries = jnp.concatenate([wide_query, jnp.zeros((8, 80), F32)], axis=1).astype(BF)
    count = 32 * CACHE_ROWS
    old_keys = C[:, :, :, 0:256].reshape(count, 256)
    s_old = dot_nt(queries, old_keys)
    s_old = jnp.where((iota((8, count), 1) & (CACHE_ROWS - 1)) < 62, s_old, -1e30)

    all_of(new_all.at[pl.ds(0, 31)], s3, r3).wait_recv()
    known = new_all[:, 0, :]
    s_new = dot_nt(queries, known[:, 0:256].astype(BF))
    s_new = jnp.where(iota((8, 32), 1) <= f, s_new, -1e30)
    top = jnp.maximum(
        jnp.max(s_old, axis=1, keepdims=True), jnp.max(s_new, axis=1, keepdims=True)
    )
    p_old = jnp.exp2(s_old * RATE - top * RATE)
    p_new = jnp.exp2(s_new * RATE - top * RATE)
    p_old = jnp.where((iota((8, count), 1) & (CACHE_ROWS - 1)) < 62, p_old, 0.0)
    p_new = jnp.where(iota((8, 32), 1) <= f, p_new, 0.0)
    mass = jnp.sum(p_old, axis=1, keepdims=True) + jnp.sum(p_new, axis=1, keepdims=True)
    old_values = C[:, :, :, 128:384].reshape(count, 256)
    o = dot(p_old.astype(BF), old_values) + dot(p_new.astype(BF), known[:, 128:384].astype(BF))
    o = o / mass
    temporal = jnp.where(lane < HD, o[0:1, 48:224], o[1:2, 48:224])
    part = dot(jnp.broadcast_to(temporal, (8, 176)).astype(BF), to_w[...])
    for k in range(8):
        last_send[k, :, 0:176] = part[0:1, k * 176 : k * 176 + 176]

    def send_last(k):
        to = lax.rem(t + k, 8)
        return remote(last_send.at[to], last_recv.at[t], s4, r4, (f, to))

    for k in range(1, 8):
        send_last(k).start()
    last_recv[t] = last_send[t]

    stored, kept = (pltpu.make_async_copy(a, out, local.at[0]) for a in (swapped, result))

    @pl.when(moves)
    def _():
        swap(result, swapped, 3).wait()
        stored.start()

    @pl.when(jnp.logical_not(moves))
    def _():
        kept.start()

    copies.retire()
    all_of(C.at[0, pl.ds(0, 15)], c_send, c_recv).wait_send()
    remote(C.at[0], C.at[1], side_send, side_recv, sibling).wait_send()

    @pl.when(moves)
    def _():
        all_of(pooled, s1, r1).wait_send()

    @pl.when(jnp.logical_not(moves))
    def _():
        all_of(pooled.at[pl.ds(0, 7)], s1, r1).wait_send()

    all_of(qkv_recv.at[pl.ds(0, 7)], s2, r2).wait_send()
    all_of(new_all.at[pl.ds(0, 31)], s3, r3).wait_send()
    all_of(last_recv.at[pl.ds(0, 7)], s4, r4).wait_recv()
    total = pick(mean_frame)
    for k in range(8):
        total = total + last_recv[k, :, 0:176]
    frame_out[...] = total.astype(BF)
    all_of(last_recv.at[pl.ds(0, 7)], s4, r4).wait_send()

    @pl.when(moves)
    def _():
        stored.wait()

    @pl.when(jnp.logical_not(moves))
    def _():
        kept.wait()


BIG = 160


def call(*operands):
    turn = operands[-1]
    vmem = pl.BlockSpec(memory_space=pltpu.VMEM)
    dma = pltpu.SemaphoreType.DMA
    held = [pltpu.VMEM(a.shape, a.dtype) for a in operands[:-1]] + [
        pltpu.VMEM(turn.shape[1:], F32)
    ]
    return pl.pallas_call(
        kernel,
        out_shape=(
            jax.ShapeDtypeStruct((TOK, D), BF),
            jax.ShapeDtypeStruct((1, 176), BF),
        ),
        in_specs=[pl.BlockSpec(memory_space=pl.ANY)] * len(operands),
        out_specs=(pl.BlockSpec(memory_space=pl.ANY), vmem),
        scratch_shapes=held
        + [
            pltpu.VMEM((2, TOK), F32),
            pltpu.VMEM((TOK, D), BF),
            pltpu.VMEM((2, TOK), F32),
            pltpu.VMEM((TOK, QW), BF),
            pltpu.VMEM((TOK, QW), BF),
            pltpu.VMEM((TOK, DP), BF),
            pltpu.VMEM((2, 4, 8, W_ROWS, WC), BF),
            pltpu.VMEM((2, 4, 8, W_ROWS, 512), BF),
            pltpu.VMEM((2, 8, 4, W_ROWS, 256), BF),
            pltpu.VMEM((2, 4, 8, W_ROWS, 512), BF),
            pltpu.VMEM((2, 8, 4, W_ROWS, 256), BF),
            pltpu.VMEM((2, 16, CACHE_ROWS, CACHE_COLS), BF),
            pltpu.VMEM((TOK, QW), BF),
            pltpu.VMEM((2, TOK, QW), BF),
            pltpu.VMEM((4, TOK, DP), BF),
            pltpu.VMEM((2, 2, 4 * TOK, 512), BF),
            pltpu.VMEM((2, 4, TOK, 256), BF),
            pltpu.VMEM((3, TOK, DP), BF),
            pltpu.VMEM((2, 64, DP), BF),
            pltpu.VMEM((2, TOK, DP), BF),
            pltpu.VMEM((TOK, DP), BF),
            pltpu.VMEM((4, TOK, DP), BF),
            pltpu.VMEM((2, TOK, 768), BF),
            pltpu.VMEM((3, TOK, DP), BF),
            pltpu.VMEM((2, 64, DP), BF),
            pltpu.VMEM((2, TOK, DP), BF),
            pltpu.VMEM((TOK, D), BF),
            pltpu.VMEM((TOK, D), BF),
            pltpu.VMEM((1, D), F32),
            pltpu.VMEM((8, 1, D), F32),
            pltpu.VMEM((8, 3, 1, 256), F32),
            pltpu.VMEM((8, 3, 1, 256), F32),
            pltpu.VMEM((1, CACHE_COLS), F32),
            pltpu.VMEM((32, 1, CACHE_COLS), F32),
            pltpu.VMEM((8, 1, 256), F32),
            pltpu.VMEM((8, 1, 256), F32),
            dma((len(operands),)),
            dma((BIG,)), dma((BIG,)),
            dma((4,)), dma((4,)),
            dma, dma, dma, dma,
            dma, dma, dma, dma, dma, dma, dma, dma,
        ],
        compiler_params=pltpu.CompilerParams(
            collective_id=0, has_side_effects=True, vmem_limit_bytes=56 * 1024 * 1024
        ),
        cost_estimate=pl.CostEstimate(
            flops=8_000_000_000, bytes_accessed=20_000_000, transcendentals=3_000_000
        ),
    )(*operands)


def constants():
    grow = np.arange(48)[:, None] == np.arange(44)[None, :]
    spread = np.stack(
        [np.arange(176)[:, None] + n * 176 == np.arange(WC)[None, :] for n in range(4)]
    )
    pad = np.zeros((4, 512, QW), bool)
    k = np.arange(QW)
    for q, (start, size) in enumerate(WINDOWS):
        at = k % 48
        row = 352 * q + k // 48 * 44 + at - start
        pad[q, :size] = (np.arange(size)[:, None] == row[None, :]) & (at < 44)[None, :]

    def wider(rows, first, columns, start):
        k = np.arange(columns) + start
        at = k % 128
        row = k // 128 * HD + at - first
        return (np.arange(rows)[:, None] == row[None, :]) & (at < HD)[None, :]

    valid = (np.arange(DP) % 48 < 44)[None, :]
    narrow = wider(256, -16, 256, 0).T
    held = [jnp.asarray(a.astype(np.float32), BF) for a in (pad, grow, spread)]
    heads = [
        jnp.asarray(a.astype(np.float32), BF)
        for a in (wider(512, 128, 512, 256), wider(256, 0, 256, 0), narrow)
    ]
    return (*held, *heads, jnp.asarray(valid.astype(np.float32)))


def body(
    patches, shift_offset, shift_slice, w_query, w_key, w_value, w_out, w_up, w_down,
    t_query, t_key, t_value, t_out, cache_keys, cache_values, cache_pos,
):
    half = HD // 2
    freq = np.float32(10000.0) ** (-np.arange(half, dtype=np.float32) / np.float32(half))
    angle = (SPAN + np.arange(FRAMES)).astype(np.float32)[:, None] * freq[None, :]
    cosine, sine = np.cos(angle), np.sin(angle)
    turn = np.stack(
        [
            np.concatenate([cosine] * 4, axis=1),
            np.concatenate([-sine, sine, -sine, sine], axis=1),
        ],
        axis=1,
    ).astype(np.float32)
    steps = np.arange(64)[:, None] * (10000.0 ** (-np.arange(half) / half))[None, :]
    sign = np.where(np.arange(2 * HD) % HD < half, -1.0, 1.0)
    table = np.stack(
        [
            np.concatenate([np.tile(np.cos(a), 4), np.tile(np.sin(a), 4) * sign], axis=1)
            for a in (64 * steps, steps)
        ]
    ).astype(np.float32)
    patch_out, frame_out = call(
        patches[0], shift_offset[None], shift_slice[None], w_query, w_key, w_value,
        w_out.T, w_up, w_down.T, t_query, t_key, t_value, t_out, cache_keys, cache_values, cache_pos[None],
        jnp.asarray(table), *constants(), jnp.asarray(turn),
    )
    return (patch_out[None], frame_out)


def solution(mesh):
    return jax.shard_map(
        body,
        mesh=mesh,
        in_specs=(
            P("frame", "tok", None),
            P("tok"),
            P("tok"),
            P("frame", "tok"),
            P("frame", "tok"),
            P("frame", "tok"),
            P("tok", "frame"),
            P("frame", "tok"),
            P("tok", "frame"),
            P("tok", None),
            P("tok", None),
            P("tok", None),
            P("tok", None),
            P("frame", "tok"),
            P("frame", "tok"),
            P("frame"),
        ),
        out_specs=(P("frame", "tok", None), P("frame", "tok")),
        check_vma=False,
    )
```

```python
import jax
import jax.numpy as jnp
import numpy as np
from jax import lax
from jax.experimental import pallas as pl
from jax.experimental.pallas import tpu as pltpu
from jax.sharding import PartitionSpec as P

HEADS = 16
HD = 88
P_SIZE = 1024
SPAN = 4096
FRAMES = 32
D = 1408
DP = 1536
QW = 384
TOK = 128
SCALE = HD ** (-0.5)
RATE = SCALE * 1.4426950408889634
MESH = pl.DeviceIdType.MESH
F32 = jnp.float32
BF = jnp.bfloat16
WC = 768
W_ROWS, CACHE_ROWS, CACHE_COLS = 48, 64, 384
WINDOWS = ((0, 384), (256, 512), (640, 512), (1024, 384))


def dot(a, b):
    return jnp.dot(a, b, preferred_element_type=F32)


def dot_nt(a, b):
    return lax.dot_general(a, b, (((1,), (1,)), ((), ())), preferred_element_type=F32)


def iota(shape, axis):
    return lax.broadcasted_iota(jnp.int32, shape, axis)


def mod(a, n):
    return lax.rem(a + n, n)


def remote(src, dst, send, recv, device):
    return pltpu.make_async_remote_copy(
        src_ref=src, dst_ref=dst, send_sem=send, recv_sem=recv,
        device_id=device, device_id_type=MESH,
    )


class Leg:
    def __init__(self, src, dst, device, send, recv):
        self.ends = (src, dst, send, recv, device)

    def start(self):
        remote(*self.ends).start()

    def wait_recv(self):
        remote(*self.ends).wait_recv()

    def wait_send(self):
        remote(*self.ends).wait_send()


class Copies:
    def __init__(self, send, recv):
        self.send, self.recv, self.used, self.open = send, recv, 0, []

    def make(self, src, dst, device):
        n = self.used
        self.used += 1
        copy = Leg(src, dst, device, self.send.at[n], self.recv.at[n])
        self.open.append(copy)
        return copy

    def start(self, src, dst, device):
        copy = self.make(src, dst, device)
        copy.start()
        return copy

    def retire(self, keep=0):
        while len(self.open) > keep:
            self.open.pop(0).wait_send()


def norm_padded(v, valid):
    mean = jnp.sum(v, axis=1, keepdims=True) * (1.0 / D)
    center = jnp.where(valid, v - mean, 0.0)
    spread = jnp.sum(center * center, axis=1, keepdims=True) * (1.0 / D)
    return center * lax.rsqrt(spread + 1e-06)


def as_column(row):
    spread = jnp.where(iota((TOK, TOK), 0) == iota((TOK, TOK), 1), row, 0.0)
    return jnp.sum(spread, axis=1, keepdims=True)


def kernel(
    patches_hbm, offset_hbm, piece_hbm, wq_hbm, wk_hbm, wv_hbm, wo_hbm, wu_hbm, wd_hbm,
    tq_hbm, tk_hbm, tv_hbm, to_hbm, ck_hbm, cv_hbm, pos_hbm, table_hbm, turn_hbm,
    out, frame_out,
    patches, offset_in, piece_in, wq, wk, wv, wo, wu, wd, tq_w, tk_w, tv_w, to_w, ck_in, cv_in, pos_in, table, turn,
    meta, xin, meta_in, src, src_in, pad, res, WA, WU, WD, C, comp, around, H1, KV, Q,
    SB, RB, RC, mixed, H2, HID, SB2, RB2, RC2,
    result, swapped, sums, pooled, qkv_send, qkv_recv, new_send, new_all, last_send, last_recv,
    local, big_send, big_recv, swap_send, swap_recv, c_send, c_recv, side_send, side_recv, s1, r1, s2, r2, s3, r3, s4, r4,
):
    f = lax.axis_index("frame")
    t = lax.axis_index("tok")
    x, zl, c = lax.div(f, 8), lax.div(lax.rem(f, 8), 2), lax.rem(f, 2)
    y, zh = lax.div(t, 2), lax.rem(t, 2)
    z = zh * 4 + zl

    def place(r):
        return (r + 2) % 8

    loads = [
        pltpu.make_async_copy(a, b, local.at[n])
        for n, (a, b) in enumerate(
            (
                (patches_hbm, patches), (offset_hbm, offset_in), (piece_hbm, piece_in),
                (wq_hbm, wq), (wk_hbm, wk), (wv_hbm, wv), (wo_hbm, wo), (wu_hbm, wu), (wd_hbm, wd),
                (ck_hbm, ck_in), (cv_hbm, cv_in), (pos_hbm, pos_in), (table_hbm, table),
                (turn_hbm.at[f], turn), (tq_hbm, tq_w), (tk_hbm, tk_w), (tv_hbm, tv_w), (to_hbm, to_w),
            )
        )
    ]
    for load in loads:
        load.start()
    new_all[...] = jnp.zeros_like(new_all)

    def dev(x_at, z_at, y_at, c_at):
        return (x_at * 8 + lax.rem(z_at, 4) * 2 + c_at, y_at * 2 + lax.div(z_at, 4))

    xp, xm = dev(mod(x + 1, 4), z, y, c), dev(mod(x - 1, 4), z, y, c)
    yp, ym = dev(x, z, mod(y + 1, 4), c), dev(x, z, mod(y - 1, 4), c)
    zp, zm = dev(x, mod(z + 1, 8), y, c), dev(x, mod(z - 1, 8), y, c)
    sibling = dev(x, z, y, 1 - c)
    partner = dev(x, mod(z + 4, 8), y, 1 - c)
    after, before = (mod(f + 1, 32), t), (mod(f - 1, 32), t)

    own_cache = x * 4 + zl

    def all_of(ref, send, recv):
        return remote(ref, ref, send, recv, sibling)

    barrier = pltpu.get_barrier_semaphore()
    friends = (xp, xm, yp, ym, zp, zm, sibling, partner, after, before)
    for friend in friends:
        pl.semaphore_signal(barrier, inc=1, device_id=friend, device_id_type=MESH)
    pl.semaphore_wait(barrier, len(friends))

    copies = Copies(big_send, big_recv)
    moves = c != zh

    def swap(src, dst, n):
        return remote(src, dst, swap_send.at[n], swap_recv.at[n], partner)

    for load in loads[0:3]:
        load.wait()
    meta[0:1, :] = offset_in[...].astype(F32)
    meta[1:2, :] = piece_in[...].astype(F32)

    @pl.when(moves)
    def _():
        swap(patches, xin, 0).start()
        swap(meta, meta_in, 1).start()

    for load in loads[3:7]:
        load.wait()
    grow = jnp.where(iota((48, 44), 0) == iota((48, 44), 1), 1.0, 0.0).astype(BF)
    total = None
    for n, w in enumerate((wq, wk, wv, wo)):
        to = jnp.where(
            iota((176, WC), 0) + n * 176 == iota((176, WC), 1), 1.0, 0.0
        ).astype(BF)
        term = dot(dot(grow, w[...]).astype(BF), to)
        total = term if total is None else total + term
    WA[0, 0, place(0)] = total.astype(BF)

    def z_first(B):
        def at(r):
            return B.at[0, 0, place(r)]

        waits = [copies.start(at(0), at(-1), zp), copies.start(at(0), at(1), zm)]
        yield
        firsts = []

        def across(run):
            firsts.append(copies.start(B.at[0, 0, run], B.at[0, 3, run], xp))
            firsts.append(copies.start(B.at[0, 0, run], B.at[0, 1, run], xm))

        half = B.shape[4] // 2
        low, high = pl.ds(0, half), pl.ds(half, half)
        for step in range(1, 5):
            for copy in waits:
                copy.wait_recv()
            if step < 3:
                waits = [
                    copies.start(at(-step), at(-step - 1), zp),
                    copies.start(at(step), at(step + 1), zm),
                ]
            elif step == 3:
                waits = [
                    copies.start(B.at[0, 0, place(-3), :, low], B.at[0, 0, place(4), :, low], zp),
                    copies.start(B.at[0, 0, place(3), :, high], B.at[0, 0, place(4), :, high], zm),
                ]
            if step == 2:
                across(pl.ds(0, 5))
            if step == 4:
                across(pl.ds(5, 3))
            if step < 4:
                yield

        def aside(x_at):
            return copies.start(B.at[0, x_at], B.at[1, x_at], sibling)

        sides = [aside(0)]
        yield
        for copy in firsts:
            copy.wait_recv()
        one, two = pl.ds(0, 4), pl.ds(4, 4)
        waits = [
            copies.start(B.at[0, 3, one], B.at[0, 2, one], xp),
            copies.start(B.at[0, 1, two], B.at[0, 2, two], xm),
        ]
        sides += [aside(3), aside(1)]
        yield
        for copy in waits:
            copy.wait_recv()
        sides.append(aside(2))
        yield
        for copy in sides:
            copy.wait_recv()

    def x_first(B):
        here = place(0)
        waits = [
            copies.start(B.at[0, here, 0], B.at[0, here, 3], xp),
            copies.start(B.at[0, here, 0], B.at[0, here, 1], xm),
        ]
        yield
        half = B.shape[4] // 2
        low, high = pl.ds(0, half), pl.ds(half, half)
        for copy in waits:
            copy.wait_recv()
        waits = [
            copies.start(B.at[0, here, 3, :, low], B.at[0, here, 2, :, low], xp),
            copies.start(B.at[0, here, 1, :, high], B.at[0, here, 2, :, high], xm),
        ]
        yield

        def at(r):
            return B.at[0, place(r)]

        one, two = pl.ds(0, 2), pl.ds(2, 2)
        for step in range(5):
            for copy in waits:
                copy.wait_recv()
            if step < 3:
                waits = [
                    copies.start(at(-step), at(-step - 1), zp),
                    copies.start(at(step), at(step + 1), zm),
                ]
                yield
            elif step == 3:
                waits = [
                    copies.start(B.at[0, place(-3), one], B.at[0, place(4), one], zp),
                    copies.start(B.at[0, place(3), two], B.at[0, place(4), two], zm),
                ]
                yield
        side = copies.start(B.at[0], B.at[1], sibling)
        yield
        side.wait_recv()

    def drain(task):
        for _ in task:
            pass

    def ahead(task, count):
        for _ in range(count):
            if next(task, "end") == "end":
                return

    def both(*tasks):
        tasks = list(tasks)
        while tasks:
            for task in list(tasks):
                if next(task, "end") == "end":
                    tasks.remove(task)
            if tasks:
                yield

    load1 = z_first(WA)
    load2, load3 = z_first(WU), z_first(WD)
    ahead(load1, 1)

    for q, (start, size) in enumerate(WINDOWS):
        r, k = iota((size, QW), 0) + start, iota((size, QW), 1)
        at = lax.rem(k, 48)
        hit = (r == 352 * q + lax.div(k, 48) * 44 + at) & (at < 44)
        pad[q, 0:size, :] = jnp.where(hit, 1.0, 0.0).astype(BF)
    valid = lax.rem(iota((1, DP), 1), 48) < 44

    def padded(rows):
        for q, (start, size) in enumerate(WINDOWS):
            res[:, q * QW : (q + 1) * QW] = dot(
                rows[:, start : start + size], pad[q, 0:size, :]
            ).astype(BF)
        normed = norm_padded(res[...].astype(F32), valid)
        return [normed[:, q * QW : (q + 1) * QW] for q in range(4)]

    quarters = padded(patches)
    offset, piece = as_column(meta[0:1, :]), as_column(meta[1:2, :])
    mine = quarters[0]
    for q in range(1, 4):
        mine = jnp.where(piece == float(q), quarters[q], mine)
    comp[...] = mine.astype(BF)
    for q in range(4):
        H1[0, :, q * QW : (q + 1) * QW] = quarters[q].astype(BF)
    hops = [
        copies.start(comp, around.at[0], after),
        copies.start(comp, around.at[1], before),
    ]
    for load in loads[7:9]:
        load.wait()
    for w, one in ((wu, WU), (wd, WD)):
        one[0, 0, place(0)] = dot(grow, w[...]).astype(BF)
    ahead(load1, 1)
    for copy in hops:
        copy.wait_recv()
    earlier = jnp.where(f > 0, around[0].astype(F32), 0.0)
    later = jnp.where(f < FRAMES - 1, around[1].astype(F32), 0.0)
    source = jnp.where(
        offset == -1.0, earlier, jnp.where(offset == 1.0, later, comp[...].astype(F32))
    )
    src[...] = source.astype(BF)

    def gather(H):
        a, b = pl.ds(0, 64), pl.ds(64, 64)
        one = copies.make(H.at[0, a], H.at[3, a], yp)
        two = copies.make(H.at[0, b], H.at[1, b], ym)
        rest = [
            copies.make(H.at[0, b], H.at[3, b], yp), copies.make(H.at[0, a], H.at[1, a], ym)
        ]
        far = [
            copies.make(H.at[3, a], H.at[2, a], yp), copies.make(H.at[1, b], H.at[2, b], ym)
        ]

        def begin():
            for copy in (one, two, *rest):
                copy.start()

        def forward():
            one.wait_recv()
            far[0].start()
            two.wait_recv()
            far[1].start()

        def near():
            for copy in rest:
                copy.wait_recv()

        def last():
            for copy in far:
                copy.wait_recv()

        return begin, forward, near, last

    begin1, forward1, near1, last1 = gather(H1)
    stays = jnp.logical_not(moves)

    @pl.when(moves)
    def _():
        swap(src, src_in, 2).start()

    @pl.when(stays)
    def _():
        for q in range(4):
            columns = slice(q * QW, (q + 1) * QW)
            H1[0, :, columns] = jnp.where(
                piece == float(q), src[...].astype(F32), H1[0, :, columns].astype(F32)
            ).astype(BF)
        begin1()

    ahead(load1, 1)

    def turned(v):
        return jnp.concatenate([v[:, 44:88], v[:, 0:44], v[:, 132:176], v[:, 88:132]], axis=1)

    for load in loads[9:13]:
        load.wait()
    spot = jnp.where(
        iota((CACHE_ROWS, 62), 0) == iota((CACHE_ROWS, 62), 1), pos_in[...].astype(F32), 0.0
    )
    spot = jnp.sum(spot, axis=1, keepdims=True)
    high = jnp.floor(spot * (1.0 / 64))
    lanes = iota((CACHE_ROWS, 64), 1).astype(F32)

    def chosen(at, n):
        hit = jnp.where(lanes == at, 1.0, 0.0)
        both = jnp.dot(hit, table[n], preferred_element_type=F32, precision=lax.Precision.HIGHEST)
        return both[0:62, 0:176], both[0:62, 176:352]

    (cos_a, sin_a), (cos_b, sin_b) = chosen(high, 0), chosen(spot - 64.0 * high, 1)
    cosine, sine = cos_a * cos_b - sin_a * sin_b, sin_a * cos_b + cos_a * sin_b
    sine = jnp.where(lax.rem(iota((62, 176), 1), HD) < HD // 2, -sine, sine)
    raw = ck_in[...].astype(F32)
    cache_row = jnp.concatenate(
        [raw * cosine + turned(raw) * sine, cv_in[...].astype(F32), jnp.zeros((62, 32), F32)], axis=1
    )
    C[0, own_cache] = jnp.zeros((CACHE_ROWS, CACHE_COLS), BF)
    C[0, own_cache, 0:62, :] = cache_row.astype(BF)
    ahead(load1, 2)

    pl.when(stays)(forward1)

    @pl.when(moves)
    def _():
        swap(patches, xin, 0).wait()
        swap(meta, meta_in, 1).wait()
        swap(src, src_in, 2).wait()
        quarters = padded(xin)
        piece = as_column(meta_in[1:2, :])
        for q in range(4):
            H1[0, :, q * QW : (q + 1) * QW] = jnp.where(
                piece == float(q), src_in[...].astype(F32), quarters[q]
            ).astype(BF)
        begin1()

    ahead(load2, 2)
    pl.when(moves)(forward1)
    ahead(load1, 1)
    ahead(load2, 1)
    near1()
    ahead(load2, 1)
    last1()
    ahead(load1, 1)
    drain(load1)
    ahead(load2, 1)

    plane_of = [c, 1 - c]
    x_of = [mod(k - x, 4) for k in range(4)]
    z_of = [lax.rem(k - z + 8 + 2, 8) for k in range(8)]

    def weight(B, at, start, size):
        pieces = []
        for k in range(32):
            p, x_at, z_at = plane_of[k % 2], x_of[k // 8], z_of[at * 4 + k // 2 % 4]
            spot = (p, x_at, z_at) if B.shape[1] == 4 else (p, z_at, x_at)
            pieces.append(B[(*spot, slice(None), slice(start, start + size))])
        return jnp.concatenate(pieces, axis=0)

    def wider(rows, first, columns, start):
        r, k = iota((rows, columns), 0) + first, iota((rows, columns), 1) + start
        at = lax.rem(k, 128)
        return jnp.where((r == lax.div(k, 128) * HD + at) & (at < HD), 1.0, 0.0).astype(BF)

    wide_q, wide_kv = wider(256, 0, 256, 0), wider(512, 128, 512, 256)
    r, k = iota((256, 256), 1) + 512, iota((256, 256), 0)
    at = lax.rem(k, 128)
    narrow = jnp.where(
        (r == 528 + lax.div(k, 128) * HD + at) & (at < HD), 1.0, 0.0
    ).astype(BF)

    rows = H1[...].reshape(4 * TOK, DP)
    sides = []
    for at in range(2):
        joined = dot(rows, weight(WA, at, 128, 512)).astype(BF)
        KV[0, at] = dot(joined, wide_kv).astype(BF)
        sides.append(copies.start(KV.at[0, at], KV.at[1, at], sibling))
    ahead(load3, 1)
    for at in range(2):
        joined = dot(rows, weight(WA, at, 0, 256)).astype(BF)
        Q[at] = dot(joined, wide_q).astype(BF).reshape(4, TOK, 256)
    ahead(load3, 1)
    for copy in sides:
        copy.wait_recv()

    def attend(block):
        total = None
        for at in range(2):
            heads = []
            for h in range(2):
                span = slice(h * 128, h * 128 + 128)
                vspan = slice(256 + h * 128, 256 + h * 128 + 128)
                q = Q[at, block, :, span]
                s = [dot_nt(q, KV[k, at, :, span]) for k in range(2)]
                top = jnp.maximum(
                    jnp.max(s[0], axis=1, keepdims=True), jnp.max(s[1], axis=1, keepdims=True)
                )
                p = [jnp.exp2(part * RATE - top * RATE) for part in s]
                mass = jnp.sum(p[0], axis=1, keepdims=True) + jnp.sum(p[1], axis=1, keepdims=True)
                o = dot(p[0].astype(BF), KV[0, at, :, vspan]) + dot(
                    p[1].astype(BF), KV[1, at, :, vspan]
                )
                heads.append((o / mass).astype(BF))
            both_heads = dot(jnp.concatenate(heads, axis=1), narrow).astype(BF)
            term = dot_nt(both_heads, weight(WA, at, 512, 256))
            total = term if total is None else total + term
        return total

    def scatter(partial, S, B, R, far_first, between):
        a, b = pl.ds(0, 64), pl.ds(64, 64)

        def send_far():
            S[0] = partial(2).astype(BF)
            return [
                copies.start(S.at[0, a], B.at[0], yp), copies.start(S.at[0, b], B.at[1], ym)
            ]

        def send_near():
            S[1] = partial(1).astype(BF)
            one = copies.start(S.at[1, b], R.at[0, b], yp)
            S[2] = partial(3).astype(BF)
            return [one, copies.start(S.at[2, a], R.at[1, a], ym)]

        if far_first:
            far = send_far()
            between(0)
            near = send_near()
            between(1)
        else:
            near = send_near()
            far = send_far()
            between(0)
        far[0].wait_recv()
        S[1, 0:64, :] = (S[1, 0:64, :].astype(F32) + B[0].astype(F32)).astype(BF)
        near.append(copies.start(S.at[1, a], R.at[0, a], yp))
        far[1].wait_recv()
        S[2, 64:128, :] = (S[2, 64:128, :].astype(F32) + B[1].astype(F32)).astype(BF)
        near.append(copies.start(S.at[2, b], R.at[1, b], ym))
        own = partial(0)
        between(2)
        for copy in near:
            copy.wait_recv()
        return own + R[0].astype(F32) + R[1].astype(F32)

    def beside_attention(n):
        if n == 0:
            ahead(load2, 1)
            ahead(load3, 1)
        elif n == 1:
            ahead(load3, 1)
            ahead(load2, 1)
        else:
            ahead(load3, 1)
            drain(load2)

    total = scatter(attend, SB, RB, RC, True, beside_attention)
    mixed[...] = (res[...].astype(F32) + total).astype(BF)
    H2[0] = norm_padded(mixed[...].astype(F32), valid).astype(BF)
    begin2, forward2, near2, last2 = gather(H2)
    begin2()

    @pl.loop(1, 16)
    def _(k):
        to = lax.rem(own_cache + k, 16)
        spot = C.at[0, own_cache]
        device = dev(lax.div(to, 4), zh * 4 + lax.rem(to, 4), y, c)
        remote(spot, spot, c_send, c_recv, device).start()

    ahead(load3, 1)

    def up(block, at):
        return jax.nn.gelu(dot(H2[block], weight(WU, at, 0, 768))).astype(BF)

    def down(hidden, at):
        return dot_nt(hidden, weight(WD, at, 0, 768))

    def up_down(block):
        return down(up(block, 0), 0) + down(up(block, 1), 1)

    for at in range(2):
        HID[at] = up(0, at)
    forward2()
    copies.retire(24)
    near2()
    ahead(load3, 1)
    drain(load3)

    def near_rows(block):
        return up_down(block)

    def far_rows(block):
        last2()
        return up_down(block)

    def own_rows(block):
        return down(HID[0], 0) + down(HID[1], 1)

    def beside_mlp(n):
        if n == 2:
            copies.retire(8)
            all_of(C.at[0, pl.ds(0, 15)], c_send, c_recv).wait_recv()
            remote(C.at[0], C.at[1], side_send, side_recv, sibling).start()

    calls = [near_rows, near_rows, far_rows, own_rows]
    total = scatter(lambda block: calls.pop(0)(block), SB2, RB2, RC2, False, beside_mlp)
    last = (mixed[...].astype(F32) + total).astype(BF)
    columns = [
        dot_nt(last[:, q * QW : (q + 1) * QW], pad[q, 0:size, :])
        for q, (_, size) in enumerate(WINDOWS)
    ]
    parts = [
        columns[0][:, 0:256],
        columns[0][:, 256:384] + columns[1][:, 0:128],
        columns[1][:, 128:384],
        columns[1][:, 384:512] + columns[2][:, 0:128],
        columns[2][:, 128:384],
        columns[2][:, 384:512] + columns[3][:, 0:128],
        columns[3][:, 128:384],
    ]
    plain = jnp.concatenate(parts, axis=1)
    sums[...] = jnp.sum(plain, axis=0, keepdims=True)

    other = f + 1 - 2 * c
    home = f - c + zh
    slot = 2 * y + c

    def share(k):
        return remote(sums, pooled.at[slot], s1, r1, (home, lax.rem(t + k, 8)))

    @pl.when(moves)
    def _():
        share(0).start()

    @pl.when(jnp.logical_not(moves))
    def _():
        pooled[slot] = sums[...]

    for k in range(1, 8):
        share(k).start()

    result[...] = plain.astype(BF)

    @pl.when(moves)
    def _():
        swap(result, swapped, 3).start()

    remote(C.at[0], C.at[1], side_send, side_recv, sibling).wait_recv()
    for load in loads[13:]:
        load.wait()

    @pl.when(moves)
    def _():
        all_of(pooled, s1, r1).wait_recv()

    @pl.when(jnp.logical_not(moves))
    def _():
        all_of(pooled.at[pl.ds(0, 7)], s1, r1).wait_recv()

    mean_frame = pooled[0]
    for k in range(1, 8):
        mean_frame = mean_frame + pooled[k]
    mean_frame = mean_frame * (1.0 / P_SIZE)
    center = mean_frame - jnp.sum(mean_frame, axis=1, keepdims=True) * (1.0 / D)
    spread = jnp.sum(center * center, axis=1, keepdims=True) * (1.0 / D)
    normed = center * lax.rsqrt(spread + 1e-06)

    def pick(v):
        got = v[:, 0:176]
        for k in range(1, 8):
            got = jnp.where(t == k, v[:, k * 176 : k * 176 + 176], got)
        return got

    features = jnp.broadcast_to(pick(normed), (8, 176)).astype(BF)
    for n, w in enumerate((tq_w, tk_w, tv_w)):
        part = dot(features, w[...])
        for k in range(8):
            qkv_send[k, n, :, 0:176] = part[0:1, k * 176 : k * 176 + 176]

    def send_heads(k):
        to = lax.rem(t + k, 8)
        return remote(qkv_send.at[to], qkv_recv.at[t], s2, r2, (f, to))

    for k in range(1, 8):
        send_heads(k).start()
    qkv_recv[t] = qkv_send[t]
    all_of(qkv_recv.at[pl.ds(0, 7)], s2, r2).wait_recv()

    whole = []
    for n in range(3):
        v = qkv_recv[0, n, :, 0:176]
        for k in range(1, 8):
            v = v + qkv_recv[k, n, :, 0:176]
        whole.append(v)

    def rot(v):
        return (v * turn[0:1, :] + turned(v) * turn[1:2, :]).astype(BF).astype(F32)

    new_send[...] = jnp.zeros_like(new_send)
    new_send[:, 0:176] = rot(whole[1])
    new_send[:, 176:352] = whole[2].astype(BF).astype(F32)


    @pl.loop(1, 32)
    def _(k):
        remote(new_send, new_all.at[f], s3, r3, (lax.rem(f + k, 32), t)).start()

    new_all[f] = new_send[...]
    query = rot(whole[0])
    lane = iota((1, 176), 1)
    wide_query = jnp.concatenate(
        [jnp.where(lane < HD, query, 0.0), jnp.where(lane >= HD, query, 0.0), jnp.zeros((6, 176), F32)],
        axis=0,
    )
    queries = jnp.concatenate([wide_query, jnp.zeros((8, 80), F32)], axis=1).astype(BF)
    count = 32 * CACHE_ROWS
    old_keys = C[:, :, :, 0:256].reshape(count, 256)
    s_old = dot_nt(queries, old_keys)
    s_old = jnp.where(lax.rem(iota((8, count), 1), CACHE_ROWS) < 62, s_old, -1e30)

    all_of(new_all.at[pl.ds(0, 31)], s3, r3).wait_recv()
    known = new_all[:, 0, :]
    s_new = dot_nt(queries, known[:, 0:256].astype(BF))
    s_new = jnp.where(iota((8, 32), 1) <= f, s_new, -1e30)
    top = jnp.maximum(
        jnp.max(s_old, axis=1, keepdims=True), jnp.max(s_new, axis=1, keepdims=True)
    )
    p_old = jnp.exp2(s_old * RATE - top * RATE)
    p_new = jnp.exp2(s_new * RATE - top * RATE)
    p_old = jnp.where(lax.rem(iota((8, count), 1), CACHE_ROWS) < 62, p_old, 0.0)
    p_new = jnp.where(iota((8, 32), 1) <= f, p_new, 0.0)
    mass = jnp.sum(p_old, axis=1, keepdims=True) + jnp.sum(p_new, axis=1, keepdims=True)
    old_values = C[:, :, :, 128:384].reshape(count, 256)
    o = dot(p_old.astype(BF), old_values) + dot(p_new.astype(BF), known[:, 128:384].astype(BF))
    o = o / mass
    temporal = jnp.where(lane < HD, o[0:1, 48:224], o[1:2, 48:224])
    part = dot(jnp.broadcast_to(temporal, (8, 176)).astype(BF), to_w[...])
    for k in range(8):
        last_send[k, :, 0:176] = part[0:1, k * 176 : k * 176 + 176]

    def send_last(k):
        to = lax.rem(t + k, 8)
        return remote(last_send.at[to], last_recv.at[t], s4, r4, (f, to))

    for k in range(1, 8):
        send_last(k).start()
    last_recv[t] = last_send[t]

    stored, kept = (pltpu.make_async_copy(a, out, local.at[0]) for a in (swapped, result))

    @pl.when(moves)
    def _():
        swap(result, swapped, 3).wait()
        stored.start()

    @pl.when(jnp.logical_not(moves))
    def _():
        kept.start()

    copies.retire()
    all_of(C.at[0, pl.ds(0, 15)], c_send, c_recv).wait_send()
    remote(C.at[0], C.at[1], side_send, side_recv, sibling).wait_send()

    @pl.when(moves)
    def _():
        all_of(pooled, s1, r1).wait_send()

    @pl.when(jnp.logical_not(moves))
    def _():
        all_of(pooled.at[pl.ds(0, 7)], s1, r1).wait_send()

    all_of(qkv_recv.at[pl.ds(0, 7)], s2, r2).wait_send()
    all_of(new_all.at[pl.ds(0, 31)], s3, r3).wait_send()
    all_of(last_recv.at[pl.ds(0, 7)], s4, r4).wait_recv()
    total = pick(mean_frame)
    for k in range(8):
        total = total + last_recv[k, :, 0:176]
    frame_out[...] = total.astype(BF)
    all_of(last_recv.at[pl.ds(0, 7)], s4, r4).wait_send()

    @pl.when(moves)
    def _():
        stored.wait()

    @pl.when(jnp.logical_not(moves))
    def _():
        kept.wait()


BIG = 160


def call(*operands):
    turn = operands[-1]
    vmem = pl.BlockSpec(memory_space=pltpu.VMEM)
    dma = pltpu.SemaphoreType.DMA
    held = [pltpu.VMEM(a.shape, a.dtype) for a in operands[:-1]] + [
        pltpu.VMEM(turn.shape[1:], F32)
    ]
    return pl.pallas_call(
        kernel,
        out_shape=(
            jax.ShapeDtypeStruct((TOK, D), BF),
            jax.ShapeDtypeStruct((1, 176), BF),
        ),
        in_specs=[pl.BlockSpec(memory_space=pl.ANY)] * len(operands),
        out_specs=(pl.BlockSpec(memory_space=pl.ANY), vmem),
        scratch_shapes=held
        + [
            pltpu.VMEM((2, TOK), F32),
            pltpu.VMEM((TOK, D), BF),
            pltpu.VMEM((2, TOK), F32),
            pltpu.VMEM((TOK, QW), BF),
            pltpu.VMEM((TOK, QW), BF),
            pltpu.VMEM((4, 512, QW), BF),
            pltpu.VMEM((TOK, DP), BF),
            pltpu.VMEM((2, 4, 8, W_ROWS, WC), BF),
            pltpu.VMEM((2, 4, 8, W_ROWS, WC), BF),
            pltpu.VMEM((2, 4, 8, W_ROWS, WC), BF),
            pltpu.VMEM((2, 16, CACHE_ROWS, CACHE_COLS), BF),
            pltpu.VMEM((TOK, QW), BF),
            pltpu.VMEM((2, TOK, QW), BF),
            pltpu.VMEM((4, TOK, DP), BF),
            pltpu.VMEM((2, 2, 4 * TOK, 512), BF),
            pltpu.VMEM((2, 4, TOK, 256), BF),
            pltpu.VMEM((3, TOK, DP), BF),
            pltpu.VMEM((2, 64, DP), BF),
            pltpu.VMEM((2, TOK, DP), BF),
            pltpu.VMEM((TOK, DP), BF),
            pltpu.VMEM((4, TOK, DP), BF),
            pltpu.VMEM((2, TOK, 768), BF),
            pltpu.VMEM((3, TOK, DP), BF),
            pltpu.VMEM((2, 64, DP), BF),
            pltpu.VMEM((2, TOK, DP), BF),
            pltpu.VMEM((TOK, D), BF),
            pltpu.VMEM((TOK, D), BF),
            pltpu.VMEM((1, D), F32),
            pltpu.VMEM((8, 1, D), F32),
            pltpu.VMEM((8, 3, 1, 256), F32),
            pltpu.VMEM((8, 3, 1, 256), F32),
            pltpu.VMEM((1, CACHE_COLS), F32),
            pltpu.VMEM((32, 1, CACHE_COLS), F32),
            pltpu.VMEM((8, 1, 256), F32),
            pltpu.VMEM((8, 1, 256), F32),
            dma((len(operands),)),
            dma((BIG,)), dma((BIG,)),
            dma((4,)), dma((4,)),
            dma, dma, dma, dma,
            dma, dma, dma, dma, dma, dma, dma, dma,
        ],
        compiler_params=pltpu.CompilerParams(
            collective_id=0, has_side_effects=True, vmem_limit_bytes=56 * 1024 * 1024
        ),
        cost_estimate=pl.CostEstimate(
            flops=8_000_000_000, bytes_accessed=20_000_000, transcendentals=3_000_000
        ),
    )(*operands)


def body(
    patches, shift_offset, shift_slice, w_query, w_key, w_value, w_out, w_up, w_down,
    t_query, t_key, t_value, t_out, cache_keys, cache_values, cache_pos,
):
    half = HD // 2
    freq = np.float32(10000.0) ** (-np.arange(half, dtype=np.float32) / np.float32(half))
    angle = (SPAN + np.arange(FRAMES)).astype(np.float32)[:, None] * freq[None, :]
    cosine, sine = np.cos(angle), np.sin(angle)
    turn = np.stack(
        [
            np.concatenate([cosine] * 4, axis=1),
            np.concatenate([-sine, sine, -sine, sine], axis=1),
        ],
        axis=1,
    ).astype(np.float32)
    steps = np.arange(64)[:, None] * (10000.0 ** (-np.arange(half) / half))[None, :]
    table = np.stack(
        [
            np.concatenate([np.cos(64 * steps)] * 4 + [np.sin(64 * steps)] * 4, axis=1),
            np.concatenate([np.cos(steps)] * 4 + [np.sin(steps)] * 4, axis=1),
        ]
    ).astype(np.float32)
    patch_out, frame_out = call(
        patches[0], shift_offset[None], shift_slice[None], w_query, w_key, w_value,
        w_out.T, w_up, w_down.T, t_query, t_key, t_value, t_out, cache_keys, cache_values, cache_pos[None],
        jnp.asarray(table), jnp.asarray(turn),
    )
    return (patch_out[None], frame_out)


def solution(mesh):
    return jax.shard_map(
        body,
        mesh=mesh,
        in_specs=(
            P("frame", "tok", None),
            P("tok"),
            P("tok"),
            P("frame", "tok"),
            P("frame", "tok"),
            P("frame", "tok"),
            P("tok", "frame"),
            P("frame", "tok"),
            P("tok", "frame"),
            P("tok", None),
            P("tok", None),
            P("tok", None),
            P("tok", None),
            P("frame", "tok"),
            P("frame", "tok"),
            P("frame"),
        ),
        out_specs=(P("frame", "tok", None), P("frame", "tok")),
        check_vma=False,
    )
```
